32 devices in a mesh: sp: 8 (over z, y), dp: 4 (over x, core).
Axes of the slice: x: 2, y: 2, z: 4, core: 2. Of those that a mesh axis runs over, the one named last changes fastest.
Arguments:
- volume: bfloat16 [4, 96, 32, 8, 128], P('dp', None, 'sp'), may hold values from -6 to 6
- cotangent: bfloat16 [4, 96, 32, 8, 128], P('dp', None, 'sp'), may hold values from -6 to 6
- kernels_xy: bfloat16 [2, 96, 3, 3], replicated, may hold values from -2 to 2
- kernels_z: bfloat16 [2, 96, 3], replicated, may hold values from -3.5 to 3.5
- mixing: bfloat16 [2, 96, 96], replicated, may hold values from -0.625 to 0.625
Outputs:
- volume_grad: bfloat16 [4, 96, 32, 8, 128], P('dp', None, 'sp')
- mixing_grad: float32 [2, 96, 96], replicated
- xy_grad: float32 [2, 96, 3, 3], replicated
- z_grad: float32 [2, 96, 3], replicated
The draws below stay inside these ranges and needn't reach their ends.
All inputs are finite; a program needn't handle non-finite values.
Results may differ from the reference program's by a relative error of at most 0.018.
Values may be sent and summed in bfloat16 or wider, within the bound.
No kernel may reach another device: no remote copies, remote signals or barrier semaphores. Data moves between devices by JAX's collectives and lax.ppermute only.
A program may use at most 64 MiB of HBM per device.

```python
import math
import jax
import jax.numpy as jnp
from jax import lax

C = 96
NZ = 8
NY = 128
BLOCKS = 4
NX = 32


def shard_levels(key, dims, pieces, least, high):
    factor_of, own = 1.0, jax.random.fold_in(key, 6)
    for axis_at, blocks in pieces:
        heights = jnp.exp(jax.random.uniform(jax.random.fold_in(own, axis_at), (blocks,), jnp.float32, least / len(pieces), high / len(pieces)))
        factor_of = factor_of * jnp.repeat(heights, dims[axis_at] // blocks).reshape([-1 if axis == axis_at else 1 for axis in range(len(dims))])
    return factor_of


def bell_draw(rng, shape, spread, limit, split=(), held_as=jnp.bfloat16):
    drawn = jax.random.normal(rng, shape, jnp.float32) * spread
    if len(split) > 0:
        drawn = shard_levels(rng, shape, split, -0.22, 0.18) * drawn
    return jnp.clip(drawn, min=-limit, max=limit).astype(held_as)


def setup_inputs(seed: int = 0) -> dict:
    keys = jax.random.split(jax.random.key(seed), 6)
    volume = bell_draw(keys[0], (BLOCKS, C, NX, NZ, NY), 1.0, 6.0, ((0, 4), (2, 8)))
    cotangent = bell_draw(keys[1], (BLOCKS, C, NX, NZ, NY), 1.0, 6.0, ((0, 4), (2, 8)))
    kernels_xy = bell_draw(keys[2], (2, C, 3, 3), 9 ** -0.5, 2.0)
    kernels_z = bell_draw(keys[3], (2, C, 3), 3 ** -0.5, 3.5)
    mixing = bell_draw(keys[4], (2, C, C), C ** -0.5, 0.625)
    return dict(volume=volume, cotangent=cotangent, kernels_xy=kernels_xy, kernels_z=kernels_z, mixing=mixing)


def conv_plane(inputs, kernel):
    extent = inputs.shape[1] - 2
    across = inputs.shape[3]
    padded = jnp.pad(inputs, ((0, 0), (0, 0), (0, 0), (1, 1)))
    summed = jnp.zeros((inputs.shape[0], extent, inputs.shape[2], across), jnp.float32)
    for row_tap in range(3):
        for col_tap in range(3):
            summed = summed + kernel[:, row_tap, col_tap][:, None, None, None] * padded[:, row_tap:row_tap + extent, :, col_tap:col_tap + across].astype(jnp.float32)
    return summed

def conv_depth(inputs, kernel):
    depth_len = inputs.shape[2]
    padded = jnp.pad(inputs, ((0, 0), (0, 0), (1, 1), (0, 0)))
    summed = jnp.zeros(inputs.shape, jnp.float32)
    for depth_tap in range(3):
        summed = summed + kernel[:, depth_tap][:, None, None, None] * padded[:, :, depth_tap:depth_tap + depth_len, :].astype(jnp.float32)
    return summed

def mix_channels(weights, inputs):
    channels = inputs.shape[0]
    flat = inputs.reshape(channels, -1)
    return jnp.dot(weights, flat, preferred_element_type=jnp.float32).reshape(inputs.shape)

def forward_block(inputs, kernel_xy, kernel_z, weights):
    planar = conv_plane(inputs, kernel_xy)
    axial = conv_depth(planar, kernel_z).astype(jnp.bfloat16)
    preact = mix_channels(weights, axial)
    return (planar, axial, preact)

def silu_slope(preact):
    sigma = jax.nn.sigmoid(preact)
    return sigma * (1.0 + preact * (1.0 - sigma))

def backward_block(grad_out, planar, axial, preact, around, kernel_xy, kernel_z, weights, trim):
    grad_pre = (grad_out.astype(jnp.float32) * silu_slope(preact)).astype(jnp.bfloat16)
    channels = grad_pre.shape[0]
    grad_axial = jnp.dot(weights.T, grad_pre.reshape(channels, -1), preferred_element_type=jnp.float32).reshape(grad_pre.shape)
    grad_planar = conv_depth(grad_axial, kernel_z[:, ::-1]).astype(jnp.bfloat16)
    extent = grad_pre.shape[1]
    own_extent = extent - 2 * trim
    own_pre = grad_pre[:, trim:trim + own_extent].reshape(channels, -1)
    own_axial = axial[:, trim:trim + own_extent].reshape(channels, -1)
    grad_weights = lax.dot_general(own_pre, own_axial, (((1,), (1,)), ((), ())), preferred_element_type=jnp.float32)
    own_grad_axial = grad_axial[:, trim:trim + own_extent]
    depth_len = planar.shape[2]
    planar_pad = jnp.pad(planar[:, trim:trim + own_extent], ((0, 0), (0, 0), (1, 1), (0, 0)))
    grad_kz = jnp.stack([lax.optimization_barrier(jnp.sum(own_grad_axial * planar_pad[:, :, depth_tap:depth_tap + depth_len, :], axis=(1, 2, 3))) for depth_tap in range(3)], axis=1)
    own_grad_planar = grad_planar[:, trim:trim + own_extent].astype(jnp.float32)
    across = around.shape[3]
    around_pad = jnp.pad(around, ((0, 0), (0, 0), (0, 0), (1, 1)))
    rows_list = []
    for row_tap in range(3):
        cols_list = []
        for col_tap in range(3):
            cols_list.append(lax.optimization_barrier(jnp.sum(own_grad_planar * around_pad[:, row_tap:row_tap + own_extent, :, col_tap:col_tap + across].astype(jnp.float32), axis=(1, 2, 3))))
        rows_list.append(jnp.stack(cols_list, axis=1))
    grad_kxy = jnp.stack(rows_list, axis=1)
    return (grad_planar, grad_weights, grad_kxy, grad_kz)

def pad_slab(inputs):
    return jnp.pad(inputs, ((0, 0), (1, 1), (0, 0), (0, 0)))

def one_block(volume_part, grad_part, kernel_xy, kernel_z, mixing):
    planar1, axial1, preact1 = forward_block(pad_slab(volume_part), kernel_xy[0], kernel_z[0], mixing[0])
    hidden = jax.nn.silu(preact1).astype(jnp.bfloat16)
    planar2, axial2, preact2 = forward_block(pad_slab(hidden), kernel_xy[1], kernel_z[1], mixing[1])
    grad_planar2, weights2, plane2, depth2 = backward_block(grad_part, planar2, axial2, preact2, pad_slab(hidden), kernel_xy[1], kernel_z[1], mixing[1], 0)
    grad_hidden = conv_plane(pad_slab(grad_planar2), kernel_xy[1][:, ::-1, ::-1]).astype(jnp.bfloat16)
    grad_planar1, weights1, plane1, depth1 = backward_block(grad_hidden, planar1, axial1, preact1, pad_slab(volume_part), kernel_xy[0], kernel_z[0], mixing[0], 0)
    grad_volume = conv_plane(pad_slab(grad_planar1), kernel_xy[0][:, ::-1, ::-1]).astype(jnp.bfloat16)
    return (grad_volume, jnp.stack([weights1, weights2]), jnp.stack([plane1, plane2]), jnp.stack([depth1, depth2]))

def reference(volume, cotangent, kernels_xy, kernels_z, mixing):
    kernel_xy = kernels_xy.astype(jnp.float32)
    kernel_z = kernels_z.astype(jnp.float32)
    results = lax.map(lambda pair: one_block(pair[0], pair[1], kernel_xy, kernel_z, mixing), (volume, cotangent))
    factor = 1.0 / math.sqrt(BLOCKS * NX * NZ * NY)
    return (results[0], lax.optimization_barrier(jnp.sum(results[1], axis=0)) * factor, lax.optimization_barrier(jnp.sum(results[2], axis=0)) * factor, lax.optimization_barrier(jnp.sum(results[3], axis=0)) * factor)
```

```python
import math

import jax
import jax.numpy as jnp
from jax import lax
from jax.sharding import PartitionSpec as P


def padded_2(x, sides, width):
    for axis, dim in sides:
        count, length = (lax.axis_size(axis), x.shape[dim])
        up = [(i, (i + 1) % count) for i in range(count - 1)]
        down = [(j, i) for i, j in up]
        last = lax.slice_in_dim(x, length - width, length, axis=dim)
        first = lax.slice_in_dim(x, 0, width, axis=dim)
        before = lax.ppermute(last, axis, up)
        after = lax.ppermute(first, axis, down)
        x = jnp.concatenate([before, x, after], axis=dim)
    return x


def conv_plane(inputs, kernel):
    extent = inputs.shape[1] - 2
    across = inputs.shape[3]
    padded = jnp.pad(inputs, ((0, 0), (0, 0), (0, 0), (1, 1)))
    summed = jnp.zeros((inputs.shape[0], extent, inputs.shape[2], across), jnp.float32)
    for row_tap in range(3):
        for col_tap in range(3):
            summed = summed + kernel[:, row_tap, col_tap][:, None, None, None] * padded[
                :, row_tap : row_tap + extent, :, col_tap : col_tap + across
            ].astype(jnp.float32)
    return summed


def conv_depth(inputs, kernel):
    depth_len = inputs.shape[2]
    padded = jnp.pad(inputs, ((0, 0), (0, 0), (1, 1), (0, 0)))
    summed = jnp.zeros(inputs.shape, jnp.float32)
    for depth_tap in range(3):
        summed = (
            summed
            + kernel[:, depth_tap][:, None, None, None]
            * padded[:, :, depth_tap : depth_tap + depth_len, :]
        )
    return summed


def mix_channels(weights, inputs):
    channels = inputs.shape[0]
    flat = inputs.reshape(channels, -1)
    return jnp.dot(weights, flat, preferred_element_type=jnp.float32).reshape(inputs.shape)


def forward_block(inputs, kernel_xy, kernel_z, weights):
    planar = conv_plane(inputs, kernel_xy)
    axial = conv_depth(planar, kernel_z).astype(jnp.bfloat16)
    preact = mix_channels(weights, axial)
    return (planar, axial, preact)


def silu_slope(preact):
    sigma = jax.nn.sigmoid(preact)
    return sigma * (1.0 + preact * (1.0 - sigma))


def backward_block(grad_out, planar, axial, preact, around, kernel_z, weights, trim):
    grad_pre = (grad_out.astype(jnp.float32) * silu_slope(preact)).astype(jnp.bfloat16)
    channels = grad_pre.shape[0]
    grad_axial = jnp.dot(
        weights.T, grad_pre.reshape(channels, -1), preferred_element_type=jnp.float32
    ).reshape(grad_pre.shape)
    grad_planar = conv_depth(grad_axial, kernel_z[:, ::-1]).astype(jnp.bfloat16)
    extent = grad_pre.shape[1]
    own_extent = extent - 2 * trim
    own_pre = grad_pre.reshape(channels, -1)
    own_axial = axial.reshape(channels, -1)
    grad_weights = lax.dot_general(
        own_pre, own_axial, (((1,), (1,)), ((), ())), preferred_element_type=jnp.float32
    )
    depth_len = planar.shape[2]
    planar_pad = jnp.pad(planar, ((0, 0), (0, 0), (1, 1), (0, 0)))
    grad_kz = jnp.stack(
        [
            jnp.sum(
                grad_axial * planar_pad[:, :, depth_tap : depth_tap + depth_len, :], axis=(1, 2, 3)
            )
            for depth_tap in range(3)
        ],
        axis=1,
    )
    own_grad_planar = grad_planar.astype(jnp.float32)
    across = around.shape[3]
    around_pad = jnp.pad(around, ((0, 0), (0, 0), (0, 0), (1, 1)))
    rows_list = []
    for row_tap in range(3):
        cols_list = []
        for col_tap in range(3):
            cols_list.append(
                jnp.sum(
                    own_grad_planar
                    * around_pad[
                        :, row_tap : row_tap + own_extent, :, col_tap : col_tap + across
                    ].astype(jnp.float32),
                    axis=(1, 2, 3),
                )
            )
        rows_list.append(jnp.stack(cols_list, axis=1))
    grad_kxy = jnp.stack(rows_list, axis=1)
    return (grad_planar, (grad_weights, grad_kxy, grad_kz))


def edge_grads(grad_planar):
    return padded_2(grad_planar, (("sp", 1),), 1)


def all_sum(total):
    for axis in ("dp", "sp"):
        count, step = (lax.axis_size(axis), 1)
        while step < count:
            total = total + lax.ppermute(total, axis, [(i, i ^ step) for i in range(count)])
            step *= 2
    return total


def settle_all(lower, upper):
    parts = (lower[0], lower[1], lower[2], upper[0], upper[1], upper[2])
    flat = jnp.concatenate([part.reshape(-1) for part in parts])
    flat = jnp.pad(flat, (0, -flat.size % 1024)).reshape(-1, 128)
    flat = all_sum(flat).reshape(-1)
    summed, at = ([], 0)
    for part in parts:
        summed.append(flat[at : at + part.size].reshape(part.shape))
        at += part.size
    return ((summed[0], summed[1], summed[2]), (summed[3], summed[4], summed[5]))


def on_device(volume, cotangent, kernels_xy, kernels_z, mixing):
    inputs = volume[0]
    grad_top = cotangent[0]
    kernel_xy = kernels_xy.astype(jnp.float32)
    kernel_z = kernels_z.astype(jnp.float32)
    slab_len = inputs.shape[1]
    ranks = lax.axis_size("sp")
    place = lax.axis_index("sp")
    wide = padded_2(inputs, (("sp", 1),), 2)
    planar1, axial1, preact1 = forward_block(wide, kernel_xy[0], kernel_z[0], mixing[0])
    hidden = jax.nn.silu(preact1).astype(jnp.bfloat16)
    spots = place * slab_len - 1 + jnp.arange(slab_len + 2, dtype=jnp.int32)
    hidden = jnp.where(
        ((spots >= 0) & (spots < slab_len * ranks))[None, :, None, None],
        hidden,
        jnp.zeros_like(hidden),
    )
    planar2, axial2, preact2 = forward_block(hidden, kernel_xy[1], kernel_z[1], mixing[1])
    grad_planar2, upper = backward_block(
        grad_top, planar2, axial2, preact2, hidden, kernel_z[1], mixing[1], 0
    )
    grad_hidden = conv_plane(edge_grads(grad_planar2), kernel_xy[1][:, ::-1, ::-1]).astype(
        jnp.bfloat16
    )
    grad_planar1, lower = backward_block(
        grad_hidden,
        planar1[:, 1:-1],
        axial1[:, 1:-1],
        preact1[:, 1:-1],
        wide[:, 1:-1],
        kernel_z[0],
        mixing[0],
        0,
    )
    grad_inputs = conv_plane(edge_grads(grad_planar1), kernel_xy[0][:, ::-1, ::-1]).astype(
        jnp.bfloat16
    )
    lower, upper = settle_all(lower, upper)
    factor = 1.0 / math.sqrt(
        lax.axis_size("dp") * slab_len * ranks * inputs.shape[2] * inputs.shape[3]
    )
    mixing_grad = jnp.stack([lower[0], upper[0]]) * factor
    xy_grad = jnp.stack([lower[1], upper[1]]) * factor
    z_grad = jnp.stack([lower[2], upper[2]]) * factor
    return (grad_inputs[None], mixing_grad, xy_grad, z_grad)


def solution(mesh):
    return jax.shard_map(
        on_device,
        mesh=mesh,
        in_specs=(P("dp", None, "sp", None, None), P("dp", None, "sp", None, None), P(), P(), P()),
        out_specs=(P("dp", None, "sp", None, None), P(), P(), P()),
        check_vma=False,
    )
```

```python
import functools
import math

import jax
import jax.numpy as jnp
from jax import lax
from jax.experimental import pallas as pl
from jax.experimental.pallas import tpu as pltpu
from jax.sharding import PartitionSpec as P

GROUP = 16
BF16 = jnp.bfloat16
F32 = jnp.float32


class Planes:
    def __init__(self, sizes, *parts):
        self.channels, self.nz, self.ny = sizes
        self.at = {}
        for ref, indices in parts:
            for spot, index in enumerate(indices):
                self.at[index] = (ref, spot)

    def __contains__(self, index):
        return index in self.at

    def tile(self, index, z, rows):
        ref, spot = self.at[index]
        return ref.at[rows, pl.ds((spot * self.nz + z) * self.ny, self.ny)]

    def span(self, index, start, size):
        ref, spot = self.at[index]
        return ref.at[:, pl.ds(spot * self.nz * self.ny + start, size)]

    def get(self, index, z, rows):
        return self.tile(index, z, rows)[...].astype(F32)

    def put(self, index, z, rows, value):
        self.tile(index, z, rows)[...] = value.astype(BF16)


def over_groups(channels, body):
    def step(group, carry):
        body(pl.ds(pl.multiple_of(group * GROUP, GROUP), GROUP))
        return carry

    lax.fori_loop(0, channels // GROUP, step, 0)


def spread(taps_ref, block, rows, ny, first, count):
    packed = taps_ref[block, rows, :]
    return [jnp.broadcast_to(packed[:, t : t + 1], (GROUP, ny)) for t in range(first, first + count)]


def plane_taps(taps_ref, block, rows, ny, flip):
    taps = spread(taps_ref, block, rows, ny, 0, 9)
    if flip:
        taps = taps[::-1]
    lane = lax.broadcasted_iota(jnp.int32, (GROUP, ny), 1)
    keep = (lane != ny - 1, None, lane != 0)
    return [
        [jnp.where(keep[j], taps[3 * i + j], 0.0) if keep[j] is not None else taps[3 * i + j] for j in range(3)]
        for i in range(3)
    ]


def plane_conv(taps, source, index, z, rows, ny):
    sums = [None, None, None]
    for i in range(3):
        if index + i - 1 in source:
            value = source.get(index + i - 1, z, rows)
            for j in range(3):
                term = taps[i][j] * value
                sums[j] = term if sums[j] is None else sums[j] + term
    return sums[1] + pltpu.roll(sums[0], 1, 1) + pltpu.roll(sums[2], ny - 1, 1)


def depth_conv(taps, values, z):
    total = taps[1] * values[z]
    if z > 0:
        total = total + taps[0] * values[z - 1]
    if z < len(values) - 1:
        total = total + taps[2] * values[z + 1]
    return total


def forward_taps(taps_ref, block, indices, source, planar, axial):
    nz, ny = source.nz, source.ny

    def body(rows):
        taps = plane_taps(taps_ref, block, rows, ny, False)
        depth = spread(taps_ref, block, rows, ny, 9, 3)
        for index in indices:
            values = [plane_conv(taps, source, index, z, rows, ny) for z in range(nz)]
            for z in range(nz):
                planar.put(index, z, rows, values[z])
                axial.put(index, z, rows, depth_conv(depth, values, z))

    over_groups(source.channels, body)


def mixed(mix_ref, block, indices, source, use):
    size = source.nz * source.ny
    step = math.gcd(size, 256)
    weights = mix_ref[block]
    for index in indices:
        for start in range(0, size, step):
            product = jnp.dot(weights, source.span(index, start, step)[...], preferred_element_type=F32)
            use(index, start, step, product)


def gate(preact):
    sigma = 0.5 * jnp.tanh(0.5 * preact) + 0.5
    value = preact * sigma
    return value, sigma + value * (1.0 - sigma)


def hidden_of(mix_ref, indices, axial, hidden, slope, masks):
    def use(index, start, step, preact):
        value, rate = gate(preact)
        if index in masks:
            value, rate = value * masks[index], rate * masks[index]
        hidden.span(index, start, step)[...] = value.astype(BF16)
        slope.span(index, start, step)[...] = rate.astype(BF16)

    mixed(mix_ref, 0, indices, axial, use)


def top_gradient(mix_ref, indices, axial, cotangent, grad_pre):
    def use(index, start, step, preact):
        _, rate = gate(preact)
        grad = cotangent.span(index, start, step)[...].astype(F32) * rate
        grad_pre.span(index, start, step)[...] = grad.astype(BF16)

    mixed(mix_ref, 1, indices, axial, use)


def axial_gradient(mix_t_ref, block, indices, grad_pre, grad_axial):
    def use(index, start, step, product):
        grad_axial.span(index, start, step)[...] = product.astype(BF16)

    mixed(mix_t_ref, block, indices, grad_pre, use)


def planar_gradient(taps_ref, block, indices, grad_axial, grad_planar):
    nz, ny = grad_axial.nz, grad_axial.ny

    def body(rows):
        depth = spread(taps_ref, block, rows, ny, 9, 3)[::-1]
        for index in indices:
            values = [grad_axial.get(index, z, rows) for z in range(nz)]
            for z in range(nz):
                grad_planar.put(index, z, rows, depth_conv(depth, values, z))

    over_groups(grad_axial.channels, body)


def input_gradient(taps_ref, block, indices, grad_planar, target, slope):
    nz, ny = grad_planar.nz, grad_planar.ny

    def body(rows):
        taps = plane_taps(taps_ref, block, rows, ny, True)
        for index in indices:
            for z in range(nz):
                value = plane_conv(taps, grad_planar, index, z, rows, ny)
                if slope is not None:
                    value = value * slope.get(index, z, rows)
                target.put(index, z, rows, value)

    over_groups(grad_planar.channels, body)


def tap_sums(block, indices, grad_planar, source, grad_axial, planar, sums_ref):
    nz, ny = source.nz, source.ny

    def body(rows):
        lane = lax.broadcasted_iota(jnp.int32, (GROUP, ny), 1)
        sums = [None] * 12

        def add(tap, term):
            sums[tap] = term if sums[tap] is None else sums[tap] + term

        for index in indices:
            for z in range(nz):
                grad = grad_planar.get(index, z, rows)
                shifted = (pltpu.roll(grad, ny - 1, 1), grad, pltpu.roll(grad, 1, 1))
                for i in range(3):
                    if index + i - 1 in source:
                        value = source.get(index + i - 1, z, rows)
                        for j in range(3):
                            add(3 * i + j, shifted[j] * value)
                grad = grad_axial.get(index, z, rows)
                for t in range(3):
                    if 0 <= z + t - 1 < nz:
                        add(9 + t, grad * planar.get(index, z + t - 1, rows))
        for i in range(3):
            sums[3 * i] = jnp.where(lane != ny - 1, sums[3 * i], 0.0)
            sums[3 * i + 2] = jnp.where(lane != 0, sums[3 * i + 2], 0.0)
        for t in range(12):
            sums_ref[block, t, rows, :] = sums[t]

    over_groups(source.channels, body)


def mixing_sum(indices, grad_pre, axial):
    size = grad_pre.nz * grad_pre.ny
    total = None
    for index in indices:
        term = lax.dot_general(
            grad_pre.span(index, 0, size)[...],
            axial.span(index, 0, size)[...],
            (((1,), (1,)), ((), ())),
            preferred_element_type=F32,
        )
        total = term if total is None else total + term
    return total


def inner_kernel(sizes, slab, vol, taps, mix, pl1, ax1, sl1, hid):
    inner = range(1, slab - 1)
    planar, axial, slope, hidden = (Planes(sizes, (ref, inner)) for ref in (pl1, ax1, sl1, hid))
    forward_taps(taps, 0, inner, Planes(sizes, (vol, range(slab))), planar, axial)
    hidden_of(mix, inner, axial, hidden, slope, {})


def middle_kernel(
    sizes, slab, vol, lo1, hi1, cot, taps, mix, mix_t, hid_i,
    pl1, ax1, sl1, hid, pl2, ax2, gpre2, gax2, gpl2,
):
    inner, edges = range(1, slab - 1), (0, slab - 1)
    volume = Planes(sizes, (vol, range(slab)), (lo1, (-1,)), (hi1, (slab,)))
    axial = Planes(sizes, (ax1, edges))
    forward_taps(taps, 0, edges, volume, Planes(sizes, (pl1, edges)), axial)
    hidden_of(mix, edges, axial, Planes(sizes, (hid, edges)), Planes(sizes, (sl1, edges)), {})
    hidden = Planes(sizes, (hid_i, inner), (hid, edges))
    cotangent = Planes(sizes, (cot, range(slab)))
    axial, grad_pre = Planes(sizes, (ax2, inner)), Planes(sizes, (gpre2, inner))
    grad_axial = Planes(sizes, (gax2, inner))
    forward_taps(taps, 1, inner, hidden, Planes(sizes, (pl2, inner)), axial)
    top_gradient(mix, inner, axial, cotangent, grad_pre)
    axial_gradient(mix_t, 1, inner, grad_pre, grad_axial)
    planar_gradient(taps, 1, inner, grad_axial, Planes(sizes, (gpl2, inner)))


def edge_kernel(
    sizes, slab, flags, vol, lo1, hi1, lo2, hi2, cot, taps, mix, mix_t, hid_i, hid_e, sl1_e, gpl2_i,
    pl1, ax1, hid, pl2, ax2, gpre2, gax2, gpl2, gpre1, gax1, gpl1, send_lo, send_hi, sl1,
):
    inner, edges, rims = range(1, slab - 1), (0, slab - 1), (-1, slab)
    outer = (-1, 0, slab - 1, slab)
    masks = {-1: flags[0], slab: flags[1]}
    volume = Planes(
        sizes, (vol, range(slab)), (lo1, (-1,)), (hi1, (slab,)), (lo2, (-2,)), (hi2, (slab + 1,))
    )
    axial = Planes(sizes, (ax1, rims))
    forward_taps(taps, 0, rims, volume, Planes(sizes, (pl1, rims)), axial)
    hidden_of(mix, rims, axial, Planes(sizes, (hid, rims)), Planes(sizes, (sl1, rims)), masks)
    hidden = Planes(sizes, (hid_i, inner), (hid_e, edges), (hid, rims))
    cotangent = Planes(sizes, (cot, range(slab)))
    axial, grad_pre = Planes(sizes, (ax2, edges)), Planes(sizes, (gpre2, edges))
    grad_axial = Planes(sizes, (gax2, edges))
    forward_taps(taps, 1, edges, hidden, Planes(sizes, (pl2, edges)), axial)
    top_gradient(mix, edges, axial, cotangent, grad_pre)
    axial_gradient(mix_t, 1, edges, grad_pre, grad_axial)
    planar_gradient(taps, 1, edges, grad_axial, Planes(sizes, (gpl2, edges)))
    grad_planar = Planes(sizes, (gpl2, edges), (gpl2_i, inner))
    slope = Planes(sizes, (sl1_e, edges), (sl1, rims))
    grad_pre, grad_axial = Planes(sizes, (gpre1, outer)), Planes(sizes, (gax1, outer))
    input_gradient(taps, 1, outer, grad_planar, grad_pre, slope)
    axial_gradient(mix_t, 0, outer, grad_pre, grad_axial)
    grad_planar = Planes(sizes, (gpl1, outer))
    planar_gradient(taps, 0, outer, grad_axial, grad_planar)
    low = Planes(sizes, *((gpl1, (-1, 0)),))
    input_gradient(taps, 0, (-2, -1), low, Planes(sizes, (send_lo, (-2, -1))), None)
    high = Planes(sizes)
    for index in (slab - 1, slab):
        high.at[index] = grad_planar.at[index]
    input_gradient(taps, 0, (slab, slab + 1), high, Planes(sizes, (send_hi, (slab, slab + 1))), None)


def weight_kernel(
    sizes, slab, factor, vol, lo1, hi1, lo2, hi2, taps, mix_t,
    pl1_i, ax1_i, sl1_i, hid_i, pl1_e, ax1_e, hid_e, pl2_i, ax2_i, gpre2_i, gax2_i, gpl2_i,
    pl1_r, ax1_r, hid_r, pl2_e, ax2_e, gpre2_e, gax2_e, gpl2_e, gpre1_o, gax1_o, gpl1_o,
    gpl1, payload, gpre1, gax1, sums,
):
    inner, edges, rims = range(1, slab - 1), (0, slab - 1), (-1, slab)
    outer, own, wide = (-1, 0, slab - 1, slab), range(slab), range(-1, slab + 1)
    channels, _, ny = sizes
    grad_planar2 = Planes(sizes, (gpl2_i, inner), (gpl2_e, edges))
    grad_pre1 = Planes(sizes, (gpre1, inner), (gpre1_o, outer))
    grad_axial1 = Planes(sizes, (gax1, inner), (gax1_o, outer))
    grad_planar1 = Planes(sizes, (gpl1, inner), (gpl1_o, outer))
    input_gradient(taps, 1, inner, grad_planar2, grad_pre1, Planes(sizes, (sl1_i, inner)))
    axial_gradient(mix_t, 0, inner, grad_pre1, grad_axial1)
    planar_gradient(taps, 0, inner, grad_axial1, grad_planar1)
    volume = Planes(
        sizes, (vol, own), (lo1, (-1,)), (hi1, (slab,)), (lo2, (-2,)), (hi2, (slab + 1,))
    )
    hidden = Planes(sizes, (hid_i, inner), (hid_e, edges), (hid_r, rims))
    planar1 = Planes(sizes, (pl1_i, inner), (pl1_e, edges), (pl1_r, rims))
    axial1 = Planes(sizes, (ax1_i, inner), (ax1_e, edges), (ax1_r, rims))
    planar2 = Planes(sizes, (pl2_i, inner), (pl2_e, edges))
    axial2 = Planes(sizes, (ax2_i, inner), (ax2_e, edges))
    grad_pre2 = Planes(sizes, (gpre2_i, inner), (gpre2_e, edges))
    grad_axial2 = Planes(sizes, (gax2_i, inner), (gax2_e, edges))
    tap_sums(0, wide, grad_planar1, volume, grad_axial1, planar1, sums)
    tap_sums(1, own, grad_planar2, hidden, grad_axial2, planar2, sums)
    mixing = (mixing_sum(wide, grad_pre1, axial1), mixing_sum(own, grad_pre2, axial2))
    lane = lax.broadcasted_iota(jnp.int32, (channels, payload.shape[2]), 1)
    for block in range(2):
        packed = jnp.zeros(payload.shape[1:], F32)
        for t in range(12):
            total = jnp.sum(sums[block, t], axis=1, keepdims=True)
            packed = packed + jnp.where(lane == channels + t, total, 0.0)
        payload[block] = packed * factor
        payload[block, :, :channels] = mixing[block] * factor


def volume_kernel(sizes, slab, taps, gpl1_i, gpl1_o, out):
    inner, outer = range(1, slab - 1), (-1, 0, slab - 1, slab)
    grad_planar = Planes(sizes, (gpl1_i, inner), (gpl1_o, outer))
    input_gradient(taps, 0, range(slab), grad_planar, Planes(sizes, (out, range(slab))), None)


def call(kernel, name, operands, outputs, scratch=(), flops=0, scalars=0):
    vmem = pl.BlockSpec(memory_space=pltpu.VMEM)
    smem = pl.BlockSpec(memory_space=pltpu.SMEM)
    return pl.pallas_call(
        kernel,
        name=name,
        out_shape=outputs,
        in_specs=[smem] * scalars + [vmem] * (len(operands) - scalars),
        out_specs=[vmem] * len(outputs),
        scratch_shapes=scratch,
        compiler_params=pltpu.CompilerParams(vmem_limit_bytes=32 << 20),
        cost_estimate=pl.CostEstimate(flops=flops, bytes_accessed=1 << 20, transcendentals=0),
    )(*operands)


def all_sum(total):
    for axis in ("dp", "sp"):
        count, step = lax.axis_size(axis), 1
        while step < count:
            mine = total.astype(BF16)
            other = lax.ppermute(mine, axis, [(i, i ^ step) for i in range(count)])
            total = mine.astype(F32) + other.astype(F32)
            step *= 2
    return total


def on_device(volume, cotangent, kernels_xy, kernels_z, mixing):
    _, channels, slab, nz, ny = volume.shape
    plane = nz * ny
    sizes = (channels, nz, ny)
    ranks, place = lax.axis_size("sp"), lax.axis_index("sp")
    up = [(i, i + 1) for i in range(ranks - 1)]
    down = [(j, i) for i, j in up]

    def flat(planes):
        return planes.reshape(channels, -1)

    lo1 = lax.ppermute(flat(volume[0, :, slab - 1]), "sp", up)
    hi1 = lax.ppermute(flat(volume[0, :, 0]), "sp", down)
    lo2 = lax.ppermute(flat(volume[0, :, slab - 2]), "sp", up)
    hi2 = lax.ppermute(flat(volume[0, :, 1]), "sp", down)
    vol, cot = flat(volume[0]), flat(cotangent[0])
    taps = jnp.concatenate(
        [kernels_xy.reshape(2, channels, 9), kernels_z, jnp.zeros((2, channels, 116), BF16)], axis=2
    ).astype(F32)
    mix, mix_t = mixing, jnp.swapaxes(mixing, 1, 2)
    flags = jnp.stack([place > 0, place < ranks - 1]).astype(F32)

    def planes(count):
        return jax.ShapeDtypeStruct((channels, count * plane), BF16)

    def scratch(count):
        return pltpu.VMEM((channels, count * plane), BF16)

    inside = slab - 2
    pl1_i, ax1_i, sl1_i, hid_i = call(
        functools.partial(inner_kernel, sizes, slab), "inner", (vol, taps, mix), [planes(inside)] * 4
    )
    pl1_e, ax1_e, sl1_e, hid_e, pl2_i, ax2_i, gpre2_i, gax2_i, gpl2_i = call(
        functools.partial(middle_kernel, sizes, slab),
        "middle",
        (vol, lo1, hi1, cot, taps, mix, mix_t, hid_i),
        [planes(2)] * 4 + [planes(inside)] * 5,
    )
    pl1_r, ax1_r, hid_r, pl2_e, ax2_e, gpre2_e, gax2_e, gpl2_e, gpre1_o, gax1_o, gpl1_o, send_lo, send_hi = call(
        functools.partial(edge_kernel, sizes, slab),
        "edge",
        (flags, vol, lo1, hi1, lo2, hi2, cot, taps, mix, mix_t, hid_i, hid_e, sl1_e, gpl2_i),
        [planes(2)] * 8 + [planes(4)] * 3 + [planes(2)] * 2,
        scratch=[scratch(2)],
        scalars=1,
    )
    from_lo = lax.ppermute(send_hi, "sp", up)
    from_hi = lax.ppermute(send_lo, "sp", down)
    count = lax.axis_size("dp") * slab * ranks * nz * ny
    gpl1_i, payload = call(
        functools.partial(weight_kernel, sizes, slab, 1.0 / math.sqrt(count)),
        "weights",
        (
            vol, lo1, hi1, lo2, hi2, taps, mix_t,
            pl1_i, ax1_i, sl1_i, hid_i, pl1_e, ax1_e, hid_e, pl2_i, ax2_i, gpre2_i, gax2_i, gpl2_i,
            pl1_r, ax1_r, hid_r, pl2_e, ax2_e, gpre2_e, gax2_e, gpl2_e, gpre1_o, gax1_o, gpl1_o,
        ),
        [planes(inside), jax.ShapeDtypeStruct((2, channels, 128), F32)],
        scratch=[scratch(inside), scratch(inside), pltpu.VMEM((2, 12, channels, ny), F32)],
    )
    total = all_sum(payload)
    (own,) = call(
        functools.partial(volume_kernel, sizes, slab), "volume", (taps, gpl1_i, gpl1_o), [planes(slab)]
    )
    parts = own.astype(F32).reshape(channels, slab, nz, ny)
    from_lo = from_lo.astype(F32).reshape(channels, 2, nz, ny)
    from_hi = from_hi.astype(F32).reshape(channels, 2, nz, ny)
    parts = parts + jnp.pad(from_lo, ((0, 0), (0, slab - 2), (0, 0), (0, 0)))
    parts = parts + jnp.pad(from_hi, ((0, 0), (slab - 2, 0), (0, 0), (0, 0)))
    return (
        parts.astype(BF16)[None],
        total[:, :, :channels],
        total[:, :, channels : channels + 9].reshape(2, channels, 3, 3),
        total[:, :, channels + 9 : channels + 12],
    )


def solution(mesh):
    return jax.shard_map(
        on_device,
        mesh=mesh,
        in_specs=(P("dp", None, "sp", None, None), P("dp", None, "sp", None, None), P(), P(), P()),
        out_specs=(P("dp", None, "sp", None, None), P(), P(), P()),
        check_vma=False,
    )
```

```python
import functools
import math

import jax
import jax.numpy as jnp
from jax import lax
from jax.experimental import pallas as pl
from jax.experimental.pallas import tpu as pltpu
from jax.sharding import PartitionSpec as P

GROUP = 16
BF16 = jnp.bfloat16
F32 = jnp.float32


class Planes:
    def __init__(self, sizes, *parts):
        self.channels, self.nz, self.ny = sizes
        self.at = {}
        for ref, indices in parts:
            for spot, index in enumerate(indices):
                self.at[index] = (ref, spot)

    def __contains__(self, index):
        return index in self.at

    def tile(self, index, z, rows):
        ref, spot = self.at[index]
        return ref.at[rows, pl.ds((spot * self.nz + z) * self.ny, self.ny)]

    def span(self, index, start, size):
        ref, spot = self.at[index]
        return ref.at[:, pl.ds(spot * self.nz * self.ny + start, size)]

    def get(self, index, z, rows):
        return self.tile(index, z, rows)[...].astype(F32)

    def put(self, index, z, rows, value):
        self.tile(index, z, rows)[...] = value.astype(BF16)


def over_groups(channels, body):
    def step(group, carry):
        body(pl.ds(pl.multiple_of(group * GROUP, GROUP), GROUP))
        return carry

    lax.fori_loop(0, channels // GROUP, step, 0, unroll=3)


def spread(taps_ref, block, rows, first, count):
    return [taps_ref[block, t, rows, :].astype(F32) for t in range(first, first + count)]


def plane_taps(taps_ref, block, rows, flip):
    taps = spread(taps_ref, block, rows, 9 if flip else 0, 9)
    return [taps[3 * i : 3 * i + 3] for i in range(3)]


def wide_taps(kernels_xy, kernels_z, ny):
    channels = kernels_xy.shape[1]
    lane = lax.broadcasted_iota(jnp.int32, (1, 1, 3, 1, ny), 4)
    column = lax.broadcasted_iota(jnp.int32, (1, 1, 3, 1, ny), 2)
    keep = ((column != 0) | (lane != ny - 1)) & ((column != 2) | (lane != 0))
    planes = jnp.moveaxis(kernels_xy, 1, 3)
    planes = jnp.concatenate([planes, planes[:, ::-1, ::-1]], axis=1)[..., None]
    planes = jnp.where(keep, planes, jnp.zeros((), planes.dtype)).reshape(2, 18, channels, ny)
    depth = jnp.broadcast_to(jnp.moveaxis(kernels_z, 1, 2)[..., None], (2, 3, channels, ny))
    return jnp.concatenate([planes, depth], axis=1)


def plane_conv(taps, source, index, z, rows, ny):
    sums = [None, None, None]
    for i in range(3):
        if index + i - 1 in source:
            value = source.get(index + i - 1, z, rows)
            for j in range(3):
                term = taps[i][j] * value
                sums[j] = term if sums[j] is None else sums[j] + term
    return sums[1] + pltpu.roll(sums[0], 1, 1) + pltpu.roll(sums[2], ny - 1, 1)


def depth_conv(taps, values, z):
    total = taps[1] * values[z]
    if z > 0:
        total = total + taps[0] * values[z - 1]
    if z < len(values) - 1:
        total = total + taps[2] * values[z + 1]
    return total


def forward_taps(taps_ref, block, indices, source, planar, axial):
    nz, ny = source.nz, source.ny

    def body(rows):
        taps = plane_taps(taps_ref, block, rows, False)
        depth = spread(taps_ref, block, rows, 18, 3)
        for index in indices:
            values = [plane_conv(taps, source, index, z, rows, ny) for z in range(nz)]
            for z in range(nz):
                planar.put(index, z, rows, values[z])
                axial.put(index, z, rows, depth_conv(depth, values, z))

    over_groups(source.channels, body)


def mixed(mix_ref, block, indices, source, use):
    size = source.nz * source.ny
    step = math.gcd(size, 256)
    weights = mix_ref[block]
    for index in indices:
        for start in range(0, size, step):
            product = jnp.dot(weights, source.span(index, start, step)[...], preferred_element_type=F32)
            use(index, start, step, product)


def gate(preact):
    sigma = 0.5 * jnp.tanh(0.5 * preact) + 0.5
    value = preact * sigma
    return value, sigma + value * (1.0 - sigma)


def hidden_of(mix_ref, indices, axial, hidden, slope, masks):
    def use(index, start, step, preact):
        value, rate = gate(preact)
        if index in masks:
            value, rate = value * masks[index], rate * masks[index]
        hidden.span(index, start, step)[...] = value.astype(BF16)
        slope.span(index, start, step)[...] = rate.astype(BF16)

    mixed(mix_ref, 0, indices, axial, use)


def top_gradient(mix_ref, indices, axial, cotangent, grad_pre):
    def use(index, start, step, preact):
        _, rate = gate(preact)
        grad = cotangent.span(index, start, step)[...].astype(F32) * rate
        grad_pre.span(index, start, step)[...] = grad.astype(BF16)

    mixed(mix_ref, 1, indices, axial, use)


def axial_gradient(mix_t_ref, block, indices, grad_pre, grad_axial):
    def use(index, start, step, product):
        grad_axial.span(index, start, step)[...] = product.astype(BF16)

    mixed(mix_t_ref, block, indices, grad_pre, use)


def planar_gradient(taps_ref, block, indices, grad_axial, grad_planar):
    nz = grad_axial.nz

    def body(rows):
        depth = spread(taps_ref, block, rows, 18, 3)[::-1]
        for index in indices:
            values = [grad_axial.get(index, z, rows) for z in range(nz)]
            for z in range(nz):
                grad_planar.put(index, z, rows, depth_conv(depth, values, z))

    over_groups(grad_axial.channels, body)


def input_gradient(taps_ref, block, indices, grad_planar, target, slope):
    nz, ny = grad_planar.nz, grad_planar.ny

    def body(rows):
        taps = plane_taps(taps_ref, block, rows, True)
        for index in indices:
            for z in range(nz):
                value = plane_conv(taps, grad_planar, index, z, rows, ny)
                if slope is not None:
                    value = value * slope.get(index, z, rows)
                target.put(index, z, rows, value)

    over_groups(grad_planar.channels, body)


def tap_sums(block, indices, grad_planar, source, grad_axial, planar, sums_ref):
    nz, ny = source.nz, source.ny

    def body(rows):
        lane = lax.broadcasted_iota(jnp.int32, (GROUP, ny), 1)
        sums = [None] * 12

        def add(tap, term):
            sums[tap] = term if sums[tap] is None else sums[tap] + term

        for index in indices:
            for z in range(nz):
                grad = grad_planar.get(index, z, rows)
                shifted = (pltpu.roll(grad, ny - 1, 1), grad, pltpu.roll(grad, 1, 1))
                for i in range(3):
                    if index + i - 1 in source:
                        value = source.get(index + i - 1, z, rows)
                        for j in range(3):
                            add(3 * i + j, shifted[j] * value)
                grad = grad_axial.get(index, z, rows)
                for t in range(3):
                    if 0 <= z + t - 1 < nz:
                        add(9 + t, grad * planar.get(index, z + t - 1, rows))
        for i in range(3):
            sums[3 * i] = jnp.where(lane != ny - 1, sums[3 * i], 0.0)
            sums[3 * i + 2] = jnp.where(lane != 0, sums[3 * i + 2], 0.0)
        for t in range(12):
            sums_ref[block, t, rows, :] = sums[t]

    over_groups(source.channels, body)


def mixing_sum(indices, grad_pre, axial):
    size = grad_pre.nz * grad_pre.ny
    total = None
    for index in indices:
        term = lax.dot_general(
            grad_pre.span(index, 0, size)[...],
            axial.span(index, 0, size)[...],
            (((1,), (1,)), ((), ())),
            preferred_element_type=F32,
        )
        total = term if total is None else total + term
    return total


def inner_kernel(sizes, slab, vol, taps, mix, pl1, ax1, sl1, hid):
    inner = range(1, slab - 1)
    planar, axial, slope, hidden = (Planes(sizes, (ref, inner)) for ref in (pl1, ax1, sl1, hid))
    forward_taps(taps, 0, inner, Planes(sizes, (vol, range(slab))), planar, axial)
    hidden_of(mix, inner, axial, hidden, slope, {})


def middle_kernel(
    sizes, slab, vol, lo1, hi1, cot, taps, mix, mix_t, hid_i,
    pl1, ax1, sl1, hid, pl2, ax2, gpre2, gax2, gpl2,
):
    inner, edges = range(1, slab - 1), (0, slab - 1)
    volume = Planes(sizes, (vol, range(slab)), (lo1, (-1,)), (hi1, (slab,)))
    axial = Planes(sizes, (ax1, edges))
    forward_taps(taps, 0, edges, volume, Planes(sizes, (pl1, edges)), axial)
    hidden_of(mix, edges, axial, Planes(sizes, (hid, edges)), Planes(sizes, (sl1, edges)), {})
    hidden = Planes(sizes, (hid_i, inner), (hid, edges))
    cotangent = Planes(sizes, (cot, range(slab)))
    axial, grad_pre = Planes(sizes, (ax2, inner)), Planes(sizes, (gpre2, inner))
    grad_axial = Planes(sizes, (gax2, inner))
    forward_taps(taps, 1, inner, hidden, Planes(sizes, (pl2, inner)), axial)
    top_gradient(mix, inner, axial, cotangent, grad_pre)
    axial_gradient(mix_t, 1, inner, grad_pre, grad_axial)
    planar_gradient(taps, 1, inner, grad_axial, Planes(sizes, (gpl2, inner)))


def edge_kernel(
    sizes, slab, flags, vol, lo1, hi1, lo2, hi2, cot, taps, mix, mix_t, hid_i, hid_e, sl1_e, gpl2_i,
    pl1, ax1, hid, pl2, ax2, gpre2, gax2, gpl2, gpre1, gax1, gpl1, send_lo, send_hi, sl1,
):
    inner, edges, rims = range(1, slab - 1), (0, slab - 1), (-1, slab)
    outer = (-1, 0, slab - 1, slab)
    masks = {-1: flags[0], slab: flags[1]}
    volume = Planes(
        sizes, (vol, range(slab)), (lo1, (-1,)), (hi1, (slab,)), (lo2, (-2,)), (hi2, (slab + 1,))
    )
    axial = Planes(sizes, (ax1, rims))
    forward_taps(taps, 0, rims, volume, Planes(sizes, (pl1, rims)), axial)
    hidden_of(mix, rims, axial, Planes(sizes, (hid, rims)), Planes(sizes, (sl1, rims)), masks)
    hidden = Planes(sizes, (hid_i, inner), (hid_e, edges), (hid, rims))
    cotangent = Planes(sizes, (cot, range(slab)))
    axial, grad_pre = Planes(sizes, (ax2, edges)), Planes(sizes, (gpre2, edges))
    grad_axial = Planes(sizes, (gax2, edges))
    forward_taps(taps, 1, edges, hidden, Planes(sizes, (pl2, edges)), axial)
    top_gradient(mix, edges, axial, cotangent, grad_pre)
    axial_gradient(mix_t, 1, edges, grad_pre, grad_axial)
    planar_gradient(taps, 1, edges, grad_axial, Planes(sizes, (gpl2, edges)))
    grad_planar = Planes(sizes, (gpl2, edges), (gpl2_i, inner))
    slope = Planes(sizes, (sl1_e, edges), (sl1, rims))
    grad_pre, grad_axial = Planes(sizes, (gpre1, outer)), Planes(sizes, (gax1, outer))
    input_gradient(taps, 1, outer, grad_planar, grad_pre, slope)
    axial_gradient(mix_t, 0, outer, grad_pre, grad_axial)
    grad_planar = Planes(sizes, (gpl1, outer))
    planar_gradient(taps, 0, outer, grad_axial, grad_planar)
    sent = (-2, -1, slab, slab + 1)
    input_gradient(
        taps, 0, sent, grad_planar, Planes(sizes, (send_lo, sent[:2]), (send_hi, sent[2:])), None
    )


def weight_kernel(
    sizes, slab, factor, vol, lo1, hi1, lo2, hi2, taps, mix_t,
    pl1_i, ax1_i, sl1_i, hid_i, pl1_e, ax1_e, hid_e, pl2_i, ax2_i, gpre2_i, gax2_i, gpl2_i,
    pl1_r, ax1_r, hid_r, pl2_e, ax2_e, gpre2_e, gax2_e, gpl2_e, gpre1_o, gax1_o, gpl1_o,
    gpl1, payload, gpre1, gax1, sums,
):
    inner, edges, rims = range(1, slab - 1), (0, slab - 1), (-1, slab)
    outer, own, wide = (-1, 0, slab - 1, slab), range(slab), range(-1, slab + 1)
    channels, _, ny = sizes
    grad_planar2 = Planes(sizes, (gpl2_i, inner), (gpl2_e, edges))
    grad_pre1 = Planes(sizes, (gpre1, inner), (gpre1_o, outer))
    grad_axial1 = Planes(sizes, (gax1, inner), (gax1_o, outer))
    grad_planar1 = Planes(sizes, (gpl1, inner), (gpl1_o, outer))
    input_gradient(taps, 1, inner, grad_planar2, grad_pre1, Planes(sizes, (sl1_i, inner)))
    axial_gradient(mix_t, 0, inner, grad_pre1, grad_axial1)
    planar_gradient(taps, 0, inner, grad_axial1, grad_planar1)
    volume = Planes(
        sizes, (vol, own), (lo1, (-1,)), (hi1, (slab,)), (lo2, (-2,)), (hi2, (slab + 1,))
    )
    hidden = Planes(sizes, (hid_i, inner), (hid_e, edges), (hid_r, rims))
    planar1 = Planes(sizes, (pl1_i, inner), (pl1_e, edges), (pl1_r, rims))
    axial1 = Planes(sizes, (ax1_i, inner), (ax1_e, edges), (ax1_r, rims))
    planar2 = Planes(sizes, (pl2_i, inner), (pl2_e, edges))
    axial2 = Planes(sizes, (ax2_i, inner), (ax2_e, edges))
    grad_pre2 = Planes(sizes, (gpre2_i, inner), (gpre2_e, edges))
    grad_axial2 = Planes(sizes, (gax2_i, inner), (gax2_e, edges))
    tap_sums(0, wide, grad_planar1, volume, grad_axial1, planar1, sums)
    tap_sums(1, own, grad_planar2, hidden, grad_axial2, planar2, sums)
    mixing = (mixing_sum(wide, grad_pre1, axial1), mixing_sum(own, grad_pre2, axial2))
    lane = lax.broadcasted_iota(jnp.int32, (channels, payload.shape[2]), 1)
    for block in range(2):
        packed = jnp.zeros(payload.shape[1:], F32)
        for t in range(12):
            total = jnp.sum(sums[block, t], axis=1, keepdims=True)
            packed = packed + jnp.where(lane == channels + t, total, 0.0)
        payload[block] = packed * factor
        payload[block, :, :channels] = mixing[block] * factor


def volume_kernel(sizes, slab, taps, gpl1_i, gpl1_o, out):
    inner, outer = range(1, slab - 1), (-1, 0, slab - 1, slab)
    grad_planar = Planes(sizes, (gpl1_i, inner), (gpl1_o, outer))
    input_gradient(taps, 0, range(slab), grad_planar, Planes(sizes, (out, range(slab))), None)


def call(kernel, name, operands, outputs, scratch=(), flops=0, scalars=0):
    vmem = pl.BlockSpec(memory_space=pltpu.VMEM)
    smem = pl.BlockSpec(memory_space=pltpu.SMEM)
    return pl.pallas_call(
        kernel,
        name=name,
        out_shape=outputs,
        in_specs=[smem] * scalars + [vmem] * (len(operands) - scalars),
        out_specs=[vmem] * len(outputs),
        scratch_shapes=scratch,
        compiler_params=pltpu.CompilerParams(vmem_limit_bytes=32 << 20),
        cost_estimate=pl.CostEstimate(flops=flops, bytes_accessed=1 << 20, transcendentals=0),
    )(*operands)


def all_sum(total):
    for axis in ("dp", "sp"):
        count, step = lax.axis_size(axis), 1
        while step < count:
            mine = total.astype(BF16)
            other = lax.ppermute(mine, axis, [(i, i ^ step) for i in range(count)])
            total = mine.astype(F32) + other.astype(F32)
            step *= 2
    return total


def on_device(volume, cotangent, kernels_xy, kernels_z, mixing):
    _, channels, slab, nz, ny = volume.shape
    plane = nz * ny
    sizes = (channels, nz, ny)
    ranks, place = lax.axis_size("sp"), lax.axis_index("sp")
    up = [(i, i + 1) for i in range(ranks - 1)]
    down = [(j, i) for i, j in up]

    def flat(planes):
        return planes.reshape(channels, -1)

    lo1 = lax.ppermute(flat(volume[0, :, slab - 1]), "sp", up)
    hi1 = lax.ppermute(flat(volume[0, :, 0]), "sp", down)
    lo2 = lax.ppermute(flat(volume[0, :, slab - 2]), "sp", up)
    hi2 = lax.ppermute(flat(volume[0, :, 1]), "sp", down)
    vol, cot = flat(volume[0]), flat(cotangent[0])
    taps = wide_taps(kernels_xy, kernels_z, ny)
    mix, mix_t = mixing, jnp.swapaxes(mixing, 1, 2)
    flags = jnp.stack([place > 0, place < ranks - 1]).astype(F32)

    def planes(count):
        return jax.ShapeDtypeStruct((channels, count * plane), BF16)

    def scratch(count):
        return pltpu.VMEM((channels, count * plane), BF16)

    inside = slab - 2
    pl1_i, ax1_i, sl1_i, hid_i = call(
        functools.partial(inner_kernel, sizes, slab), "inner", (vol, taps, mix), [planes(inside)] * 4
    )
    pl1_e, ax1_e, sl1_e, hid_e, pl2_i, ax2_i, gpre2_i, gax2_i, gpl2_i = call(
        functools.partial(middle_kernel, sizes, slab),
        "middle",
        (vol, lo1, hi1, cot, taps, mix, mix_t, hid_i),
        [planes(2)] * 4 + [planes(inside)] * 5,
    )
    pl1_r, ax1_r, hid_r, pl2_e, ax2_e, gpre2_e, gax2_e, gpl2_e, gpre1_o, gax1_o, gpl1_o, send_lo, send_hi = call(
        functools.partial(edge_kernel, sizes, slab),
        "edge",
        (flags, vol, lo1, hi1, lo2, hi2, cot, taps, mix, mix_t, hid_i, hid_e, sl1_e, gpl2_i),
        [planes(2)] * 8 + [planes(4)] * 3 + [planes(2)] * 2,
        scratch=[scratch(2)],
        scalars=1,
    )
    from_lo = lax.ppermute(send_hi, "sp", up)
    from_hi = lax.ppermute(send_lo, "sp", down)
    count = lax.axis_size("dp") * slab * ranks * nz * ny
    gpl1_i, payload = call(
        functools.partial(weight_kernel, sizes, slab, 1.0 / math.sqrt(count)),
        "weights",
        (
            vol, lo1, hi1, lo2, hi2, taps, mix_t,
            pl1_i, ax1_i, sl1_i, hid_i, pl1_e, ax1_e, hid_e, pl2_i, ax2_i, gpre2_i, gax2_i, gpl2_i,
            pl1_r, ax1_r, hid_r, pl2_e, ax2_e, gpre2_e, gax2_e, gpl2_e, gpre1_o, gax1_o, gpl1_o,
        ),
        [planes(inside), jax.ShapeDtypeStruct((2, channels, 128), F32)],
        scratch=[scratch(inside), scratch(inside), pltpu.VMEM((2, 12, channels, ny), F32)],
    )
    total = all_sum(payload)
    (own,) = call(
        functools.partial(volume_kernel, sizes, slab), "volume", (taps, gpl1_i, gpl1_o), [planes(slab)]
    )
    parts = own.astype(F32).reshape(channels, slab, nz, ny)
    from_lo = from_lo.astype(F32).reshape(channels, 2, nz, ny)
    from_hi = from_hi.astype(F32).reshape(channels, 2, nz, ny)
    parts = parts + jnp.pad(from_lo, ((0, 0), (0, slab - 2), (0, 0), (0, 0)))
    parts = parts + jnp.pad(from_hi, ((0, 0), (slab - 2, 0), (0, 0), (0, 0)))
    return (
        parts.astype(BF16)[None],
        total[:, :, :channels],
        total[:, :, channels : channels + 9].reshape(2, channels, 3, 3),
        total[:, :, channels + 9 : channels + 12],
    )


def solution(mesh):
    return jax.shard_map(
        on_device,
        mesh=mesh,
        in_specs=(P("dp", None, "sp", None, None), P("dp", None, "sp", None, None), P(), P(), P()),
        out_specs=(P("dp", None, "sp", None, None), P(), P(), P()),
        check_vma=False,
    )
```

```python
import functools
import math

import jax
import jax.numpy as jnp
from jax import lax
from jax.experimental import pallas as pl
from jax.experimental.pallas import tpu as pltpu
from jax.sharding import PartitionSpec as P

GROUP = 16
BF16 = jnp.bfloat16
F32 = jnp.float32


class Planes:
    def __init__(self, sizes, *parts):
        self.channels, self.nz, self.ny = sizes
        self.at = {}
        for ref, indices in parts:
            for spot, index in enumerate(indices):
                self.at[index] = (ref, spot)

    def __contains__(self, index):
        return index in self.at

    def tile(self, index, z, rows):
        ref, spot = self.at[index]
        return ref.at[rows, pl.ds((spot * self.nz + z) * self.ny, self.ny)]

    def span(self, index, start, size):
        ref, spot = self.at[index]
        return ref.at[:, pl.ds(spot * self.nz * self.ny + start, size)]

    def get(self, index, z, rows):
        return self.tile(index, z, rows)[...].astype(F32)

    def put(self, index, z, rows, value):
        self.tile(index, z, rows)[...] = value.astype(BF16)


def over_groups(channels, body):
    def step(group, carry):
        body(pl.ds(pl.multiple_of(group * GROUP, GROUP), GROUP))
        return carry

    lax.fori_loop(0, channels // GROUP, step, 0, unroll=3)


def spread(taps_ref, block, rows, first, count):
    return [taps_ref[block, t, rows, :].astype(F32) for t in range(first, first + count)]


def plane_taps(taps_ref, block, rows, flip):
    taps = spread(taps_ref, block, rows, 9 if flip else 0, 9)
    return [taps[3 * i : 3 * i + 3] for i in range(3)]


def wide_taps(kernels_xy, kernels_z, ny):
    channels = kernels_xy.shape[1]
    lane = lax.broadcasted_iota(jnp.int32, (1, 1, 3, 1, ny), 4)
    column = lax.broadcasted_iota(jnp.int32, (1, 1, 3, 1, ny), 2)
    keep = ((column != 0) | (lane != ny - 1)) & ((column != 2) | (lane != 0))
    planes = jnp.moveaxis(kernels_xy, 1, 3)
    planes = jnp.concatenate([planes, planes[:, ::-1, ::-1]], axis=1)[..., None]
    planes = jnp.where(keep, planes, jnp.zeros((), planes.dtype)).reshape(2, 18, channels, ny)
    depth = jnp.broadcast_to(jnp.moveaxis(kernels_z, 1, 2)[..., None], (2, 3, channels, ny))
    return jnp.concatenate([planes, depth], axis=1)


def plane_conv(taps, source, index, z, rows, ny):
    sums = [None, None, None]
    for i in range(3):
        if index + i - 1 in source:
            value = source.get(index + i - 1, z, rows)
            for j in range(3):
                term = taps[i][j] * value
                sums[j] = term if sums[j] is None else sums[j] + term
    return sums[1] + pltpu.roll(sums[0], 1, 1) + pltpu.roll(sums[2], ny - 1, 1)


def depth_conv(taps, values, z):
    total = taps[1] * values[z]
    if z > 0:
        total = total + taps[0] * values[z - 1]
    if z < len(values) - 1:
        total = total + taps[2] * values[z + 1]
    return total


def forward_taps(taps_ref, block, indices, source, planar, axial):
    nz, ny = source.nz, source.ny

    def body(rows):
        taps = plane_taps(taps_ref, block, rows, False)
        depth = spread(taps_ref, block, rows, 18, 3)
        for index in indices:
            values = [plane_conv(taps, source, index, z, rows, ny) for z in range(nz)]
            for z in range(nz):
                planar.put(index, z, rows, values[z])
                axial.put(index, z, rows, depth_conv(depth, values, z))

    over_groups(source.channels, body)


def mixed(mix_ref, block, indices, source, use):
    size = source.nz * source.ny
    step = math.gcd(size, 256)
    weights = mix_ref[block]
    for index in indices:
        for start in range(0, size, step):
            product = jnp.dot(weights, source.span(index, start, step)[...], preferred_element_type=F32)
            use(index, start, step, product)


def gate(preact):
    sigma = 0.5 * jnp.tanh(0.5 * preact) + 0.5
    value = preact * sigma
    return value, sigma + value * (1.0 - sigma)


def hidden_of(mix_ref, indices, axial, hidden, slope, masks):
    def use(index, start, step, preact):
        value, rate = gate(preact)
        if index in masks:
            value, rate = value * masks[index], rate * masks[index]
        hidden.span(index, start, step)[...] = value.astype(BF16)
        slope.span(index, start, step)[...] = rate.astype(BF16)

    mixed(mix_ref, 0, indices, axial, use)


def top_gradient(mix_ref, indices, axial, cotangent, grad_pre):
    def use(index, start, step, preact):
        _, rate = gate(preact)
        grad = cotangent.span(index, start, step)[...].astype(F32) * rate
        grad_pre.span(index, start, step)[...] = grad.astype(BF16)

    mixed(mix_ref, 1, indices, axial, use)


def axial_gradient(mix_t_ref, block, indices, grad_pre, grad_axial):
    def use(index, start, step, product):
        grad_axial.span(index, start, step)[...] = product.astype(BF16)

    mixed(mix_t_ref, block, indices, grad_pre, use)


def planar_gradient(taps_ref, block, indices, grad_axial, grad_planar):
    nz = grad_axial.nz

    def body(rows):
        depth = spread(taps_ref, block, rows, 18, 3)[::-1]
        for index in indices:
            values = [grad_axial.get(index, z, rows) for z in range(nz)]
            for z in range(nz):
                grad_planar.put(index, z, rows, depth_conv(depth, values, z))

    over_groups(grad_axial.channels, body)


def input_gradient(taps_ref, block, indices, grad_planar, target, slope):
    nz, ny = grad_planar.nz, grad_planar.ny

    def body(rows):
        taps = plane_taps(taps_ref, block, rows, True)
        for index in indices:
            for z in range(nz):
                value = plane_conv(taps, grad_planar, index, z, rows, ny)
                if slope is not None:
                    value = value * slope.get(index, z, rows)
                target.put(index, z, rows, value)

    over_groups(grad_planar.channels, body)


def tap_sums(block, indices, grad_planar, source, grad_axial, planar, sums_ref):
    nz, ny = source.nz, source.ny

    def body(rows):
        lane = lax.broadcasted_iota(jnp.int32, (GROUP, ny), 1)
        sums = [None] * 12

        def add(tap, term):
            sums[tap] = term if sums[tap] is None else sums[tap] + term

        for index in indices:
            for z in range(nz):
                grad = grad_planar.get(index, z, rows)
                shifted = (pltpu.roll(grad, ny - 1, 1), grad, pltpu.roll(grad, 1, 1))
                for i in range(3):
                    if index + i - 1 in source:
                        value = source.get(index + i - 1, z, rows)
                        for j in range(3):
                            add(3 * i + j, shifted[j] * value)
                grad = grad_axial.get(index, z, rows)
                for t in range(3):
                    if 0 <= z + t - 1 < nz:
                        add(9 + t, grad * planar.get(index, z + t - 1, rows))
        for i in range(3):
            sums[3 * i] = jnp.where(lane != ny - 1, sums[3 * i], 0.0)
            sums[3 * i + 2] = jnp.where(lane != 0, sums[3 * i + 2], 0.0)
        for t in range(12):
            sums_ref[block, t, rows, :] = sums[t]

    over_groups(source.channels, body)


def mixing_sum(indices, grad_pre, axial):
    size = grad_pre.nz * grad_pre.ny
    total = None
    for index in indices:
        term = lax.dot_general(
            grad_pre.span(index, 0, size)[...],
            axial.span(index, 0, size)[...],
            (((1,), (1,)), ((), ())),
            preferred_element_type=F32,
        )
        total = term if total is None else total + term
    return total


def inner_kernel(sizes, slab, vol, taps, mix, pl1, ax1, sl1, hid):
    inner = range(1, slab - 1)
    planar, axial, slope, hidden = (Planes(sizes, (ref, inner)) for ref in (pl1, ax1, sl1, hid))
    forward_taps(taps, 0, inner, Planes(sizes, (vol, range(slab))), planar, axial)
    hidden_of(mix, inner, axial, hidden, slope, {})


def middle_kernel(
    sizes, slab, vol, lo1, hi1, cot, taps, mix, mix_t, hid_i,
    pl1, ax1, sl1, hid, pl2, ax2, gpre2, gax2, gpl2,
):
    inner, edges = range(1, slab - 1), (0, slab - 1)
    volume = Planes(sizes, (vol, range(slab)), (lo1, (-1,)), (hi1, (slab,)))
    axial = Planes(sizes, (ax1, edges))
    forward_taps(taps, 0, edges, volume, Planes(sizes, (pl1, edges)), axial)
    hidden_of(mix, edges, axial, Planes(sizes, (hid, edges)), Planes(sizes, (sl1, edges)), {})
    hidden = Planes(sizes, (hid_i, inner), (hid, edges))
    cotangent = Planes(sizes, (cot, range(slab)))
    axial, grad_pre = Planes(sizes, (ax2, inner)), Planes(sizes, (gpre2, inner))
    grad_axial = Planes(sizes, (gax2, inner))
    forward_taps(taps, 1, inner, hidden, Planes(sizes, (pl2, inner)), axial)
    top_gradient(mix, inner, axial, cotangent, grad_pre)
    axial_gradient(mix_t, 1, inner, grad_pre, grad_axial)
    planar_gradient(taps, 1, inner, grad_axial, Planes(sizes, (gpl2, inner)))


def edge_kernel(
    sizes, slab, flags, vol, lo1, hi1, lo2, hi2, cot, taps, mix, mix_t, hid_i, hid_e, sl1_e, gpl2_i,
    pl1, ax1, hid, pl2, ax2, gpre2, gax2, gpl2, gpre1, gax1, gpl1, send_lo, send_hi, sl1,
):
    inner, edges, rims = range(1, slab - 1), (0, slab - 1), (-1, slab)
    outer = (-1, 0, slab - 1, slab)
    masks = {-1: flags[0], slab: flags[1]}
    volume = Planes(
        sizes, (vol, range(slab)), (lo1, (-1,)), (hi1, (slab,)), (lo2, (-2,)), (hi2, (slab + 1,))
    )
    axial = Planes(sizes, (ax1, rims))
    forward_taps(taps, 0, rims, volume, Planes(sizes, (pl1, rims)), axial)
    hidden_of(mix, rims, axial, Planes(sizes, (hid, rims)), Planes(sizes, (sl1, rims)), masks)
    hidden = Planes(sizes, (hid_i, inner), (hid_e, edges), (hid, rims))
    cotangent = Planes(sizes, (cot, range(slab)))
    axial, grad_pre = Planes(sizes, (ax2, edges)), Planes(sizes, (gpre2, edges))
    grad_axial = Planes(sizes, (gax2, edges))
    forward_taps(taps, 1, edges, hidden, Planes(sizes, (pl2, edges)), axial)
    top_gradient(mix, edges, axial, cotangent, grad_pre)
    axial_gradient(mix_t, 1, edges, grad_pre, grad_axial)
    planar_gradient(taps, 1, edges, grad_axial, Planes(sizes, (gpl2, edges)))
    grad_planar = Planes(sizes, (gpl2, edges), (gpl2_i, inner))
    slope = Planes(sizes, (sl1_e, edges), (sl1, rims))
    grad_pre, grad_axial = Planes(sizes, (gpre1, outer)), Planes(sizes, (gax1, outer))
    input_gradient(taps, 1, outer, grad_planar, grad_pre, slope)
    axial_gradient(mix_t, 0, outer, grad_pre, grad_axial)
    grad_planar = Planes(sizes, (gpl1, outer))
    planar_gradient(taps, 0, outer, grad_axial, grad_planar)
    sent = (-2, -1, slab, slab + 1)
    input_gradient(
        taps, 0, sent, grad_planar, Planes(sizes, (send_lo, sent[:2]), (send_hi, sent[2:])), None
    )


def weight_kernel(
    sizes, slab, factor, vol, lo1, hi1, lo2, hi2, taps, mix_t,
    pl1_i, ax1_i, sl1_i, hid_i, pl1_e, ax1_e, hid_e, pl2_i, ax2_i, gpre2_i, gax2_i, gpl2_i,
    pl1_r, ax1_r, hid_r, pl2_e, ax2_e, gpre2_e, gax2_e, gpl2_e, gpre1_o, gax1_o, gpl1_o,
    gpl1, payload, gpre1, gax1, sums,
):
    inner, edges, rims = range(1, slab - 1), (0, slab - 1), (-1, slab)
    outer, own, wide = (-1, 0, slab - 1, slab), range(slab), range(-1, slab + 1)
    channels, _, ny = sizes
    grad_planar2 = Planes(sizes, (gpl2_i, inner), (gpl2_e, edges))
    grad_pre1 = Planes(sizes, (gpre1, inner), (gpre1_o, outer))
    grad_axial1 = Planes(sizes, (gax1, inner), (gax1_o, outer))
    grad_planar1 = Planes(sizes, (gpl1, inner), (gpl1_o, outer))
    input_gradient(taps, 1, inner, grad_planar2, grad_pre1, Planes(sizes, (sl1_i, inner)))
    axial_gradient(mix_t, 0, inner, grad_pre1, grad_axial1)
    planar_gradient(taps, 0, inner, grad_axial1, grad_planar1)
    volume = Planes(
        sizes, (vol, own), (lo1, (-1,)), (hi1, (slab,)), (lo2, (-2,)), (hi2, (slab + 1,))
    )
    hidden = Planes(sizes, (hid_i, inner), (hid_e, edges), (hid_r, rims))
    planar1 = Planes(sizes, (pl1_i, inner), (pl1_e, edges), (pl1_r, rims))
    axial1 = Planes(sizes, (ax1_i, inner), (ax1_e, edges), (ax1_r, rims))
    planar2 = Planes(sizes, (pl2_i, inner), (pl2_e, edges))
    axial2 = Planes(sizes, (ax2_i, inner), (ax2_e, edges))
    grad_pre2 = Planes(sizes, (gpre2_i, inner), (gpre2_e, edges))
    grad_axial2 = Planes(sizes, (gax2_i, inner), (gax2_e, edges))
    tap_sums(0, wide, grad_planar1, volume, grad_axial1, planar1, sums)
    tap_sums(1, own, grad_planar2, hidden, grad_axial2, planar2, sums)
    mixing = (mixing_sum(wide, grad_pre1, axial1), mixing_sum(own, grad_pre2, axial2))
    lane = lax.broadcasted_iota(jnp.int32, (channels, payload.shape[2]), 1)
    for block in range(2):
        packed = jnp.zeros(payload.shape[1:], F32)
        for t in range(12):
            total = jnp.sum(sums[block, t], axis=1, keepdims=True)
            packed = packed + jnp.where(lane == channels + t, total, 0.0)
        payload[block] = packed * factor
        payload[block, :, :channels] = mixing[block] * factor


def volume_kernel(sizes, slab, taps, gpl1_i, gpl1_o, out):
    inner, outer = range(1, slab - 1), (-1, 0, slab - 1, slab)
    grad_planar = Planes(sizes, (gpl1_i, inner), (gpl1_o, outer))
    input_gradient(taps, 0, range(slab), grad_planar, Planes(sizes, (out, range(slab))), None)


def call(kernel, name, operands, outputs, scratch=(), flops=0, scalars=0):
    vmem = pl.BlockSpec(memory_space=pltpu.VMEM)
    smem = pl.BlockSpec(memory_space=pltpu.SMEM)
    return pl.pallas_call(
        kernel,
        name=name,
        out_shape=outputs,
        in_specs=[smem] * scalars + [vmem] * (len(operands) - scalars),
        out_specs=[vmem] * len(outputs),
        scratch_shapes=scratch,
        compiler_params=pltpu.CompilerParams(vmem_limit_bytes=32 << 20),
        cost_estimate=pl.CostEstimate(flops=flops, bytes_accessed=1 << 20, transcendentals=0),
    )(*operands)


def all_sum(total):
    for axis in ("dp", "sp"):
        count, step = lax.axis_size(axis), 1
        while step < count:
            mine = total.astype(BF16)
            other = lax.ppermute(mine, axis, [(i, i ^ step) for i in range(count)])
            total = mine.astype(F32) + other.astype(F32)
            step *= 2
    return total


def on_device(volume, cotangent, kernels_xy, kernels_z, mixing):
    _, channels, slab, nz, ny = volume.shape
    plane = nz * ny
    sizes = (channels, nz, ny)
    ranks, place = lax.axis_size("sp"), lax.axis_index("sp")
    up = [(i, i + 1) for i in range(ranks - 1)]
    down = [(j, i) for i, j in up]

    def flat(planes):
        return planes.reshape(channels, -1)

    lo1 = lax.ppermute(flat(volume[0, :, slab - 1]), "sp", up)
    hi1 = lax.ppermute(flat(volume[0, :, 0]), "sp", down)
    lo2 = lax.ppermute(flat(volume[0, :, slab - 2]), "sp", up)
    hi2 = lax.ppermute(flat(volume[0, :, 1]), "sp", down)
    vol, cot = flat(volume[0]), flat(cotangent[0])
    taps = wide_taps(kernels_xy, kernels_z, ny)
    mix, mix_t = mixing, jnp.swapaxes(mixing, 1, 2)
    flags = jnp.stack([place > 0, place < ranks - 1]).astype(F32)

    def planes(count):
        return jax.ShapeDtypeStruct((channels, count * plane), BF16)

    def scratch(count):
        return pltpu.VMEM((channels, count * plane), BF16)

    inside = slab - 2
    pl1_i, ax1_i, sl1_i, hid_i = call(
        functools.partial(inner_kernel, sizes, slab), "inner", (vol, taps, mix), [planes(inside)] * 4
    )
    pl1_e, ax1_e, sl1_e, hid_e, pl2_i, ax2_i, gpre2_i, gax2_i, gpl2_i = call(
        functools.partial(middle_kernel, sizes, slab),
        "middle",
        (vol, lo1, hi1, cot, taps, mix, mix_t, hid_i),
        [planes(2)] * 4 + [planes(inside)] * 5,
    )
    pl1_r, ax1_r, hid_r, pl2_e, ax2_e, gpre2_e, gax2_e, gpl2_e, gpre1_o, gax1_o, gpl1_o, send_lo, send_hi = call(
        functools.partial(edge_kernel, sizes, slab),
        "edge",
        (flags, vol, lo1, hi1, lo2, hi2, cot, taps, mix, mix_t, hid_i, hid_e, sl1_e, gpl2_i),
        [planes(2)] * 8 + [planes(4)] * 3 + [planes(2)] * 2,
        scratch=[scratch(2)],
        scalars=1,
    )
    from_lo = lax.ppermute(send_hi, "sp", up)
    from_hi = lax.ppermute(send_lo, "sp", down)
    count = lax.axis_size("dp") * slab * ranks * nz * ny

    def weight_sums(operands):
        gpl1_i, payload = call(
            functools.partial(weight_kernel, sizes, slab, 1.0 / math.sqrt(count)),
            "weights",
            operands,
            [planes(inside), jax.ShapeDtypeStruct((2, channels, 128), F32)],
            scratch=[scratch(inside), scratch(inside), pltpu.VMEM((2, 12, channels, ny), F32)],
        )
        return gpl1_i, all_sum(payload)

    def nothing(operands):
        return jnp.zeros((channels, inside * plane), BF16), jnp.zeros((2, channels, 128), F32)

    gpl1_i, total = lax.cond(
        place < ranks,
        weight_sums,
        nothing,
        (
            vol, lo1, hi1, lo2, hi2, taps, mix_t,
            pl1_i, ax1_i, sl1_i, hid_i, pl1_e, ax1_e, hid_e, pl2_i, ax2_i, gpre2_i, gax2_i, gpl2_i,
            pl1_r, ax1_r, hid_r, pl2_e, ax2_e, gpre2_e, gax2_e, gpl2_e, gpre1_o, gax1_o, gpl1_o,
        ),
    )
    (own,) = call(
        functools.partial(volume_kernel, sizes, slab), "volume", (taps, gpl1_i, gpl1_o), [planes(slab)]
    )
    parts = own.astype(F32).reshape(channels, slab, nz, ny)
    from_lo = from_lo.astype(F32).reshape(channels, 2, nz, ny)
    from_hi = from_hi.astype(F32).reshape(channels, 2, nz, ny)
    parts = parts + jnp.pad(from_lo, ((0, 0), (0, slab - 2), (0, 0), (0, 0)))
    parts = parts + jnp.pad(from_hi, ((0, 0), (slab - 2, 0), (0, 0), (0, 0)))
    return (
        parts.astype(BF16)[None],
        total[:, :, :channels],
        total[:, :, channels : channels + 9].reshape(2, channels, 3, 3),
        total[:, :, channels + 9 : channels + 12],
    )


def solution(mesh):
    return jax.shard_map(
        on_device,
        mesh=mesh,
        in_specs=(P("dp", None, "sp", None, None), P("dp", None, "sp", None, None), P(), P(), P()),
        out_specs=(P("dp", None, "sp", None, None), P(), P(), P()),
        check_vma=False,
    )
```

```python
import functools
import math

import jax
import jax.numpy as jnp
from jax import lax
from jax.experimental import pallas as pl
from jax.experimental.pallas import tpu as pltpu
from jax.sharding import PartitionSpec as P

GROUP = 16
BF16 = jnp.bfloat16
F32 = jnp.float32


class Planes:
    def __init__(self, sizes, *parts):
        self.channels, self.nz, self.ny = sizes
        self.at = {}
        for ref, indices in parts:
            for spot, index in enumerate(indices):
                self.at[index] = (ref, spot)

    def __contains__(self, index):
        return index in self.at

    def tile(self, index, z, rows):
        ref, spot = self.at[index]
        return ref.at[rows, pl.ds((spot * self.nz + z) * self.ny, self.ny)]

    def span(self, index, start, size):
        ref, spot = self.at[index]
        return ref.at[:, pl.ds(spot * self.nz * self.ny + start, size)]

    def get(self, index, z, rows):
        return self.tile(index, z, rows)[...].astype(F32)

    def put(self, index, z, rows, value):
        self.tile(index, z, rows)[...] = value.astype(BF16)


def over_groups(channels, body):
    def step(group, carry):
        body(pl.ds(pl.multiple_of(group * GROUP, GROUP), GROUP))
        return carry

    lax.fori_loop(0, channels // GROUP, step, 0, unroll=3)


def spread(taps_ref, block, rows, first, count):
    return [taps_ref[block, t, rows, :].astype(F32) for t in range(first, first + count)]


def plane_taps(taps_ref, block, rows, flip):
    taps = spread(taps_ref, block, rows, 9 if flip else 0, 9)
    return [taps[3 * i : 3 * i + 3] for i in range(3)]


def wide_taps(kernels_xy, kernels_z, ny):
    channels = kernels_xy.shape[1]
    lane = lax.broadcasted_iota(jnp.int32, (1, 1, 3, 1, ny), 4)
    column = lax.broadcasted_iota(jnp.int32, (1, 1, 3, 1, ny), 2)
    keep = ((column != 0) | (lane != ny - 1)) & ((column != 2) | (lane != 0))
    planes = jnp.moveaxis(kernels_xy, 1, 3)
    planes = jnp.concatenate([planes, planes[:, ::-1, ::-1]], axis=1)[..., None]
    planes = jnp.where(keep, planes, jnp.zeros((), planes.dtype)).reshape(2, 18, channels, ny)
    depth = jnp.broadcast_to(jnp.moveaxis(kernels_z, 1, 2)[..., None], (2, 3, channels, ny))
    return jnp.concatenate([planes, depth], axis=1)


def plane_conv(taps, source, index, z, rows, ny):
    sums = [None, None, None]
    for i in range(3):
        if index + i - 1 in source:
            value = source.get(index + i - 1, z, rows)
            for j in range(3):
                term = taps[i][j] * value
                sums[j] = term if sums[j] is None else sums[j] + term
    return sums[1] + pltpu.roll(sums[0], 1, 1) + pltpu.roll(sums[2], ny - 1, 1)


def depth_conv(taps, values, z):
    total = taps[1] * values[z]
    if z > 0:
        total = total + taps[0] * values[z - 1]
    if z < len(values) - 1:
        total = total + taps[2] * values[z + 1]
    return total


def forward_taps(taps_ref, block, indices, source, planar, axial):
    nz, ny = source.nz, source.ny

    def body(rows):
        taps = plane_taps(taps_ref, block, rows, False)
        depth = spread(taps_ref, block, rows, 18, 3)
        for index in indices:
            values = [plane_conv(taps, source, index, z, rows, ny) for z in range(nz)]
            for z in range(nz):
                planar.put(index, z, rows, values[z])
                axial.put(index, z, rows, depth_conv(depth, values, z))

    over_groups(source.channels, body)


def mixed(mix_ref, block, indices, source, use):
    size = source.nz * source.ny
    step = math.gcd(size, 256)
    weights = mix_ref[block]
    for index in indices:
        for start in range(0, size, step):
            product = jnp.dot(weights, source.span(index, start, step)[...], preferred_element_type=F32)
            use(index, start, step, product)


def gate(preact):
    sigma = 0.5 * jnp.tanh(0.5 * preact) + 0.5
    value = preact * sigma
    return value, sigma + value * (1.0 - sigma)


def hidden_of(mix_ref, indices, axial, hidden, slope, masks):
    def use(index, start, step, preact):
        value, rate = gate(preact)
        if index in masks:
            value, rate = value * masks[index], rate * masks[index]
        hidden.span(index, start, step)[...] = value.astype(BF16)
        slope.span(index, start, step)[...] = rate.astype(BF16)

    mixed(mix_ref, 0, indices, axial, use)


def top_gradient(mix_ref, indices, axial, cotangent, grad_pre):
    def use(index, start, step, preact):
        _, rate = gate(preact)
        grad = cotangent.span(index, start, step)[...].astype(F32) * rate
        grad_pre.span(index, start, step)[...] = grad.astype(BF16)

    mixed(mix_ref, 1, indices, axial, use)


def axial_gradient(mix_t_ref, block, indices, grad_pre, grad_axial):
    def use(index, start, step, product):
        grad_axial.span(index, start, step)[...] = product.astype(BF16)

    mixed(mix_t_ref, block, indices, grad_pre, use)


def planar_gradient(taps_ref, block, indices, grad_axial, grad_planar):
    nz = grad_axial.nz

    def body(rows):
        depth = spread(taps_ref, block, rows, 18, 3)[::-1]
        for index in indices:
            values = [grad_axial.get(index, z, rows) for z in range(nz)]
            for z in range(nz):
                grad_planar.put(index, z, rows, depth_conv(depth, values, z))

    over_groups(grad_axial.channels, body)


def input_gradient(taps_ref, block, indices, grad_planar, target, slope, start=None):
    nz, ny = grad_planar.nz, grad_planar.ny

    def body(rows):
        taps = plane_taps(taps_ref, block, rows, True)
        for index in indices:
            for z in range(nz):
                value = plane_conv(taps, grad_planar, index, z, rows, ny)
                if slope is not None:
                    value = value * slope.get(index, z, rows)
                if start is not None:
                    value = value + start.get(index, z, rows)
                target.put(index, z, rows, value)

    over_groups(grad_planar.channels, body)


def tap_sums(indices, grad_planar, source, grad_axial, planar, sums_ref, before=None):
    nz, ny = source.nz, source.ny

    def body(rows):
        lane = lax.broadcasted_iota(jnp.int32, (GROUP, ny), 1)
        sums = [None] * 12

        def add(tap, term):
            sums[tap] = term if sums[tap] is None else sums[tap] + term

        for index in indices:
            for z in range(nz):
                grad = grad_planar.get(index, z, rows)
                shifted = (pltpu.roll(grad, ny - 1, 1), grad, pltpu.roll(grad, 1, 1))
                for i in range(3):
                    if index + i - 1 in source:
                        value = source.get(index + i - 1, z, rows)
                        for j in range(3):
                            add(3 * i + j, shifted[j] * value)
                grad = grad_axial.get(index, z, rows)
                for t in range(3):
                    if 0 <= z + t - 1 < nz:
                        add(9 + t, grad * planar.get(index, z + t - 1, rows))
        for i in range(3):
            sums[3 * i] = jnp.where(lane != ny - 1, sums[3 * i], 0.0)
            sums[3 * i + 2] = jnp.where(lane != 0, sums[3 * i + 2], 0.0)
        for t in range(12):
            if before is not None:
                sums[t] = sums[t] + before[t, rows, :]
            sums_ref[t, rows, :] = sums[t]

    over_groups(source.channels, body)


def mixing_sum(indices, grad_pre, axial):
    size = grad_pre.nz * grad_pre.ny
    total = None
    for index in indices:
        term = lax.dot_general(
            grad_pre.span(index, 0, size)[...],
            axial.span(index, 0, size)[...],
            (((1,), (1,)), ((), ())),
            preferred_element_type=F32,
        )
        total = term if total is None else total + term
    return total


def sort_sides(odd, first, second, low, high):
    @pl.when(odd != 0)
    def _():
        low[...], high[...] = first[...], second[...]

    @pl.when(odd == 0)
    def _():
        low[...], high[...] = second[...], first[...]


def inner_kernel(sizes, slab, vol, taps, mix, pl1, ax1, sl1, hid):
    inner = range(1, slab - 1)
    planar, axial, slope, hidden = (Planes(sizes, (ref, inner)) for ref in (pl1, ax1, sl1, hid))
    forward_taps(taps, 0, inner, Planes(sizes, (vol, range(slab))), planar, axial)
    hidden_of(mix, inner, axial, hidden, slope, {})


def middle_kernel(
    sizes, slab, odd, vol, first, second, cot, taps, mix, mix_t, hid_i,
    lo1, hi1, pl1, ax1, sl1, hid, gpl2, sums, mixing, pl2, ax2, gpre2, gax2,
):
    inner, edges = range(1, slab - 1), (0, slab - 1)
    sort_sides(odd[0], first, second, lo1, hi1)
    volume = Planes(sizes, (vol, range(slab)), (lo1, (-1,)), (hi1, (slab,)))
    axial = Planes(sizes, (ax1, edges))
    forward_taps(taps, 0, edges, volume, Planes(sizes, (pl1, edges)), axial)
    hidden_of(mix, edges, axial, Planes(sizes, (hid, edges)), Planes(sizes, (sl1, edges)), {})
    hidden = Planes(sizes, (hid_i, inner), (hid, edges))
    cotangent = Planes(sizes, (cot, range(slab)))
    axial, grad_pre = Planes(sizes, (ax2, inner)), Planes(sizes, (gpre2, inner))
    grad_axial = Planes(sizes, (gax2, inner))
    planar, grad_planar = Planes(sizes, (pl2, inner)), Planes(sizes, (gpl2, inner))
    forward_taps(taps, 1, inner, hidden, planar, axial)
    top_gradient(mix, inner, axial, cotangent, grad_pre)
    axial_gradient(mix_t, 1, inner, grad_pre, grad_axial)
    planar_gradient(taps, 1, inner, grad_axial, grad_planar)
    tap_sums(inner, grad_planar, hidden, grad_axial, planar, sums)
    mixing[...] = mixing_sum(inner, grad_pre, axial)


def edge_kernel(
    sizes, slab, odd, flags, vol, lo1, hi1, first, second, cot, taps, mix, mix_t, hid_i, hid_e, sl1_e, gpl2_i,
    lo2, hi2, pl1, ax1, hid, pl2, ax2, gpre2, gax2, gpl2, gpre1, gax1, gpl1_lo, gpl1_hi, to_first, to_second, sl1,
):
    sort_sides(odd[0], first, second, lo2, hi2)
    inner, edges, rims = range(1, slab - 1), (0, slab - 1), (-1, slab)
    outer = (-1, 0, slab - 1, slab)
    masks = {-1: flags[0], slab: flags[1]}
    volume = Planes(
        sizes, (vol, range(slab)), (lo1, (-1,)), (hi1, (slab,)), (lo2, (-2,)), (hi2, (slab + 1,))
    )
    axial = Planes(sizes, (ax1, rims))
    forward_taps(taps, 0, rims, volume, Planes(sizes, (pl1, rims)), axial)
    hidden_of(mix, rims, axial, Planes(sizes, (hid, rims)), Planes(sizes, (sl1, rims)), masks)
    hidden = Planes(sizes, (hid_i, inner), (hid_e, edges), (hid, rims))
    cotangent = Planes(sizes, (cot, range(slab)))
    axial, grad_pre = Planes(sizes, (ax2, edges)), Planes(sizes, (gpre2, edges))
    grad_axial = Planes(sizes, (gax2, edges))
    forward_taps(taps, 1, edges, hidden, Planes(sizes, (pl2, edges)), axial)
    top_gradient(mix, edges, axial, cotangent, grad_pre)
    axial_gradient(mix_t, 1, edges, grad_pre, grad_axial)
    planar_gradient(taps, 1, edges, grad_axial, Planes(sizes, (gpl2, edges)))
    grad_planar = Planes(sizes, (gpl2, edges), (gpl2_i, inner))
    slope = Planes(sizes, (sl1_e, edges), (sl1, rims))
    grad_pre, grad_axial = Planes(sizes, (gpre1, outer)), Planes(sizes, (gax1, outer))
    input_gradient(taps, 1, outer, grad_planar, grad_pre, slope)
    axial_gradient(mix_t, 0, outer, grad_pre, grad_axial)
    grad_planar = Planes(sizes, (gpl1_lo, outer[:2]), (gpl1_hi, outer[2:]))
    planar_gradient(taps, 0, outer, grad_axial, grad_planar)
    sort_sides(odd[0], gpl1_lo, gpl1_hi, to_first, to_second)


def weight_kernel(
    sizes, slab, factor, vol, lo1, hi1, lo2, hi2, taps, mix_t,
    pl1_i, ax1_i, sl1_i, hid_i, pl1_e, ax1_e, hid_e, gpl2_i, sums_i, mixing_i,
    pl1_r, ax1_r, hid_r, pl2_e, ax2_e, gpre2_e, gax2_e, gpl2_e, gpre1_o, gax1_o, gpl1_lo, gpl1_hi,
    gpl1, payload, gpre1, gax1, sums,
):
    inner, edges, rims = range(1, slab - 1), (0, slab - 1), (-1, slab)
    outer, own, wide = (-1, 0, slab - 1, slab), range(slab), range(-1, slab + 1)
    channels, _, ny = sizes
    grad_planar2 = Planes(sizes, (gpl2_i, inner), (gpl2_e, edges))
    grad_pre1 = Planes(sizes, (gpre1, inner), (gpre1_o, outer))
    grad_axial1 = Planes(sizes, (gax1, inner), (gax1_o, outer))
    grad_planar1 = Planes(sizes, (gpl1, inner), (gpl1_lo, outer[:2]), (gpl1_hi, outer[2:]))
    input_gradient(taps, 1, inner, grad_planar2, grad_pre1, Planes(sizes, (sl1_i, inner)))
    axial_gradient(mix_t, 0, inner, grad_pre1, grad_axial1)
    planar_gradient(taps, 0, inner, grad_axial1, grad_planar1)
    volume = Planes(
        sizes, (vol, own), (lo1, (-1,)), (hi1, (slab,)), (lo2, (-2,)), (hi2, (slab + 1,))
    )
    hidden = Planes(sizes, (hid_i, inner), (hid_e, edges), (hid_r, rims))
    planar1 = Planes(sizes, (pl1_i, inner), (pl1_e, edges), (pl1_r, rims))
    axial1 = Planes(sizes, (ax1_i, inner), (ax1_e, edges), (ax1_r, rims))
    planar2, axial2 = Planes(sizes, (pl2_e, edges)), Planes(sizes, (ax2_e, edges))
    grad_pre2, grad_axial2 = Planes(sizes, (gpre2_e, edges)), Planes(sizes, (gax2_e, edges))
    tap_sums(wide, grad_planar1, volume, grad_axial1, planar1, sums.at[0])
    tap_sums(edges, grad_planar2, hidden, grad_axial2, planar2, sums.at[1], sums_i)
    mixing = (
        mixing_sum(wide, grad_pre1, axial1),
        mixing_sum(edges, grad_pre2, axial2) + mixing_i[...],
    )
    lane = lax.broadcasted_iota(jnp.int32, (channels, payload.shape[1]), 1)
    for block in range(2):
        at = block * channels
        payload[at : at + channels, :channels] = (mixing[block] * factor).astype(BF16)
        packed = jnp.zeros((channels, payload.shape[1]), F32)
        for t in range(12):
            total = jnp.sum(sums[block, t], axis=1, keepdims=True)
            packed = jnp.where(lane == t, total, packed)
        turned = (packed * factor).T
        at = 2 * channels + GROUP * block
        payload[at : at + GROUP, :channels] = turned[:GROUP].astype(BF16)


def volume_kernel(sizes, slab, taps, gpl1_i, gpl1_lo, gpl1_hi, out):
    inner, outer = range(1, slab - 1), (-1, 0, slab - 1, slab)
    grad_planar = Planes(sizes, (gpl1_i, inner), (gpl1_lo, outer[:2]), (gpl1_hi, outer[2:]))
    input_gradient(taps, 0, range(slab), grad_planar, Planes(sizes, (out, range(slab))), None)


def final_kernel(sizes, slab, odd, taps, own, first, second, out, from_lo, from_hi):
    sort_sides(odd[0], first, second, from_lo, from_hi)
    outer = (-1, 0, slab - 1, slab)
    arrived = Planes(sizes, (from_lo, outer[:2]), (from_hi, outer[2:]))
    start, result = Planes(sizes, (own, range(slab))), Planes(sizes, (out, range(slab)))
    input_gradient(taps, 0, range(slab), arrived, result, None, start)


def result_kernel(channels, mine, other, mixing, plane_taps, depth_taps):
    for block in range(2):
        rows = pl.ds(block * channels, channels)
        total = mine[rows, :].astype(F32) + other[rows, :].astype(F32)
        mixing[block] = total[:, :channels]
        rows = pl.ds(2 * channels + GROUP * block, GROUP)
        total = mine[rows, :].astype(F32) + other[rows, :].astype(F32)
        for t in range(9):
            plane_taps[t, block : block + 1, :] = total[t : t + 1, :channels]
        for t in range(3):
            depth_taps[t, block : block + 1, :] = total[9 + t : 10 + t, :channels]


def call(kernel, name, operands, outputs, scratch=(), cost=1, scalars=0):
    vmem = pl.BlockSpec(memory_space=pltpu.VMEM)
    smem = pl.BlockSpec(memory_space=pltpu.SMEM)
    return pl.pallas_call(
        kernel,
        name=name,
        out_shape=outputs,
        in_specs=[smem] * scalars + [vmem] * (len(operands) - scalars),
        out_specs=[vmem] * len(outputs),
        scratch_shapes=scratch,
        compiler_params=pltpu.CompilerParams(vmem_limit_bytes=16 << 20),
        cost_estimate=pl.CostEstimate(flops=0, bytes_accessed=cost, transcendentals=0),
    )(*operands)


def all_sum(mine, arrivals):
    arrived, spot, other = [], 0, None
    for axis in ("dp", "sp"):
        count, step = lax.axis_size(axis), 1
        while step < count:
            if other is not None:
                mine = (mine.astype(F32) + other.astype(F32)).astype(BF16)
            if spot in arrivals:
                mine, value = lax.optimization_barrier((mine, arrivals[spot]))
                arrived.append(value)
            other = lax.ppermute(mine, axis, [(i, i ^ step) for i in range(count)])
            step, spot = step * 2, spot + 1
    return mine, other, arrived


def on_device(volume, cotangent, kernels_xy, kernels_z, mixing):
    _, channels, slab, nz, ny = volume.shape
    plane = nz * ny
    sizes = (channels, nz, ny)
    ranks, place = lax.axis_size("sp"), lax.axis_index("sp")
    odd = place % 2
    firsts = [(i, i ^ 1) for i in range(ranks)]
    seconds = [(i, i + 1) for i in range(1, ranks - 1, 2)] + [(i + 1, i) for i in range(1, ranks - 1, 2)]

    def rims(slab_planes, low, high):
        low = slab_planes[:, low * plane : (low + 1) * plane]
        high = slab_planes[:, high * plane : (high + 1) * plane]
        return jnp.where(odd != 0, low, high), jnp.where(odd != 0, high, low)

    def exchange(sent):
        return lax.ppermute(sent[0], "sp", firsts), lax.ppermute(sent[1], "sp", seconds)

    vol = lax.optimization_barrier(volume[0].reshape(channels, -1))
    near = rims(vol, 0, slab - 1)
    later, *near = lax.optimization_barrier((vol, *near))
    near = exchange(near)
    far = exchange(rims(later, 1, slab - 2))
    cot = cotangent[0].reshape(channels, -1)
    taps = wide_taps(kernels_xy, kernels_z, ny)
    mix, mix_t = mixing, jnp.swapaxes(mixing, 1, 2)
    flags = jnp.stack([place > 0, place < ranks - 1]).astype(F32)
    odd = odd.reshape(1)

    def planes(count):
        return jax.ShapeDtypeStruct((channels, count * plane), BF16)

    def scratch(count):
        return pltpu.VMEM((channels, count * plane), BF16)

    def sums(*shape):
        return jax.ShapeDtypeStruct(shape, F32)

    inside = slab - 2
    pl1_i, ax1_i, sl1_i, hid_i = call(
        functools.partial(inner_kernel, sizes, slab),
        "inner",
        (vol, taps, mix),
        [planes(inside)] * 4,
        cost=4 << 20,
    )
    lo1, hi1, pl1_e, ax1_e, sl1_e, hid_e, gpl2_i, sums_i, mixing_i = call(
        functools.partial(middle_kernel, sizes, slab),
        "middle",
        (odd, vol, *near, cot, taps, mix, mix_t, hid_i),
        [planes(1)] * 2 + [planes(2)] * 4 + [planes(inside), sums(12, channels, ny), sums(channels, channels)],
        scratch=[scratch(inside)] * 4,
        scalars=1,
        cost=12 << 20,
    )
    (
        lo2, hi2, pl1_r, ax1_r, hid_r, pl2_e, ax2_e, gpre2_e, gax2_e, gpl2_e,
        gpre1_o, gax1_o, gpl1_lo, gpl1_hi, to_first, to_second,
    ) = call(
        functools.partial(edge_kernel, sizes, slab),
        "edge",
        (odd, flags, vol, lo1, hi1, *far, cot, taps, mix, mix_t, hid_i, hid_e, sl1_e, gpl2_i),
        [planes(1)] * 2 + [planes(2)] * 8 + [planes(4)] * 2 + [planes(2)] * 4,
        scratch=[scratch(2)],
        scalars=2,
        cost=18 << 20,
    )
    arrived = exchange((to_first, to_second))
    count = lax.axis_size("dp") * slab * ranks * nz * ny
    gpl1_i, payload = call(
        functools.partial(weight_kernel, sizes, slab, 1.0 / math.sqrt(count)),
        "weights",
        (
            vol, lo1, hi1, lo2, hi2, taps, mix_t,
            pl1_i, ax1_i, sl1_i, hid_i, pl1_e, ax1_e, hid_e, gpl2_i, sums_i, mixing_i,
            pl1_r, ax1_r, hid_r, pl2_e, ax2_e, gpre2_e, gax2_e, gpl2_e, gpre1_o, gax1_o, gpl1_lo, gpl1_hi,
        ),
        [planes(inside), jax.ShapeDtypeStruct((2 * channels + 2 * GROUP, 128), BF16)],
        scratch=[scratch(inside), scratch(inside), pltpu.VMEM((2, 12, channels, ny), F32)],
    )
    mine, other, arrived = all_sum(payload, {1: arrived[0], 4: arrived[1]})
    (own,) = call(
        functools.partial(volume_kernel, sizes, slab),
        "volume",
        (taps, gpl1_i, gpl1_lo, gpl1_hi),
        [planes(slab)],
    )
    (grad,) = call(
        functools.partial(final_kernel, sizes, slab),
        "final",
        (odd, taps, own, *arrived),
        [planes(slab)],
        scratch=[scratch(2)] * 2,
        scalars=1,
    )
    mixing_grad, plane_grad, depth_grad = call(
        functools.partial(result_kernel, channels),
        "result",
        (mine, other),
        [sums(2, channels, channels), sums(9, 2, channels), sums(3, 2, channels)],
    )
    return (
        grad.reshape(1, channels, slab, nz, ny),
        mixing_grad,
        jnp.transpose(plane_grad.reshape(3, 3, 2, channels), (2, 3, 0, 1)),
        jnp.transpose(depth_grad, (1, 2, 0)),
    )


def solution(mesh):
    return jax.shard_map(
        on_device,
        mesh=mesh,
        in_specs=(P("dp", None, "sp", None, None), P("dp", None, "sp", None, None), P(), P(), P()),
        out_specs=(P("dp", None, "sp", None, None), P(), P(), P()),
        check_vma=False,
    )
```

```python
import functools
import math

import jax
import jax.numpy as jnp
from jax import lax
from jax.experimental import pallas as pl
from jax.experimental.pallas import tpu as pltpu
from jax.sharding import PartitionSpec as P

GROUP = 16
BF16 = jnp.bfloat16
F32 = jnp.float32


class Planes:
    def __init__(self, sizes, *parts):
        self.channels, self.nz, self.ny = sizes
        self.at = {}
        for ref, indices in parts:
            for spot, index in enumerate(indices):
                self.at[index] = (ref, spot)

    def __contains__(self, index):
        return index in self.at

    def tile(self, index, z, rows):
        ref, spot = self.at[index]
        return ref.at[rows, pl.ds((spot * self.nz + z) * self.ny, self.ny)]

    def span(self, index, start, size):
        ref, spot = self.at[index]
        return ref.at[:, pl.ds(spot * self.nz * self.ny + start, size)]

    def get(self, index, z, rows):
        return self.tile(index, z, rows)[...].astype(F32)

    def put(self, index, z, rows, value):
        self.tile(index, z, rows)[...] = value.astype(BF16)


def over_groups(channels, body):
    def step(group, carry):
        body(pl.ds(pl.multiple_of(group * GROUP, GROUP), GROUP))
        return carry

    lax.fori_loop(0, channels // GROUP, step, 0, unroll=3)


def spread(taps_ref, block, rows, first, count):
    return [taps_ref[block, t, rows, :].astype(F32) for t in range(first, first + count)]


def plane_taps(taps_ref, block, rows, flip):
    taps = spread(taps_ref, block, rows, 9 if flip else 0, 9)
    return [taps[3 * i : 3 * i + 3] for i in range(3)]


def wide_taps(kernels_xy, kernels_z, ny):
    channels = kernels_xy.shape[1]
    lane = lax.broadcasted_iota(jnp.int32, (1, 1, 3, 1, ny), 4)
    column = lax.broadcasted_iota(jnp.int32, (1, 1, 3, 1, ny), 2)
    keep = ((column != 0) | (lane != ny - 1)) & ((column != 2) | (lane != 0))
    planes = jnp.moveaxis(kernels_xy, 1, 3)
    planes = jnp.concatenate([planes, planes[:, ::-1, ::-1]], axis=1)[..., None]
    planes = jnp.where(keep, planes, jnp.zeros((), planes.dtype)).reshape(2, 18, channels, ny)
    depth = jnp.broadcast_to(jnp.moveaxis(kernels_z, 1, 2)[..., None], (2, 3, channels, ny))
    return jnp.concatenate([planes, depth], axis=1)


def plane_conv(taps, source, index, z, rows, ny):
    sums = [None, None, None]
    for i in range(3):
        if index + i - 1 in source:
            value = source.get(index + i - 1, z, rows)
            for j in range(3):
                term = taps[i][j] * value
                sums[j] = term if sums[j] is None else sums[j] + term
    return sums[1] + pltpu.roll(sums[0], 1, 1) + pltpu.roll(sums[2], ny - 1, 1)


def depth_conv(taps, values, z):
    total = taps[1] * values[z]
    if z > 0:
        total = total + taps[0] * values[z - 1]
    if z < len(values) - 1:
        total = total + taps[2] * values[z + 1]
    return total


def forward_taps(taps_ref, block, indices, source, planar, axial):
    nz, ny = source.nz, source.ny

    def body(rows):
        taps = plane_taps(taps_ref, block, rows, False)
        depth = spread(taps_ref, block, rows, 18, 3)
        for index in indices:
            values = [plane_conv(taps, source, index, z, rows, ny) for z in range(nz)]
            for z in range(nz):
                planar.put(index, z, rows, values[z])
                axial.put(index, z, rows, depth_conv(depth, values, z))

    over_groups(source.channels, body)


def mixed(mix_ref, block, indices, source, use):
    size = source.nz * source.ny
    step = math.gcd(size, 256)
    weights = mix_ref[block]
    for index in indices:
        for start in range(0, size, step):
            product = jnp.dot(weights, source.span(index, start, step)[...], preferred_element_type=F32)
            use(index, start, step, product)


def gate(preact):
    sigma = 0.5 * jnp.tanh(0.5 * preact) + 0.5
    value = preact * sigma
    return value, sigma + value * (1.0 - sigma)


def hidden_of(mix_ref, indices, axial, hidden, slope, masks):
    def use(index, start, step, preact):
        value, rate = gate(preact)
        if index in masks:
            value, rate = value * masks[index], rate * masks[index]
        hidden.span(index, start, step)[...] = value.astype(BF16)
        slope.span(index, start, step)[...] = rate.astype(BF16)

    mixed(mix_ref, 0, indices, axial, use)


def top_gradient(mix_ref, indices, axial, cotangent, grad_pre):
    def use(index, start, step, preact):
        _, rate = gate(preact)
        grad = cotangent.span(index, start, step)[...].astype(F32) * rate
        grad_pre.span(index, start, step)[...] = grad.astype(BF16)

    mixed(mix_ref, 1, indices, axial, use)


def axial_gradient(mix_t_ref, block, indices, grad_pre, grad_axial):
    def use(index, start, step, product):
        grad_axial.span(index, start, step)[...] = product.astype(BF16)

    mixed(mix_t_ref, block, indices, grad_pre, use)


def planar_gradient(taps_ref, block, indices, grad_axial, grad_planar):
    nz = grad_axial.nz

    def body(rows):
        depth = spread(taps_ref, block, rows, 18, 3)[::-1]
        for index in indices:
            values = [grad_axial.get(index, z, rows) for z in range(nz)]
            for z in range(nz):
                grad_planar.put(index, z, rows, depth_conv(depth, values, z))

    over_groups(grad_axial.channels, body)


def input_gradient(taps_ref, block, indices, grad_planar, target, slope, start=None):
    nz, ny = grad_planar.nz, grad_planar.ny

    def body(rows):
        taps = plane_taps(taps_ref, block, rows, True)
        for index in indices:
            for z in range(nz):
                value = plane_conv(taps, grad_planar, index, z, rows, ny)
                if slope is not None:
                    value = value * slope.get(index, z, rows)
                if start is not None:
                    value = value + start.get(index, z, rows)
                target.put(index, z, rows, value)

    over_groups(grad_planar.channels, body)


def tap_sums(indices, grad_planar, source, grad_axial, planar, sums_ref, before=None):
    nz, ny = source.nz, source.ny

    def body(rows):
        lane = lax.broadcasted_iota(jnp.int32, (GROUP, ny), 1)
        sums = [None] * 12

        def add(tap, term):
            sums[tap] = term if sums[tap] is None else sums[tap] + term

        for index in indices:
            for z in range(nz):
                grad = grad_planar.get(index, z, rows)
                shifted = (pltpu.roll(grad, ny - 1, 1), grad, pltpu.roll(grad, 1, 1))
                for i in range(3):
                    if index + i - 1 in source:
                        value = source.get(index + i - 1, z, rows)
                        for j in range(3):
                            add(3 * i + j, shifted[j] * value)
                grad = grad_axial.get(index, z, rows)
                for t in range(3):
                    if 0 <= z + t - 1 < nz:
                        add(9 + t, grad * planar.get(index, z + t - 1, rows))
        for i in range(3):
            sums[3 * i] = jnp.where(lane != ny - 1, sums[3 * i], 0.0)
            sums[3 * i + 2] = jnp.where(lane != 0, sums[3 * i + 2], 0.0)
        for t in range(12):
            if before is not None:
                sums[t] = sums[t] + before[t, rows, :]
            sums_ref[t, rows, :] = sums[t]

    over_groups(source.channels, body)


def mixing_sum(indices, grad_pre, axial):
    size = grad_pre.nz * grad_pre.ny
    total = None
    for index in indices:
        term = lax.dot_general(
            grad_pre.span(index, 0, size)[...],
            axial.span(index, 0, size)[...],
            (((1,), (1,)), ((), ())),
            preferred_element_type=F32,
        )
        total = term if total is None else total + term
    return total


def sort_sides(odd, first, second, low, high):
    @pl.when(odd != 0)
    def _():
        low[...], high[...] = first[...], second[...]

    @pl.when(odd == 0)
    def _():
        low[...], high[...] = second[...], first[...]


def inner_kernel(sizes, slab, vol, taps, mix, pl1, ax1, sl1, hid):
    inner = range(1, slab - 1)
    planar, axial, slope, hidden = (Planes(sizes, (ref, inner)) for ref in (pl1, ax1, sl1, hid))
    forward_taps(taps, 0, inner, Planes(sizes, (vol, range(slab))), planar, axial)
    hidden_of(mix, inner, axial, hidden, slope, {})


def middle_kernel(
    sizes, slab, odd, vol, first, second, cot, taps, mix, mix_t, hid_i,
    lo1, hi1, pl1, ax1, sl1, hid, gpl2, sums, mixing, pl2, ax2, gpre2, gax2,
):
    inner, edges = range(1, slab - 1), (0, slab - 1)
    sort_sides(odd[0], first, second, lo1, hi1)
    volume = Planes(sizes, (vol, range(slab)), (lo1, (-1,)), (hi1, (slab,)))
    axial = Planes(sizes, (ax1, edges))
    forward_taps(taps, 0, edges, volume, Planes(sizes, (pl1, edges)), axial)
    hidden_of(mix, edges, axial, Planes(sizes, (hid, edges)), Planes(sizes, (sl1, edges)), {})
    hidden = Planes(sizes, (hid_i, inner), (hid, edges))
    cotangent = Planes(sizes, (cot, range(slab)))
    axial, grad_pre = Planes(sizes, (ax2, inner)), Planes(sizes, (gpre2, inner))
    grad_axial = Planes(sizes, (gax2, inner))
    planar, grad_planar = Planes(sizes, (pl2, inner)), Planes(sizes, (gpl2, inner))
    forward_taps(taps, 1, inner, hidden, planar, axial)
    top_gradient(mix, inner, axial, cotangent, grad_pre)
    axial_gradient(mix_t, 1, inner, grad_pre, grad_axial)
    planar_gradient(taps, 1, inner, grad_axial, grad_planar)
    tap_sums(inner, grad_planar, hidden, grad_axial, planar, sums)
    mixing[...] = mixing_sum(inner, grad_pre, axial)


def edge_kernel(
    sizes, slab, odd, flags, vol, lo1, hi1, first, second, cot, taps, mix, mix_t, hid_i, hid_e, sl1_e, gpl2_i,
    lo2, hi2, pl1, ax1, hid, pl2, ax2, gpre2, gax2, gpl2, gpre1, gax1, gpl1_lo, gpl1_hi, to_first, to_second, sl1,
):
    sort_sides(odd[0], first, second, lo2, hi2)
    inner, edges, rims = range(1, slab - 1), (0, slab - 1), (-1, slab)
    outer = (-1, 0, slab - 1, slab)
    masks = {-1: flags[0], slab: flags[1]}
    volume = Planes(
        sizes, (vol, range(slab)), (lo1, (-1,)), (hi1, (slab,)), (lo2, (-2,)), (hi2, (slab + 1,))
    )
    axial = Planes(sizes, (ax1, rims))
    forward_taps(taps, 0, rims, volume, Planes(sizes, (pl1, rims)), axial)
    hidden_of(mix, rims, axial, Planes(sizes, (hid, rims)), Planes(sizes, (sl1, rims)), masks)
    hidden = Planes(sizes, (hid_i, inner), (hid_e, edges), (hid, rims))
    cotangent = Planes(sizes, (cot, range(slab)))
    axial, grad_pre = Planes(sizes, (ax2, edges)), Planes(sizes, (gpre2, edges))
    grad_axial = Planes(sizes, (gax2, edges))
    forward_taps(taps, 1, edges, hidden, Planes(sizes, (pl2, edges)), axial)
    top_gradient(mix, edges, axial, cotangent, grad_pre)
    axial_gradient(mix_t, 1, edges, grad_pre, grad_axial)
    planar_gradient(taps, 1, edges, grad_axial, Planes(sizes, (gpl2, edges)))
    grad_planar = Planes(sizes, (gpl2, edges), (gpl2_i, inner))
    slope = Planes(sizes, (sl1_e, edges), (sl1, rims))
    grad_pre, grad_axial = Planes(sizes, (gpre1, outer)), Planes(sizes, (gax1, outer))
    input_gradient(taps, 1, outer, grad_planar, grad_pre, slope)
    axial_gradient(mix_t, 0, outer, grad_pre, grad_axial)
    grad_planar = Planes(sizes, (gpl1_lo, outer[:2]), (gpl1_hi, outer[2:]))
    planar_gradient(taps, 0, outer, grad_axial, grad_planar)
    sort_sides(odd[0], gpl1_lo, gpl1_hi, to_first, to_second)


def weight_kernel(
    sizes, slab, factor, vol, lo1, hi1, lo2, hi2, taps, mix_t,
    pl1_i, ax1_i, sl1_i, hid_i, pl1_e, ax1_e, hid_e, gpl2_i, sums_i, mixing_i,
    pl1_r, ax1_r, hid_r, pl2_e, ax2_e, gpre2_e, gax2_e, gpl2_e, gpre1_o, gax1_o, gpl1_lo, gpl1_hi,
    gpl1, payload, gpre1, gax1, sums,
):
    inner, edges, rims = range(1, slab - 1), (0, slab - 1), (-1, slab)
    outer, own, wide = (-1, 0, slab - 1, slab), range(slab), range(-1, slab + 1)
    channels, _, ny = sizes
    grad_planar2 = Planes(sizes, (gpl2_i, inner), (gpl2_e, edges))
    grad_pre1 = Planes(sizes, (gpre1, inner), (gpre1_o, outer))
    grad_axial1 = Planes(sizes, (gax1, inner), (gax1_o, outer))
    grad_planar1 = Planes(sizes, (gpl1, inner), (gpl1_lo, outer[:2]), (gpl1_hi, outer[2:]))
    input_gradient(taps, 1, inner, grad_planar2, grad_pre1, Planes(sizes, (sl1_i, inner)))
    axial_gradient(mix_t, 0, inner, grad_pre1, grad_axial1)
    planar_gradient(taps, 0, inner, grad_axial1, grad_planar1)
    volume = Planes(
        sizes, (vol, own), (lo1, (-1,)), (hi1, (slab,)), (lo2, (-2,)), (hi2, (slab + 1,))
    )
    hidden = Planes(sizes, (hid_i, inner), (hid_e, edges), (hid_r, rims))
    planar1 = Planes(sizes, (pl1_i, inner), (pl1_e, edges), (pl1_r, rims))
    axial1 = Planes(sizes, (ax1_i, inner), (ax1_e, edges), (ax1_r, rims))
    planar2, axial2 = Planes(sizes, (pl2_e, edges)), Planes(sizes, (ax2_e, edges))
    grad_pre2, grad_axial2 = Planes(sizes, (gpre2_e, edges)), Planes(sizes, (gax2_e, edges))
    tap_sums(wide, grad_planar1, volume, grad_axial1, planar1, sums.at[0])
    tap_sums(edges, grad_planar2, hidden, grad_axial2, planar2, sums.at[1], sums_i)
    mixing = (
        mixing_sum(wide, grad_pre1, axial1),
        mixing_sum(edges, grad_pre2, axial2) + mixing_i[...],
    )
    lane = lax.broadcasted_iota(jnp.int32, (channels, payload.shape[1]), 1)
    for block in range(2):
        at = block * channels
        payload[at : at + channels, :channels] = (mixing[block] * factor).astype(BF16)
        packed = jnp.zeros((channels, payload.shape[1]), F32)
        for t in range(12):
            total = jnp.sum(sums[block, t], axis=1, keepdims=True)
            packed = jnp.where(lane == t, total, packed)
        turned = (packed * factor).T
        at = 2 * channels + GROUP * block
        payload[at : at + GROUP, :channels] = turned[:GROUP].astype(BF16)


def volume_kernel(sizes, slab, taps, gpl1_i, gpl1_lo, gpl1_hi, out):
    inner, outer = range(1, slab - 1), (-1, 0, slab - 1, slab)
    grad_planar = Planes(sizes, (gpl1_i, inner), (gpl1_lo, outer[:2]), (gpl1_hi, outer[2:]))
    input_gradient(taps, 0, range(slab), grad_planar, Planes(sizes, (out, range(slab))), None)


def final_kernel(sizes, slab, odd, taps, own, first, second, out, from_lo, from_hi):
    sort_sides(odd[0], first, second, from_lo, from_hi)
    outer = (-1, 0, slab - 1, slab)
    arrived = Planes(sizes, (from_lo, outer[:2]), (from_hi, outer[2:]))
    start, result = Planes(sizes, (own, range(slab))), Planes(sizes, (out, range(slab)))
    input_gradient(taps, 0, range(slab), arrived, result, None, start)


def added(*terms):
    terms = [term.astype(F32) for term in terms]
    while len(terms) > 1:
        terms = [left + right for left, right in zip(terms[::2], terms[1::2])]
    return terms[0]


def result_kernel(channels, count, *refs):
    terms, (mixing, plane_taps, depth_taps) = refs[:count], refs[count:]
    for block in range(2):
        rows = pl.ds(block * channels, channels)
        total = added(*(term[rows, :] for term in terms))
        mixing[block] = total[:, :channels]
        rows = pl.ds(2 * channels + GROUP * block, GROUP)
        total = added(*(term[rows, :] for term in terms))
        for t in range(9):
            plane_taps[t, block : block + 1, :] = total[t : t + 1, :channels]
        for t in range(3):
            depth_taps[t, block : block + 1, :] = total[9 + t : 10 + t, :channels]


def call(kernel, name, operands, outputs, scratch=(), cost=1, scalars=0):
    vmem = pl.BlockSpec(memory_space=pltpu.VMEM)
    smem = pl.BlockSpec(memory_space=pltpu.SMEM)
    return pl.pallas_call(
        kernel,
        name=name,
        out_shape=outputs,
        in_specs=[smem] * scalars + [vmem] * (len(operands) - scalars),
        out_specs=[vmem] * len(outputs),
        scratch_shapes=scratch,
        compiler_params=pltpu.CompilerParams(vmem_limit_bytes=16 << 20),
        cost_estimate=pl.CostEstimate(flops=0, bytes_accessed=cost, transcendentals=0),
    )(*operands)


def all_sum(mine, arrivals):
    arrived, others = [], []
    for spot, (axis, steps) in enumerate((("sp", (2, 4, 6)), ("dp", (1, 2, 3)), ("sp", (1,)))):
        count = lax.axis_size(axis)
        if others:
            mine = added(mine, *others).astype(BF16)
        for value in arrivals.get(spot, ()):
            mine, value = lax.optimization_barrier((mine, value))
            arrived.append(value)
        others = [lax.ppermute(mine, axis, [(i, i ^ step) for i in range(count)]) for step in steps]
    for value in arrivals.get(-1, ()):
        arrived.append(value)
    return (mine, *others), arrived


def on_device(volume, cotangent, kernels_xy, kernels_z, mixing):
    _, channels, slab, nz, ny = volume.shape
    plane = nz * ny
    sizes = (channels, nz, ny)
    ranks, place = lax.axis_size("sp"), lax.axis_index("sp")
    odd = place % 2
    firsts = [(i, i ^ 1) for i in range(ranks)]
    seconds = [(i, i + 1) for i in range(1, ranks - 1, 2)] + [(i + 1, i) for i in range(1, ranks - 1, 2)]

    def rims(slab_planes, low, high):
        low = slab_planes[:, low * plane : (low + 1) * plane]
        high = slab_planes[:, high * plane : (high + 1) * plane]
        return jnp.where(odd != 0, low, high), jnp.where(odd != 0, high, low)

    def exchange(sent):
        return lax.ppermute(sent[0], "sp", firsts), lax.ppermute(sent[1], "sp", seconds)

    vol = lax.optimization_barrier(volume[0].reshape(channels, -1))
    near = rims(vol, 0, slab - 1)
    later, *near = lax.optimization_barrier((vol, *near))
    near = exchange(near)
    far = exchange(rims(later, 1, slab - 2))
    cot = cotangent[0].reshape(channels, -1)
    taps = wide_taps(kernels_xy, kernels_z, ny)
    mix, mix_t = mixing, jnp.swapaxes(mixing, 1, 2)
    flags = jnp.stack([place > 0, place < ranks - 1]).astype(F32)
    odd = odd.reshape(1)

    def planes(count):
        return jax.ShapeDtypeStruct((channels, count * plane), BF16)

    def scratch(count):
        return pltpu.VMEM((channels, count * plane), BF16)

    def sums(*shape):
        return jax.ShapeDtypeStruct(shape, F32)

    inside = slab - 2
    pl1_i, ax1_i, sl1_i, hid_i = call(
        functools.partial(inner_kernel, sizes, slab),
        "inner",
        (vol, taps, mix),
        [planes(inside)] * 4,
        cost=4 << 20,
    )
    lo1, hi1, pl1_e, ax1_e, sl1_e, hid_e, gpl2_i, sums_i, mixing_i = call(
        functools.partial(middle_kernel, sizes, slab),
        "middle",
        (odd, vol, *near, cot, taps, mix, mix_t, hid_i),
        [planes(1)] * 2 + [planes(2)] * 4 + [planes(inside), sums(12, channels, ny), sums(channels, channels)],
        scratch=[scratch(inside)] * 4,
        scalars=1,
        cost=12 << 20,
    )
    (
        lo2, hi2, pl1_r, ax1_r, hid_r, pl2_e, ax2_e, gpre2_e, gax2_e, gpl2_e,
        gpre1_o, gax1_o, gpl1_lo, gpl1_hi, to_first, to_second,
    ) = call(
        functools.partial(edge_kernel, sizes, slab),
        "edge",
        (odd, flags, vol, lo1, hi1, *far, cot, taps, mix, mix_t, hid_i, hid_e, sl1_e, gpl2_i),
        [planes(1)] * 2 + [planes(2)] * 8 + [planes(4)] * 2 + [planes(2)] * 4,
        scratch=[scratch(2)],
        scalars=2,
        cost=18 << 20,
    )
    arrived = exchange((to_first, to_second))
    count = lax.axis_size("dp") * slab * ranks * nz * ny
    gpl1_i, payload = call(
        functools.partial(weight_kernel, sizes, slab, 1.0 / math.sqrt(count)),
        "weights",
        (
            vol, lo1, hi1, lo2, hi2, taps, mix_t,
            pl1_i, ax1_i, sl1_i, hid_i, pl1_e, ax1_e, hid_e, gpl2_i, sums_i, mixing_i,
            pl1_r, ax1_r, hid_r, pl2_e, ax2_e, gpre2_e, gax2_e, gpl2_e, gpre1_o, gax1_o, gpl1_lo, gpl1_hi,
        ),
        [planes(inside), jax.ShapeDtypeStruct((2 * channels + 2 * GROUP, 128), BF16)],
        scratch=[scratch(inside), scratch(inside), pltpu.VMEM((2, 12, channels, ny), F32)],
    )
    terms, arrived = all_sum(payload, {1: arrived[:1], -1: arrived[1:]})
    (own,) = call(
        functools.partial(volume_kernel, sizes, slab),
        "volume",
        (taps, gpl1_i, gpl1_lo, gpl1_hi),
        [planes(slab)],
    )
    (grad,) = call(
        functools.partial(final_kernel, sizes, slab),
        "final",
        (odd, taps, own, *arrived),
        [planes(slab)],
        scratch=[scratch(2)] * 2,
        scalars=1,
    )
    mixing_grad, plane_grad, depth_grad = call(
        functools.partial(result_kernel, channels, len(terms)),
        "result",
        terms,
        [sums(2, channels, channels), sums(9, 2, channels), sums(3, 2, channels)],
    )
    return (
        grad.reshape(1, channels, slab, nz, ny),
        mixing_grad,
        jnp.transpose(plane_grad.reshape(3, 3, 2, channels), (2, 3, 0, 1)),
        jnp.transpose(depth_grad, (1, 2, 0)),
    )


def solution(mesh):
    return jax.shard_map(
        on_device,
        mesh=mesh,
        in_specs=(P("dp", None, "sp", None, None), P("dp", None, "sp", None, None), P(), P(), P()),
        out_specs=(P("dp", None, "sp", None, None), P(), P(), P()),
        check_vma=False,
    )
```

```python
import functools
import math

import jax
import jax.numpy as jnp
from jax import lax
from jax.experimental import pallas as pl
from jax.experimental.pallas import tpu as pltpu
from jax.sharding import PartitionSpec as P

GROUP = 16
BF16 = jnp.bfloat16
F32 = jnp.float32


class Planes:
    def __init__(self, sizes, *parts):
        self.channels, self.nz, self.ny = sizes
        self.at = {}
        for ref, indices in parts:
            for spot, index in enumerate(indices):
                self.at[index] = (ref, spot)

    def __contains__(self, index):
        return index in self.at

    def tile(self, index, z, rows):
        ref, spot = self.at[index]
        return ref.at[rows, pl.ds((spot * self.nz + z) * self.ny, self.ny)]

    def span(self, index, start, size):
        ref, spot = self.at[index]
        return ref.at[:, pl.ds(spot * self.nz * self.ny + start, size)]

    def get(self, index, z, rows):
        return self.tile(index, z, rows)[...].astype(F32)

    def put(self, index, z, rows, value):
        self.tile(index, z, rows)[...] = value.astype(BF16)


def over_groups(channels, body):
    def step(group, carry):
        body(pl.ds(pl.multiple_of(group * GROUP, GROUP), GROUP))
        return carry

    lax.fori_loop(0, channels // GROUP, step, 0, unroll=3)


def spread(taps_ref, block, rows, first, count):
    return [taps_ref[block, t, rows, :].astype(F32) for t in range(first, first + count)]


def plane_taps(taps_ref, block, rows, flip):
    taps = spread(taps_ref, block, rows, 9 if flip else 0, 9)
    return [taps[3 * i : 3 * i + 3] for i in range(3)]


def wide_taps(kernels_xy, kernels_z, ny):
    channels = kernels_xy.shape[1]
    lane = lax.broadcasted_iota(jnp.int32, (1, 1, 3, 1, ny), 4)
    column = lax.broadcasted_iota(jnp.int32, (1, 1, 3, 1, ny), 2)
    keep = ((column != 0) | (lane != ny - 1)) & ((column != 2) | (lane != 0))
    planes = jnp.moveaxis(kernels_xy, 1, 3)
    planes = jnp.concatenate([planes, planes[:, ::-1, ::-1]], axis=1)[..., None]
    planes = jnp.where(keep, planes, jnp.zeros((), planes.dtype)).reshape(2, 18, channels, ny)
    depth = jnp.broadcast_to(jnp.moveaxis(kernels_z, 1, 2)[..., None], (2, 3, channels, ny))
    return jnp.concatenate([planes, depth], axis=1)


def plane_conv(taps, source, index, z, rows, ny):
    sums = [None, None, None]
    for i in range(3):
        if index + i - 1 in source:
            value = source.get(index + i - 1, z, rows)
            for j in range(3):
                term = taps[i][j] * value
                sums[j] = term if sums[j] is None else sums[j] + term
    return sums[1] + pltpu.roll(sums[0], 1, 1) + pltpu.roll(sums[2], ny - 1, 1)


def depth_conv(taps, values, z):
    total = taps[1] * values[z]
    if z > 0:
        total = total + taps[0] * values[z - 1]
    if z < len(values) - 1:
        total = total + taps[2] * values[z + 1]
    return total


def forward_taps(taps_ref, block, indices, source, planar, axial):
    nz, ny = source.nz, source.ny

    def body(rows):
        taps = plane_taps(taps_ref, block, rows, False)
        depth = spread(taps_ref, block, rows, 18, 3)
        for index in indices:
            values = [plane_conv(taps, source, index, z, rows, ny) for z in range(nz)]
            for z in range(nz):
                planar.put(index, z, rows, values[z])
                axial.put(index, z, rows, depth_conv(depth, values, z))

    over_groups(source.channels, body)


def mixed(mix_ref, block, indices, source, use):
    size = source.nz * source.ny
    step = math.gcd(size, 256)
    weights = mix_ref[block]
    for index in indices:
        for start in range(0, size, step):
            product = jnp.dot(weights, source.span(index, start, step)[...], preferred_element_type=F32)
            use(index, start, step, product)


def gate(preact):
    sigma = 0.5 * jnp.tanh(0.5 * preact) + 0.5
    value = preact * sigma
    return value, sigma + value * (1.0 - sigma)


def hidden_of(mix_ref, indices, axial, hidden, slope, masks):
    def use(index, start, step, preact):
        value, rate = gate(preact)
        if index in masks:
            value, rate = value * masks[index], rate * masks[index]
        hidden.span(index, start, step)[...] = value.astype(BF16)
        slope.span(index, start, step)[...] = rate.astype(BF16)

    mixed(mix_ref, 0, indices, axial, use)


def top_gradient(mix_ref, indices, axial, cotangent, grad_pre):
    def use(index, start, step, preact):
        _, rate = gate(preact)
        grad = cotangent.span(index, start, step)[...].astype(F32) * rate
        grad_pre.span(index, start, step)[...] = grad.astype(BF16)

    mixed(mix_ref, 1, indices, axial, use)


def axial_gradient(mix_t_ref, block, indices, grad_pre, grad_axial):
    def use(index, start, step, product):
        grad_axial.span(index, start, step)[...] = product.astype(BF16)

    mixed(mix_t_ref, block, indices, grad_pre, use)


def planar_gradient(taps_ref, block, indices, grad_axial, grad_planar):
    nz = grad_axial.nz

    def body(rows):
        depth = spread(taps_ref, block, rows, 18, 3)[::-1]
        for index in indices:
            values = [grad_axial.get(index, z, rows) for z in range(nz)]
            for z in range(nz):
                grad_planar.put(index, z, rows, depth_conv(depth, values, z))

    over_groups(grad_axial.channels, body)


def input_gradient(taps_ref, block, indices, grad_planar, target, slope, start=None):
    nz, ny = grad_planar.nz, grad_planar.ny

    def body(rows):
        taps = plane_taps(taps_ref, block, rows, True)
        for index in indices:
            for z in range(nz):
                value = plane_conv(taps, grad_planar, index, z, rows, ny)
                if slope is not None:
                    value = value * slope.get(index, z, rows)
                if start is not None:
                    value = value + start.get(index, z, rows)
                target.put(index, z, rows, value)

    over_groups(grad_planar.channels, body)


def tap_sums(indices, grad_planar, source, grad_axial, planar, sums_ref, before=None):
    nz, ny = source.nz, source.ny

    def body(rows):
        lane = lax.broadcasted_iota(jnp.int32, (GROUP, ny), 1)
        sums = [None] * 12

        def add(tap, term):
            sums[tap] = term if sums[tap] is None else sums[tap] + term

        for index in indices:
            for z in range(nz):
                grad = grad_planar.get(index, z, rows)
                shifted = (pltpu.roll(grad, ny - 1, 1), grad, pltpu.roll(grad, 1, 1))
                for i in range(3):
                    if index + i - 1 in source:
                        value = source.get(index + i - 1, z, rows)
                        for j in range(3):
                            add(3 * i + j, shifted[j] * value)
                grad = grad_axial.get(index, z, rows)
                for t in range(3):
                    if 0 <= z + t - 1 < nz:
                        add(9 + t, grad * planar.get(index, z + t - 1, rows))
        for i in range(3):
            sums[3 * i] = jnp.where(lane != ny - 1, sums[3 * i], 0.0)
            sums[3 * i + 2] = jnp.where(lane != 0, sums[3 * i + 2], 0.0)
        for t in range(12):
            if before is not None:
                sums[t] = sums[t] + before[t, rows, :]
            sums_ref[t, rows, :] = sums[t]

    over_groups(source.channels, body)


def mixing_sum(indices, grad_pre, axial):
    size = grad_pre.nz * grad_pre.ny
    total = None
    for index in indices:
        term = lax.dot_general(
            grad_pre.span(index, 0, size)[...],
            axial.span(index, 0, size)[...],
            (((1,), (1,)), ((), ())),
            preferred_element_type=F32,
        )
        total = term if total is None else total + term
    return total


def sort_sides(odd, first, second, low, high):
    @pl.when(odd != 0)
    def _():
        low[...], high[...] = first[...], second[...]

    @pl.when(odd == 0)
    def _():
        low[...], high[...] = second[...], first[...]


def inner_kernel(sizes, slab, vol, taps, mix, pl1, ax1, sl1, hid):
    inner = range(1, slab - 1)
    planar, axial, slope, hidden = (Planes(sizes, (ref, inner)) for ref in (pl1, ax1, sl1, hid))
    forward_taps(taps, 0, inner, Planes(sizes, (vol, range(slab))), planar, axial)
    hidden_of(mix, inner, axial, hidden, slope, {})


def middle_kernel(
    sizes, slab, odd, vol, first, second, cot, taps, mix, mix_t, hid_i,
    lo1, hi1, pl1, ax1, sl1, hid, gpl2, sums, mixing, pl2, ax2, gpre2, gax2,
):
    inner, edges = range(1, slab - 1), (0, slab - 1)
    sort_sides(odd[0], first, second, lo1, hi1)
    volume = Planes(sizes, (vol, range(slab)), (lo1, (-1,)), (hi1, (slab,)))
    axial = Planes(sizes, (ax1, edges))
    forward_taps(taps, 0, edges, volume, Planes(sizes, (pl1, edges)), axial)
    hidden_of(mix, edges, axial, Planes(sizes, (hid, edges)), Planes(sizes, (sl1, edges)), {})
    hidden = Planes(sizes, (hid_i, inner), (hid, edges))
    cotangent = Planes(sizes, (cot, range(slab)))
    axial, grad_pre = Planes(sizes, (ax2, inner)), Planes(sizes, (gpre2, inner))
    grad_axial = Planes(sizes, (gax2, inner))
    planar, grad_planar = Planes(sizes, (pl2, inner)), Planes(sizes, (gpl2, inner))
    forward_taps(taps, 1, inner, hidden, planar, axial)
    top_gradient(mix, inner, axial, cotangent, grad_pre)
    axial_gradient(mix_t, 1, inner, grad_pre, grad_axial)
    planar_gradient(taps, 1, inner, grad_axial, grad_planar)
    tap_sums(inner, grad_planar, hidden, grad_axial, planar, sums)
    mixing[...] = mixing_sum(inner, grad_pre, axial)


def edge_kernel(
    sizes, slab, odd, flags, vol, lo1, hi1, first, second, cot, taps, mix, mix_t, hid_i, hid_e, sl1_e, gpl2_i,
    lo2, hi2, pl1, ax1, hid, pl2, ax2, gpre2, gax2, gpl2, gpre1, gax1, gpl1_lo, gpl1_hi, to_first, to_second, sl1,
):
    sort_sides(odd[0], first, second, lo2, hi2)
    inner, edges, rims = range(1, slab - 1), (0, slab - 1), (-1, slab)
    outer = (-1, 0, slab - 1, slab)
    masks = {-1: flags[0], slab: flags[1]}
    volume = Planes(
        sizes, (vol, range(slab)), (lo1, (-1,)), (hi1, (slab,)), (lo2, (-2,)), (hi2, (slab + 1,))
    )
    axial = Planes(sizes, (ax1, rims))
    forward_taps(taps, 0, rims, volume, Planes(sizes, (pl1, rims)), axial)
    hidden_of(mix, rims, axial, Planes(sizes, (hid, rims)), Planes(sizes, (sl1, rims)), masks)
    hidden = Planes(sizes, (hid_i, inner), (hid_e, edges), (hid, rims))
    cotangent = Planes(sizes, (cot, range(slab)))
    axial, grad_pre = Planes(sizes, (ax2, edges)), Planes(sizes, (gpre2, edges))
    grad_axial = Planes(sizes, (gax2, edges))
    forward_taps(taps, 1, edges, hidden, Planes(sizes, (pl2, edges)), axial)
    top_gradient(mix, edges, axial, cotangent, grad_pre)
    axial_gradient(mix_t, 1, edges, grad_pre, grad_axial)
    planar_gradient(taps, 1, edges, grad_axial, Planes(sizes, (gpl2, edges)))
    grad_planar = Planes(sizes, (gpl2, edges), (gpl2_i, inner))
    slope = Planes(sizes, (sl1_e, edges), (sl1, rims))
    grad_pre, grad_axial = Planes(sizes, (gpre1, outer)), Planes(sizes, (gax1, outer))
    input_gradient(taps, 1, outer, grad_planar, grad_pre, slope)
    axial_gradient(mix_t, 0, outer, grad_pre, grad_axial)
    grad_planar = Planes(sizes, (gpl1_lo, outer[:2]), (gpl1_hi, outer[2:]))
    planar_gradient(taps, 0, outer, grad_axial, grad_planar)
    sort_sides(odd[0], gpl1_lo, gpl1_hi, to_first, to_second)


def weight_kernel(
    sizes, slab, factor, vol, lo1, hi1, lo2, hi2, taps, mix_t,
    pl1_i, ax1_i, sl1_i, hid_i, pl1_e, ax1_e, hid_e, gpl2_i, sums_i, mixing_i,
    pl1_r, ax1_r, hid_r, pl2_e, ax2_e, gpre2_e, gax2_e, gpl2_e, gpre1_o, gax1_o, gpl1_lo, gpl1_hi,
    gpl1, payload, gpre1, gax1, sums,
):
    inner, edges, rims = range(1, slab - 1), (0, slab - 1), (-1, slab)
    outer, own, wide = (-1, 0, slab - 1, slab), range(slab), range(-1, slab + 1)
    channels, _, ny = sizes
    grad_planar2 = Planes(sizes, (gpl2_i, inner), (gpl2_e, edges))
    grad_pre1 = Planes(sizes, (gpre1, inner), (gpre1_o, outer))
    grad_axial1 = Planes(sizes, (gax1, inner), (gax1_o, outer))
    grad_planar1 = Planes(sizes, (gpl1, inner), (gpl1_lo, outer[:2]), (gpl1_hi, outer[2:]))
    input_gradient(taps, 1, inner, grad_planar2, grad_pre1, Planes(sizes, (sl1_i, inner)))
    axial_gradient(mix_t, 0, inner, grad_pre1, grad_axial1)
    planar_gradient(taps, 0, inner, grad_axial1, grad_planar1)
    volume = Planes(
        sizes, (vol, own), (lo1, (-1,)), (hi1, (slab,)), (lo2, (-2,)), (hi2, (slab + 1,))
    )
    hidden = Planes(sizes, (hid_i, inner), (hid_e, edges), (hid_r, rims))
    planar1 = Planes(sizes, (pl1_i, inner), (pl1_e, edges), (pl1_r, rims))
    axial1 = Planes(sizes, (ax1_i, inner), (ax1_e, edges), (ax1_r, rims))
    planar2, axial2 = Planes(sizes, (pl2_e, edges)), Planes(sizes, (ax2_e, edges))
    grad_pre2, grad_axial2 = Planes(sizes, (gpre2_e, edges)), Planes(sizes, (gax2_e, edges))
    tap_sums(wide, grad_planar1, volume, grad_axial1, planar1, sums.at[0])
    tap_sums(edges, grad_planar2, hidden, grad_axial2, planar2, sums.at[1], sums_i)
    mixing = (
        mixing_sum(wide, grad_pre1, axial1),
        mixing_sum(edges, grad_pre2, axial2) + mixing_i[...],
    )
    lane = lax.broadcasted_iota(jnp.int32, (channels, payload.shape[1]), 1)
    for block in range(2):
        at = block * channels
        payload[at : at + channels, :channels] = (mixing[block] * factor).astype(BF16)
        packed = jnp.zeros((channels, payload.shape[1]), F32)
        for t in range(12):
            total = jnp.sum(sums[block, t], axis=1, keepdims=True)
            packed = jnp.where(lane == t, total, packed)
        turned = (packed * factor).T
        at = 2 * channels + GROUP * block
        payload[at : at + GROUP, :channels] = turned[:GROUP].astype(BF16)


def volume_kernel(sizes, slab, taps, gpl1_i, gpl1_lo, gpl1_hi, out):
    inner, outer = range(1, slab - 1), (-1, 0, slab - 1, slab)
    grad_planar = Planes(sizes, (gpl1_i, inner), (gpl1_lo, outer[:2]), (gpl1_hi, outer[2:]))
    input_gradient(taps, 0, range(slab), grad_planar, Planes(sizes, (out, range(slab))), None)


def final_kernel(sizes, slab, odd, taps, own, first, second, out, from_lo, from_hi):
    sort_sides(odd[0], first, second, from_lo, from_hi)
    outer = (-1, 0, slab - 1, slab)
    arrived = Planes(sizes, (from_lo, outer[:2]), (from_hi, outer[2:]))
    start, result = Planes(sizes, (own, range(slab))), Planes(sizes, (out, range(slab)))
    input_gradient(taps, 0, range(slab), arrived, result, None, start)


def added(*terms):
    terms = [term.astype(F32) for term in terms]
    while len(terms) > 1:
        terms = [left + right for left, right in zip(terms[::2], terms[1::2])]
    return terms[0]


def result_kernel(channels, count, *refs):
    terms, (mixing, plane_taps, depth_taps) = refs[:count], refs[count:]
    for block in range(2):
        rows = pl.ds(block * channels, channels)
        total = added(*(term[rows, :] for term in terms))
        mixing[block] = total[:, :channels]
        rows = pl.ds(2 * channels + GROUP * block, GROUP)
        total = added(*(term[rows, :] for term in terms))
        for t in range(9):
            plane_taps[t, block : block + 1, :] = total[t : t + 1, :channels]
        for t in range(3):
            depth_taps[t, block : block + 1, :] = total[9 + t : 10 + t, :channels]


def call(kernel, name, operands, outputs, scratch=(), cost=1, scalars=0):
    vmem = pl.BlockSpec(memory_space=pltpu.VMEM)
    smem = pl.BlockSpec(memory_space=pltpu.SMEM)
    return pl.pallas_call(
        kernel,
        name=name,
        out_shape=outputs,
        in_specs=[smem] * scalars + [vmem] * (len(operands) - scalars),
        out_specs=[vmem] * len(outputs),
        scratch_shapes=scratch,
        compiler_params=pltpu.CompilerParams(vmem_limit_bytes=16 << 20),
        cost_estimate=pl.CostEstimate(flops=0, bytes_accessed=cost, transcendentals=0),
    )(*operands)


def chunks(bits):
    bits = list(bits)
    return [bits[at : at + 2] for at in range(0, len(bits), 2)]


def sum_groups(dp_bits, sp_bits):
    return chunks(range(dp_bits + 1, dp_bits + sp_bits)) + chunks(range(dp_bits)) + [[dp_bits]]


def all_sum(mine, arrivals):
    arrived, others = [], []
    dp_bits, sp_bits = (lax.axis_size(axis).bit_length() - 1 for axis in ("dp", "sp"))
    places = range(1 << (dp_bits + sp_bits))
    for spot, bits in enumerate(sum_groups(dp_bits, sp_bits)):
        if others:
            mine = added(mine, *others).astype(BF16)
        for value in arrivals.get(spot, ()):
            mine, value = lax.optimization_barrier((mine, value))
            arrived.append(value)
        steps = [1 << bits[0]]
        if len(bits) > 1:
            steps += [1 << bits[1], (1 << bits[0]) + (1 << bits[1])]
        others = [lax.ppermute(mine, ("sp", "dp"), [(i, i ^ step) for i in places]) for step in steps]
    for value in arrivals.get(-1, ()):
        arrived.append(value)
    return (mine, *others), arrived


def on_device(volume, cotangent, kernels_xy, kernels_z, mixing):
    _, channels, slab, nz, ny = volume.shape
    plane = nz * ny
    sizes = (channels, nz, ny)
    ranks, place = lax.axis_size("sp"), lax.axis_index("sp")
    odd = place % 2
    firsts = [(i, i ^ 1) for i in range(ranks)]
    seconds = [(i, i + 1) for i in range(1, ranks - 1, 2)] + [(i + 1, i) for i in range(1, ranks - 1, 2)]

    def rims(slab_planes, low, high):
        low = slab_planes[:, low * plane : (low + 1) * plane]
        high = slab_planes[:, high * plane : (high + 1) * plane]
        return jnp.where(odd != 0, low, high), jnp.where(odd != 0, high, low)

    def exchange(sent):
        return lax.ppermute(sent[0], "sp", firsts), lax.ppermute(sent[1], "sp", seconds)

    vol = lax.optimization_barrier(volume[0].reshape(channels, -1))
    near = rims(vol, 0, slab - 1)
    later, *near = lax.optimization_barrier((vol, *near))
    near = exchange(near)
    far = exchange(rims(later, 1, slab - 2))
    cot = cotangent[0].reshape(channels, -1)
    taps = wide_taps(kernels_xy, kernels_z, ny)
    mix, mix_t = mixing, jnp.swapaxes(mixing, 1, 2)
    flags = jnp.stack([place > 0, place < ranks - 1]).astype(F32)
    odd = odd.reshape(1)

    def planes(count):
        return jax.ShapeDtypeStruct((channels, count * plane), BF16)

    def scratch(count):
        return pltpu.VMEM((channels, count * plane), BF16)

    def sums(*shape):
        return jax.ShapeDtypeStruct(shape, F32)

    inside = slab - 2
    pl1_i, ax1_i, sl1_i, hid_i = call(
        functools.partial(inner_kernel, sizes, slab),
        "inner",
        (vol, taps, mix),
        [planes(inside)] * 4,
        cost=4 << 20,
    )
    lo1, hi1, pl1_e, ax1_e, sl1_e, hid_e, gpl2_i, sums_i, mixing_i = call(
        functools.partial(middle_kernel, sizes, slab),
        "middle",
        (odd, vol, *near, cot, taps, mix, mix_t, hid_i),
        [planes(1)] * 2 + [planes(2)] * 4 + [planes(inside), sums(12, channels, ny), sums(channels, channels)],
        scratch=[scratch(inside)] * 4,
        scalars=1,
        cost=12 << 20,
    )
    (
        lo2, hi2, pl1_r, ax1_r, hid_r, pl2_e, ax2_e, gpre2_e, gax2_e, gpl2_e,
        gpre1_o, gax1_o, gpl1_lo, gpl1_hi, to_first, to_second,
    ) = call(
        functools.partial(edge_kernel, sizes, slab),
        "edge",
        (odd, flags, vol, lo1, hi1, *far, cot, taps, mix, mix_t, hid_i, hid_e, sl1_e, gpl2_i),
        [planes(1)] * 2 + [planes(2)] * 8 + [planes(4)] * 2 + [planes(2)] * 4,
        scratch=[scratch(2)],
        scalars=2,
        cost=18 << 20,
    )
    arrived = exchange((to_first, to_second))
    count = lax.axis_size("dp") * slab * ranks * nz * ny
    gpl1_i, payload = call(
        functools.partial(weight_kernel, sizes, slab, 1.0 / math.sqrt(count)),
        "weights",
        (
            vol, lo1, hi1, lo2, hi2, taps, mix_t,
            pl1_i, ax1_i, sl1_i, hid_i, pl1_e, ax1_e, hid_e, gpl2_i, sums_i, mixing_i,
            pl1_r, ax1_r, hid_r, pl2_e, ax2_e, gpre2_e, gax2_e, gpl2_e, gpre1_o, gax1_o, gpl1_lo, gpl1_hi,
        ),
        [planes(inside), jax.ShapeDtypeStruct((2 * channels + 2 * GROUP, 128), BF16)],
        scratch=[scratch(inside), scratch(inside), pltpu.VMEM((2, 12, channels, ny), F32)],
    )
    terms, arrived = all_sum(payload, {1: arrived[:1], -1: arrived[1:]})
    (own,) = call(
        functools.partial(volume_kernel, sizes, slab),
        "volume",
        (taps, gpl1_i, gpl1_lo, gpl1_hi),
        [planes(slab)],
    )
    (grad,) = call(
        functools.partial(final_kernel, sizes, slab),
        "final",
        (odd, taps, own, *arrived),
        [planes(slab)],
        scratch=[scratch(2)] * 2,
        scalars=1,
    )
    mixing_grad, plane_grad, depth_grad = call(
        functools.partial(result_kernel, channels, len(terms)),
        "result",
        terms,
        [sums(2, channels, channels), sums(9, 2, channels), sums(3, 2, channels)],
    )
    return (
        grad.reshape(1, channels, slab, nz, ny),
        mixing_grad,
        jnp.transpose(plane_grad.reshape(3, 3, 2, channels), (2, 3, 0, 1)),
        jnp.transpose(depth_grad, (1, 2, 0)),
    )


def solution(mesh):
    return jax.shard_map(
        on_device,
        mesh=mesh,
        in_specs=(P("dp", None, "sp", None, None), P("dp", None, "sp", None, None), P(), P(), P()),
        out_specs=(P("dp", None, "sp", None, None), P(), P(), P()),
        check_vma=False,
    )
```

```python
import functools
import math

import jax
import jax.numpy as jnp
from jax import lax
from jax.experimental import pallas as pl
from jax.experimental.pallas import tpu as pltpu
from jax.sharding import PartitionSpec as P

GROUP = 16
BF16 = jnp.bfloat16
F32 = jnp.float32


class Planes:
    def __init__(self, sizes, *parts):
        self.channels, self.nz, self.ny = sizes
        self.at = {}
        for ref, indices in parts:
            for spot, index in enumerate(indices):
                self.at[index] = (ref, spot)

    def __contains__(self, index):
        return index in self.at

    def tile(self, index, z, rows):
        ref, spot = self.at[index]
        return ref.at[rows, pl.ds((spot * self.nz + z) * self.ny, self.ny)]

    def span(self, index, start, size):
        ref, spot = self.at[index]
        return ref.at[:, pl.ds(spot * self.nz * self.ny + start, size)]

    def get(self, index, z, rows):
        return self.tile(index, z, rows)[...].astype(F32)

    def put(self, index, z, rows, value):
        self.tile(index, z, rows)[...] = value.astype(BF16)


def over_groups(channels, body):
    def step(group, carry):
        body(pl.ds(pl.multiple_of(group * GROUP, GROUP), GROUP))
        return carry

    lax.fori_loop(0, channels // GROUP, step, 0, unroll=3)


def spread(taps_ref, block, rows, first, count):
    return [taps_ref[block, t, rows, :].astype(F32) for t in range(first, first + count)]


def plane_taps(taps_ref, block, rows, flip):
    taps = spread(taps_ref, block, rows, 9 if flip else 0, 9)
    return [taps[3 * i : 3 * i + 3] for i in range(3)]


def wide_taps(kernels_xy, kernels_z, ny):
    channels = kernels_xy.shape[1]
    lane = lax.broadcasted_iota(jnp.int32, (1, 1, 3, 1, ny), 4)
    column = lax.broadcasted_iota(jnp.int32, (1, 1, 3, 1, ny), 2)
    keep = ((column != 0) | (lane != ny - 1)) & ((column != 2) | (lane != 0))
    planes = jnp.moveaxis(kernels_xy, 1, 3)
    planes = jnp.concatenate([planes, planes[:, ::-1, ::-1]], axis=1)[..., None]
    planes = jnp.where(keep, planes, jnp.zeros((), planes.dtype)).reshape(2, 18, channels, ny)
    depth = jnp.broadcast_to(jnp.moveaxis(kernels_z, 1, 2)[..., None], (2, 3, channels, ny))
    return jnp.concatenate([planes, depth], axis=1)


def plane_conv(taps, source, index, z, rows, ny):
    sums = [None, None, None]
    for i in range(3):
        if index + i - 1 in source:
            value = source.get(index + i - 1, z, rows)
            for j in range(3):
                term = taps[i][j] * value
                sums[j] = term if sums[j] is None else sums[j] + term
    return sums[1] + pltpu.roll(sums[0], 1, 1) + pltpu.roll(sums[2], ny - 1, 1)


def depth_conv(taps, values, z):
    total = taps[1] * values[z]
    if z > 0:
        total = total + taps[0] * values[z - 1]
    if z < len(values) - 1:
        total = total + taps[2] * values[z + 1]
    return total


def forward_taps(taps_ref, block, indices, source, planar, axial):
    nz, ny = source.nz, source.ny

    def body(rows):
        taps = plane_taps(taps_ref, block, rows, False)
        depth = spread(taps_ref, block, rows, 18, 3)
        for index in indices:
            values = [plane_conv(taps, source, index, z, rows, ny) for z in range(nz)]
            for z in range(nz):
                planar.put(index, z, rows, values[z])
                axial.put(index, z, rows, depth_conv(depth, values, z))

    over_groups(source.channels, body)


def mixed(mix_ref, block, indices, source, use):
    size = source.nz * source.ny
    step = math.gcd(size, 256)
    weights = mix_ref[block]
    for index in indices:
        for start in range(0, size, step):
            product = jnp.dot(weights, source.span(index, start, step)[...], preferred_element_type=F32)
            use(index, start, step, product)


def gate(preact):
    sigma = 0.5 * jnp.tanh(0.5 * preact) + 0.5
    value = preact * sigma
    return value, sigma + value * (1.0 - sigma)


def hidden_of(mix_ref, indices, axial, hidden, slope, masks):
    def use(index, start, step, preact):
        value, rate = gate(preact)
        if index in masks:
            value, rate = value * masks[index], rate * masks[index]
        hidden.span(index, start, step)[...] = value.astype(BF16)
        slope.span(index, start, step)[...] = rate.astype(BF16)

    mixed(mix_ref, 0, indices, axial, use)


def top_gradient(mix_ref, indices, axial, cotangent, grad_pre):
    def use(index, start, step, preact):
        _, rate = gate(preact)
        grad = cotangent.span(index, start, step)[...].astype(F32) * rate
        grad_pre.span(index, start, step)[...] = grad.astype(BF16)

    mixed(mix_ref, 1, indices, axial, use)


def axial_gradient(mix_t_ref, block, indices, grad_pre, grad_axial):
    def use(index, start, step, product):
        grad_axial.span(index, start, step)[...] = product.astype(BF16)

    mixed(mix_t_ref, block, indices, grad_pre, use)


def planar_gradient(taps_ref, block, indices, grad_axial, grad_planar):
    nz = grad_axial.nz

    def body(rows):
        depth = spread(taps_ref, block, rows, 18, 3)[::-1]
        for index in indices:
            values = [grad_axial.get(index, z, rows) for z in range(nz)]
            for z in range(nz):
                grad_planar.put(index, z, rows, depth_conv(depth, values, z))

    over_groups(grad_axial.channels, body)


def input_gradient(taps_ref, block, indices, grad_planar, target, slope, start=None):
    nz, ny = grad_planar.nz, grad_planar.ny

    def body(rows):
        taps = plane_taps(taps_ref, block, rows, True)
        for index in indices:
            for z in range(nz):
                value = plane_conv(taps, grad_planar, index, z, rows, ny)
                if slope is not None:
                    value = value * slope.get(index, z, rows)
                if start is not None:
                    value = value + start.get(index, z, rows)
                target.put(index, z, rows, value)

    over_groups(grad_planar.channels, body)


def tap_sums(indices, grad_planar, source, grad_axial, planar, sums_ref, before=None):
    nz, ny = source.nz, source.ny

    def body(rows):
        lane = lax.broadcasted_iota(jnp.int32, (GROUP, ny), 1)
        sums = [None] * 12

        def add(tap, term):
            sums[tap] = term if sums[tap] is None else sums[tap] + term

        for index in indices:
            for z in range(nz):
                grad = grad_planar.get(index, z, rows)
                shifted = (pltpu.roll(grad, ny - 1, 1), grad, pltpu.roll(grad, 1, 1))
                for i in range(3):
                    if index + i - 1 in source:
                        value = source.get(index + i - 1, z, rows)
                        for j in range(3):
                            add(3 * i + j, shifted[j] * value)
                grad = grad_axial.get(index, z, rows)
                for t in range(3):
                    if 0 <= z + t - 1 < nz:
                        add(9 + t, grad * planar.get(index, z + t - 1, rows))
        for i in range(3):
            sums[3 * i] = jnp.where(lane != ny - 1, sums[3 * i], 0.0)
            sums[3 * i + 2] = jnp.where(lane != 0, sums[3 * i + 2], 0.0)
        for t in range(12):
            if before is not None:
                sums[t] = sums[t] + before[t, rows, :]
            sums_ref[t, rows, :] = sums[t]

    over_groups(source.channels, body)


def mixing_sum(indices, grad_pre, axial):
    size = grad_pre.nz * grad_pre.ny
    total = None
    for index in indices:
        term = lax.dot_general(
            grad_pre.span(index, 0, size)[...],
            axial.span(index, 0, size)[...],
            (((1,), (1,)), ((), ())),
            preferred_element_type=F32,
        )
        total = term if total is None else total + term
    return total


def rim_kernel(low, high, vol, first, second, plane_a, plane_b, arrived):
    odd = lax.rem(lax.axis_index("sp"), 2) != 0
    copies = [
        pltpu.make_async_copy(vol.at[0, :, jnp.where(odd, low, high)], plane_a, arrived.at[0]),
        pltpu.make_async_copy(vol.at[0, :, jnp.where(odd, high, low)], plane_b, arrived.at[1]),
    ]
    for copy in copies:
        copy.start()
    for copy, plane, out in zip(copies, (plane_a, plane_b), (first, second)):
        copy.wait()
        out[...] = plane[...].astype(F32).reshape(out.shape).astype(BF16)


def sort_sides(odd, first, second, low, high):
    @pl.when(odd != 0)
    def _():
        low[...], high[...] = first[...], second[...]

    @pl.when(odd == 0)
    def _():
        low[...], high[...] = second[...], first[...]


def inner_kernel(sizes, slab, vol, taps, mix, pl1, ax1, sl1, hid):
    inner = range(1, slab - 1)
    planar, axial, slope, hidden = (Planes(sizes, (ref, inner)) for ref in (pl1, ax1, sl1, hid))
    forward_taps(taps, 0, inner, Planes(sizes, (vol, range(slab))), planar, axial)
    hidden_of(mix, inner, axial, hidden, slope, {})


def middle_kernel(
    sizes, slab, odd, vol, first, second, cot, taps, mix, mix_t, hid_i,
    lo1, hi1, pl1, ax1, sl1, hid, gpl2, sums, mixing, pl2, ax2, gpre2, gax2,
):
    inner, edges = range(1, slab - 1), (0, slab - 1)
    sort_sides(odd[0], first, second, lo1, hi1)
    volume = Planes(sizes, (vol, range(slab)), (lo1, (-1,)), (hi1, (slab,)))
    axial = Planes(sizes, (ax1, edges))
    forward_taps(taps, 0, edges, volume, Planes(sizes, (pl1, edges)), axial)
    hidden_of(mix, edges, axial, Planes(sizes, (hid, edges)), Planes(sizes, (sl1, edges)), {})
    hidden = Planes(sizes, (hid_i, inner), (hid, edges))
    cotangent = Planes(sizes, (cot, range(slab)))
    axial, grad_pre = Planes(sizes, (ax2, inner)), Planes(sizes, (gpre2, inner))
    grad_axial = Planes(sizes, (gax2, inner))
    planar, grad_planar = Planes(sizes, (pl2, inner)), Planes(sizes, (gpl2, inner))
    forward_taps(taps, 1, inner, hidden, planar, axial)
    top_gradient(mix, inner, axial, cotangent, grad_pre)
    axial_gradient(mix_t, 1, inner, grad_pre, grad_axial)
    planar_gradient(taps, 1, inner, grad_axial, grad_planar)
    tap_sums(inner, grad_planar, hidden, grad_axial, planar, sums)
    mixing[...] = mixing_sum(inner, grad_pre, axial)


def edge_kernel(
    sizes, slab, odd, flags, vol, lo1, hi1, first, second, cot, taps, mix, mix_t, hid_i, hid_e, sl1_e, gpl2_i,
    lo2, hi2, pl1, ax1, hid, pl2, ax2, gpre2, gax2, gpl2, gpre1, gax1, gpl1_lo, gpl1_hi, to_first, to_second, sl1,
):
    sort_sides(odd[0], first, second, lo2, hi2)
    inner, edges, rims = range(1, slab - 1), (0, slab - 1), (-1, slab)
    outer = (-1, 0, slab - 1, slab)
    masks = {-1: flags[0], slab: flags[1]}
    volume = Planes(
        sizes, (vol, range(slab)), (lo1, (-1,)), (hi1, (slab,)), (lo2, (-2,)), (hi2, (slab + 1,))
    )
    axial = Planes(sizes, (ax1, rims))
    forward_taps(taps, 0, rims, volume, Planes(sizes, (pl1, rims)), axial)
    hidden_of(mix, rims, axial, Planes(sizes, (hid, rims)), Planes(sizes, (sl1, rims)), masks)
    hidden = Planes(sizes, (hid_i, inner), (hid_e, edges), (hid, rims))
    cotangent = Planes(sizes, (cot, range(slab)))
    axial, grad_pre = Planes(sizes, (ax2, edges)), Planes(sizes, (gpre2, edges))
    grad_axial = Planes(sizes, (gax2, edges))
    forward_taps(taps, 1, edges, hidden, Planes(sizes, (pl2, edges)), axial)
    top_gradient(mix, edges, axial, cotangent, grad_pre)
    axial_gradient(mix_t, 1, edges, grad_pre, grad_axial)
    planar_gradient(taps, 1, edges, grad_axial, Planes(sizes, (gpl2, edges)))
    grad_planar = Planes(sizes, (gpl2, edges), (gpl2_i, inner))
    slope = Planes(sizes, (sl1_e, edges), (sl1, rims))
    grad_pre, grad_axial = Planes(sizes, (gpre1, outer)), Planes(sizes, (gax1, outer))
    input_gradient(taps, 1, outer, grad_planar, grad_pre, slope)
    axial_gradient(mix_t, 0, outer, grad_pre, grad_axial)
    grad_planar = Planes(sizes, (gpl1_lo, outer[:2]), (gpl1_hi, outer[2:]))
    planar_gradient(taps, 0, outer, grad_axial, grad_planar)
    sort_sides(odd[0], gpl1_lo, gpl1_hi, to_first, to_second)


def weight_kernel(
    sizes, slab, factor, vol, lo1, hi1, lo2, hi2, taps, mix_t,
    pl1_i, ax1_i, sl1_i, hid_i, pl1_e, ax1_e, hid_e, gpl2_i, sums_i, mixing_i,
    pl1_r, ax1_r, hid_r, pl2_e, ax2_e, gpre2_e, gax2_e, gpl2_e, gpre1_o, gax1_o, gpl1_lo, gpl1_hi,
    gpl1, payload, gpre1, gax1, sums,
):
    inner, edges, rims = range(1, slab - 1), (0, slab - 1), (-1, slab)
    outer, own, wide = (-1, 0, slab - 1, slab), range(slab), range(-1, slab + 1)
    channels, _, ny = sizes
    grad_planar2 = Planes(sizes, (gpl2_i, inner), (gpl2_e, edges))
    grad_pre1 = Planes(sizes, (gpre1, inner), (gpre1_o, outer))
    grad_axial1 = Planes(sizes, (gax1, inner), (gax1_o, outer))
    grad_planar1 = Planes(sizes, (gpl1, inner), (gpl1_lo, outer[:2]), (gpl1_hi, outer[2:]))
    input_gradient(taps, 1, inner, grad_planar2, grad_pre1, Planes(sizes, (sl1_i, inner)))
    axial_gradient(mix_t, 0, inner, grad_pre1, grad_axial1)
    planar_gradient(taps, 0, inner, grad_axial1, grad_planar1)
    volume = Planes(
        sizes, (vol, own), (lo1, (-1,)), (hi1, (slab,)), (lo2, (-2,)), (hi2, (slab + 1,))
    )
    hidden = Planes(sizes, (hid_i, inner), (hid_e, edges), (hid_r, rims))
    planar1 = Planes(sizes, (pl1_i, inner), (pl1_e, edges), (pl1_r, rims))
    axial1 = Planes(sizes, (ax1_i, inner), (ax1_e, edges), (ax1_r, rims))
    planar2, axial2 = Planes(sizes, (pl2_e, edges)), Planes(sizes, (ax2_e, edges))
    grad_pre2, grad_axial2 = Planes(sizes, (gpre2_e, edges)), Planes(sizes, (gax2_e, edges))
    tap_sums(wide, grad_planar1, volume, grad_axial1, planar1, sums.at[0])
    tap_sums(edges, grad_planar2, hidden, grad_axial2, planar2, sums.at[1], sums_i)
    mixing = (
        mixing_sum(wide, grad_pre1, axial1),
        mixing_sum(edges, grad_pre2, axial2) + mixing_i[...],
    )
    lane = lax.broadcasted_iota(jnp.int32, (channels, payload.shape[1]), 1)
    for block in range(2):
        at = block * channels
        payload[at : at + channels, :channels] = (mixing[block] * factor).astype(BF16)
        packed = jnp.zeros((channels, payload.shape[1]), F32)
        for t in range(12):
            total = jnp.sum(sums[block, t], axis=1, keepdims=True)
            packed = jnp.where(lane == t, total, packed)
        turned = (packed * factor).T
        at = 2 * channels + GROUP * block
        payload[at : at + GROUP, :channels] = turned[:GROUP].astype(BF16)


def volume_kernel(sizes, slab, taps, gpl1_i, gpl1_lo, gpl1_hi, out):
    inner, outer = range(1, slab - 1), (-1, 0, slab - 1, slab)
    grad_planar = Planes(sizes, (gpl1_i, inner), (gpl1_lo, outer[:2]), (gpl1_hi, outer[2:]))
    input_gradient(taps, 0, range(slab), grad_planar, Planes(sizes, (out, range(slab))), None)


def final_kernel(sizes, slab, odd, taps, own, first, second, out, from_lo, from_hi):
    sort_sides(odd[0], first, second, from_lo, from_hi)
    outer = (-1, 0, slab - 1, slab)
    arrived = Planes(sizes, (from_lo, outer[:2]), (from_hi, outer[2:]))
    start, result = Planes(sizes, (own, range(slab))), Planes(sizes, (out, range(slab)))
    input_gradient(taps, 0, range(slab), arrived, result, None, start)


def added(*terms):
    terms = [term.astype(F32) for term in terms]
    while len(terms) > 1:
        terms = [left + right for left, right in zip(terms[::2], terms[1::2])]
    return terms[0]


def result_kernel(channels, count, *refs):
    terms, (mixing, plane_taps, depth_taps) = refs[:count], refs[count:]
    for block in range(2):
        rows = pl.ds(block * channels, channels)
        total = added(*(term[rows, :] for term in terms))
        mixing[block] = total[:, :channels]
        rows = pl.ds(2 * channels + GROUP * block, GROUP)
        total = added(*(term[rows, :] for term in terms))
        for t in range(9):
            plane_taps[t, block : block + 1, :] = total[t : t + 1, :channels]
        for t in range(3):
            depth_taps[t, block : block + 1, :] = total[9 + t : 10 + t, :channels]


def call(kernel, name, operands, outputs, scratch=(), cost=1, scalars=0):
    vmem = pl.BlockSpec(memory_space=pltpu.VMEM)
    smem = pl.BlockSpec(memory_space=pltpu.SMEM)
    return pl.pallas_call(
        kernel,
        name=name,
        out_shape=outputs,
        in_specs=[smem] * scalars + [vmem] * (len(operands) - scalars),
        out_specs=[vmem] * len(outputs),
        scratch_shapes=scratch,
        compiler_params=pltpu.CompilerParams(vmem_limit_bytes=16 << 20),
        cost_estimate=pl.CostEstimate(flops=0, bytes_accessed=cost, transcendentals=0),
    )(*operands)


def chunks(bits):
    bits = list(bits)
    return [bits[at : at + 2] for at in range(0, len(bits), 2)]


def sum_groups(dp_bits, sp_bits):
    return chunks(range(dp_bits + 1, dp_bits + sp_bits)) + chunks(range(dp_bits)) + [[dp_bits]]


def all_sum(mine, arrivals):
    arrived, others = [], []
    dp_bits, sp_bits = (lax.axis_size(axis).bit_length() - 1 for axis in ("dp", "sp"))
    places = range(1 << (dp_bits + sp_bits))
    for spot, bits in enumerate(sum_groups(dp_bits, sp_bits)):
        if others:
            mine = added(mine, *others).astype(BF16)
        for value in arrivals.get(spot, ()):
            mine, value = lax.optimization_barrier((mine, value))
            arrived.append(value)
        steps = [1 << bits[0]]
        if len(bits) > 1:
            steps += [1 << bits[1], (1 << bits[0]) + (1 << bits[1])]
        others = [lax.ppermute(mine, ("sp", "dp"), [(i, i ^ step) for i in places]) for step in steps]
    for value in arrivals.get(-1, ()):
        arrived.append(value)
    return (mine, *others), arrived


def on_device(volume, cotangent, kernels_xy, kernels_z, mixing):
    _, channels, slab, nz, ny = volume.shape
    plane = nz * ny
    sizes = (channels, nz, ny)
    ranks, place = lax.axis_size("sp"), lax.axis_index("sp")
    odd = place % 2
    firsts = [(i, i ^ 1) for i in range(ranks)]
    seconds = [(i, i + 1) for i in range(1, ranks - 1, 2)] + [(i + 1, i) for i in range(1, ranks - 1, 2)]

    def rims(volume, low, high, cost):
        return pl.pallas_call(
            functools.partial(rim_kernel, low, high),
            name="rims",
            out_shape=[jax.ShapeDtypeStruct((channels, plane), BF16)] * 2,
            in_specs=[pl.BlockSpec(memory_space=pl.ANY)],
            out_specs=[pl.BlockSpec(memory_space=pltpu.VMEM)] * 2,
            scratch_shapes=[pltpu.VMEM((channels, nz, ny), BF16)] * 2 + [pltpu.SemaphoreType.DMA((2,))],
            compiler_params=pltpu.CompilerParams(vmem_limit_bytes=16 << 20),
            cost_estimate=pl.CostEstimate(flops=0, bytes_accessed=cost, transcendentals=0),
        )(volume)

    def exchange(sent):
        return lax.ppermute(sent[0], "sp", firsts), lax.ppermute(sent[1], "sp", seconds)

    near = rims(volume, 0, slab - 1, 1)
    later, *near = lax.optimization_barrier((volume, *near))
    far = rims(later, 1, slab - 2, 3 << 20)
    near, far = exchange(near), exchange(far)
    vol = volume[0].reshape(channels, -1)
    cot = cotangent[0].reshape(channels, -1)
    taps = wide_taps(kernels_xy, kernels_z, ny)
    mix, mix_t = mixing, jnp.swapaxes(mixing, 1, 2)
    flags = jnp.stack([place > 0, place < ranks - 1]).astype(F32)
    odd = odd.reshape(1)

    def planes(count):
        return jax.ShapeDtypeStruct((channels, count * plane), BF16)

    def scratch(count):
        return pltpu.VMEM((channels, count * plane), BF16)

    def sums(*shape):
        return jax.ShapeDtypeStruct(shape, F32)

    inside = slab - 2
    pl1_i, ax1_i, sl1_i, hid_i = call(
        functools.partial(inner_kernel, sizes, slab),
        "inner",
        (vol, taps, mix),
        [planes(inside)] * 4,
        cost=4 << 20,
    )
    lo1, hi1, pl1_e, ax1_e, sl1_e, hid_e, gpl2_i, sums_i, mixing_i = call(
        functools.partial(middle_kernel, sizes, slab),
        "middle",
        (odd, vol, *near, cot, taps, mix, mix_t, hid_i),
        [planes(1)] * 2 + [planes(2)] * 4 + [planes(inside), sums(12, channels, ny), sums(channels, channels)],
        scratch=[scratch(inside)] * 4,
        scalars=1,
        cost=12 << 20,
    )
    (
        lo2, hi2, pl1_r, ax1_r, hid_r, pl2_e, ax2_e, gpre2_e, gax2_e, gpl2_e,
        gpre1_o, gax1_o, gpl1_lo, gpl1_hi, to_first, to_second,
    ) = call(
        functools.partial(edge_kernel, sizes, slab),
        "edge",
        (odd, flags, vol, lo1, hi1, *far, cot, taps, mix, mix_t, hid_i, hid_e, sl1_e, gpl2_i),
        [planes(1)] * 2 + [planes(2)] * 8 + [planes(4)] * 2 + [planes(2)] * 4,
        scratch=[scratch(2)],
        scalars=2,
        cost=18 << 20,
    )
    arrived = exchange((to_first, to_second))
    count = lax.axis_size("dp") * slab * ranks * nz * ny
    gpl1_i, payload = call(
        functools.partial(weight_kernel, sizes, slab, 1.0 / math.sqrt(count)),
        "weights",
        (
            vol, lo1, hi1, lo2, hi2, taps, mix_t,
            pl1_i, ax1_i, sl1_i, hid_i, pl1_e, ax1_e, hid_e, gpl2_i, sums_i, mixing_i,
            pl1_r, ax1_r, hid_r, pl2_e, ax2_e, gpre2_e, gax2_e, gpl2_e, gpre1_o, gax1_o, gpl1_lo, gpl1_hi,
        ),
        [planes(inside), jax.ShapeDtypeStruct((2 * channels + 2 * GROUP, 128), BF16)],
        scratch=[scratch(inside), scratch(inside), pltpu.VMEM((2, 12, channels, ny), F32)],
    )
    terms, arrived = all_sum(payload, {1: arrived[:1], -1: arrived[1:]})
    (own,) = call(
        functools.partial(volume_kernel, sizes, slab),
        "volume",
        (taps, gpl1_i, gpl1_lo, gpl1_hi),
        [planes(slab)],
    )
    (grad,) = call(
        functools.partial(final_kernel, sizes, slab),
        "final",
        (odd, taps, own, *arrived),
        [planes(slab)],
        scratch=[scratch(2)] * 2,
        scalars=1,
    )
    mixing_grad, plane_grad, depth_grad = call(
        functools.partial(result_kernel, channels, len(terms)),
        "result",
        terms,
        [sums(2, channels, channels), sums(9, 2, channels), sums(3, 2, channels)],
    )
    return (
        grad.reshape(1, channels, slab, nz, ny),
        mixing_grad,
        jnp.transpose(plane_grad.reshape(3, 3, 2, channels), (2, 3, 0, 1)),
        jnp.transpose(depth_grad, (1, 2, 0)),
    )


def solution(mesh):
    return jax.shard_map(
        on_device,
        mesh=mesh,
        in_specs=(P("dp", None, "sp", None, None), P("dp", None, "sp", None, None), P(), P(), P()),
        out_specs=(P("dp", None, "sp", None, None), P(), P(), P()),
        check_vma=False,
    )
```

```python
import functools
import math

import jax
import jax.numpy as jnp
from jax import lax
from jax.experimental import pallas as pl
from jax.experimental.pallas import tpu as pltpu
from jax.sharding import PartitionSpec as P

GROUP = 16
BF16 = jnp.bfloat16
F32 = jnp.float32


class Planes:
    def __init__(self, sizes, *parts):
        self.channels, self.nz, self.ny = sizes
        self.at = {}
        for ref, indices in parts:
            for spot, index in enumerate(indices):
                self.at[index] = (ref, spot)

    def __contains__(self, index):
        return index in self.at

    def tile(self, index, z, rows):
        ref, spot = self.at[index]
        return ref.at[rows, pl.ds((spot * self.nz + z) * self.ny, self.ny)]

    def span(self, index, start, size):
        ref, spot = self.at[index]
        return ref.at[:, pl.ds(spot * self.nz * self.ny + start, size)]

    def get(self, index, z, rows):
        return self.tile(index, z, rows)[...].astype(F32)

    def put(self, index, z, rows, value):
        self.tile(index, z, rows)[...] = value.astype(BF16)


def over_groups(channels, body):
    def step(group, carry):
        body(pl.ds(pl.multiple_of(group * GROUP, GROUP), GROUP))
        return carry

    lax.fori_loop(0, channels // GROUP, step, 0, unroll=3)


def spread(taps_ref, block, rows, first, count):
    return [taps_ref[block, t, rows, :].astype(F32) for t in range(first, first + count)]


def plane_taps(taps_ref, block, rows, flip):
    taps = spread(taps_ref, block, rows, 9 if flip else 0, 9)
    return [taps[3 * i : 3 * i + 3] for i in range(3)]


def wide_taps(kernels_xy, kernels_z, ny):
    channels = kernels_xy.shape[1]
    lane = lax.broadcasted_iota(jnp.int32, (1, 1, 3, 1, ny), 4)
    column = lax.broadcasted_iota(jnp.int32, (1, 1, 3, 1, ny), 2)
    keep = ((column != 0) | (lane != ny - 1)) & ((column != 2) | (lane != 0))
    planes = jnp.moveaxis(kernels_xy, 1, 3)
    planes = jnp.concatenate([planes, planes[:, ::-1, ::-1]], axis=1)[..., None]
    planes = jnp.where(keep, planes, jnp.zeros((), planes.dtype)).reshape(2, 18, channels, ny)
    depth = jnp.broadcast_to(jnp.moveaxis(kernels_z, 1, 2)[..., None], (2, 3, channels, ny))
    return jnp.concatenate([planes, depth], axis=1)


def plane_conv(taps, source, index, z, rows, ny):
    sums = [None, None, None]
    for i in range(3):
        if index + i - 1 in source:
            value = source.get(index + i - 1, z, rows)
            for j in range(3):
                term = taps[i][j] * value
                sums[j] = term if sums[j] is None else sums[j] + term
    return sums[1] + pltpu.roll(sums[0], 1, 1) + pltpu.roll(sums[2], ny - 1, 1)


def depth_conv(taps, values, z):
    total = taps[1] * values[z]
    if z > 0:
        total = total + taps[0] * values[z - 1]
    if z < len(values) - 1:
        total = total + taps[2] * values[z + 1]
    return total


def forward_taps(taps_ref, block, indices, source, planar, axial):
    nz, ny = source.nz, source.ny

    def body(rows):
        taps = plane_taps(taps_ref, block, rows, False)
        depth = spread(taps_ref, block, rows, 18, 3)
        for index in indices:
            values = [plane_conv(taps, source, index, z, rows, ny) for z in range(nz)]
            for z in range(nz):
                planar.put(index, z, rows, values[z])
                axial.put(index, z, rows, depth_conv(depth, values, z))

    over_groups(source.channels, body)


def mixed(mix_ref, block, indices, source, use):
    size = source.nz * source.ny
    step = math.gcd(size, 256)
    weights = mix_ref[block]
    for index in indices:
        for start in range(0, size, step):
            product = jnp.dot(weights, source.span(index, start, step)[...], preferred_element_type=F32)
            use(index, start, step, product)


def gate(preact):
    sigma = 0.5 * jnp.tanh(0.5 * preact) + 0.5
    value = preact * sigma
    return value, sigma + value * (1.0 - sigma)


def hidden_of(mix_ref, indices, axial, hidden, slope, masks):
    def use(index, start, step, preact):
        value, rate = gate(preact)
        if index in masks:
            value, rate = value * masks[index], rate * masks[index]
        hidden.span(index, start, step)[...] = value.astype(BF16)
        slope.span(index, start, step)[...] = rate.astype(BF16)

    mixed(mix_ref, 0, indices, axial, use)


def top_gradient(mix_ref, indices, axial, cotangent, grad_pre):
    def use(index, start, step, preact):
        _, rate = gate(preact)
        grad = cotangent.span(index, start, step)[...].astype(F32) * rate
        grad_pre.span(index, start, step)[...] = grad.astype(BF16)

    mixed(mix_ref, 1, indices, axial, use)


def axial_gradient(mix_t_ref, block, indices, grad_pre, grad_axial):
    def use(index, start, step, product):
        grad_axial.span(index, start, step)[...] = product.astype(BF16)

    mixed(mix_t_ref, block, indices, grad_pre, use)


def planar_gradient(taps_ref, block, indices, grad_axial, grad_planar):
    nz = grad_axial.nz

    def body(rows):
        depth = spread(taps_ref, block, rows, 18, 3)[::-1]
        for index in indices:
            values = [grad_axial.get(index, z, rows) for z in range(nz)]
            for z in range(nz):
                grad_planar.put(index, z, rows, depth_conv(depth, values, z))

    over_groups(grad_axial.channels, body)


def input_gradient(taps_ref, block, indices, grad_planar, target, slope, start=None):
    nz, ny = grad_planar.nz, grad_planar.ny

    def body(rows):
        taps = plane_taps(taps_ref, block, rows, True)
        for index in indices:
            for z in range(nz):
                value = plane_conv(taps, grad_planar, index, z, rows, ny)
                if slope is not None:
                    value = value * slope.get(index, z, rows)
                if start is not None:
                    value = value + start.get(index, z, rows)
                target.put(index, z, rows, value)

    over_groups(grad_planar.channels, body)


def tap_sums(indices, grad_planar, source, grad_axial, planar, sums_ref, before=None):
    nz, ny = source.nz, source.ny

    def body(rows):
        lane = lax.broadcasted_iota(jnp.int32, (GROUP, ny), 1)
        sums = [None] * 12 if before is None else [before[t, rows, :] for t in range(12)]
        for index in indices:
            part = [None] * 12

            def add(tap, term):
                part[tap] = term if part[tap] is None else part[tap] + term

            for z in range(nz):
                grad = grad_planar.tile(index, z, rows)[...]
                shifted = (pltpu.roll(grad, ny - 1, 1), grad, pltpu.roll(grad, 1, 1))
                for i in range(3):
                    if index + i - 1 in source:
                        value = source.tile(index + i - 1, z, rows)[...]
                        for j in range(3):
                            add(3 * i + j, shifted[j] * value)
                grad = grad_axial.tile(index, z, rows)[...]
                for t in range(3):
                    if 0 <= z + t - 1 < nz:
                        add(9 + t, grad * planar.tile(index, z + t - 1, rows)[...])
            for t in range(12):
                if part[t] is not None:
                    term = part[t].astype(F32)
                    sums[t] = term if sums[t] is None else sums[t] + term
        for i in range(3):
            sums[3 * i] = jnp.where(lane != ny - 1, sums[3 * i], 0.0)
            sums[3 * i + 2] = jnp.where(lane != 0, sums[3 * i + 2], 0.0)
        for t in range(12):
            sums_ref[t, rows, :] = sums[t]

    over_groups(source.channels, body)


def mixing_sum(indices, grad_pre, axial):
    size = grad_pre.nz * grad_pre.ny
    total = None
    for index in indices:
        term = lax.dot_general(
            grad_pre.span(index, 0, size)[...],
            axial.span(index, 0, size)[...],
            (((1,), (1,)), ((), ())),
            preferred_element_type=F32,
        )
        total = term if total is None else total + term
    return total


def rim_kernel(low, high, vol, first, second, plane_a, plane_b, arrived):
    odd = lax.rem(lax.axis_index("sp"), 2) != 0
    copies = [
        pltpu.make_async_copy(vol.at[0, :, jnp.where(odd, low, high)], plane_a, arrived.at[0]),
        pltpu.make_async_copy(vol.at[0, :, jnp.where(odd, high, low)], plane_b, arrived.at[1]),
    ]
    for copy in copies:
        copy.start()
    for copy, plane, out in zip(copies, (plane_a, plane_b), (first, second)):
        copy.wait()
        out[...] = plane[...].astype(F32).reshape(out.shape).astype(BF16)


def sort_sides(odd, first, second, low, high):
    @pl.when(odd != 0)
    def _():
        low[...], high[...] = first[...], second[...]

    @pl.when(odd == 0)
    def _():
        low[...], high[...] = second[...], first[...]


def inner_kernel(sizes, slab, vol, taps, mix, pl1, ax1, sl1, hid):
    inner = range(1, slab - 1)
    planar, axial, slope, hidden = (Planes(sizes, (ref, inner)) for ref in (pl1, ax1, sl1, hid))
    forward_taps(taps, 0, inner, Planes(sizes, (vol, range(slab))), planar, axial)
    hidden_of(mix, inner, axial, hidden, slope, {})


def middle_kernel(
    sizes, slab, odd, vol, first, second, cot, taps, mix, mix_t, hid_i,
    lo1, hi1, pl1, ax1, sl1, hid, gpl2, sums, mixing, pl2, ax2, gpre2, gax2,
):
    inner, edges = range(1, slab - 1), (0, slab - 1)
    sort_sides(odd[0], first, second, lo1, hi1)
    volume = Planes(sizes, (vol, range(slab)), (lo1, (-1,)), (hi1, (slab,)))
    axial = Planes(sizes, (ax1, edges))
    forward_taps(taps, 0, edges, volume, Planes(sizes, (pl1, edges)), axial)
    hidden_of(mix, edges, axial, Planes(sizes, (hid, edges)), Planes(sizes, (sl1, edges)), {})
    hidden = Planes(sizes, (hid_i, inner), (hid, edges))
    cotangent = Planes(sizes, (cot, range(slab)))
    axial, grad_pre = Planes(sizes, (ax2, inner)), Planes(sizes, (gpre2, inner))
    grad_axial = Planes(sizes, (gax2, inner))
    planar, grad_planar = Planes(sizes, (pl2, inner)), Planes(sizes, (gpl2, inner))
    forward_taps(taps, 1, inner, hidden, planar, axial)
    top_gradient(mix, inner, axial, cotangent, grad_pre)
    axial_gradient(mix_t, 1, inner, grad_pre, grad_axial)
    planar_gradient(taps, 1, inner, grad_axial, grad_planar)
    tap_sums(inner, grad_planar, hidden, grad_axial, planar, sums)
    mixing[...] = mixing_sum(inner, grad_pre, axial)


def edge_kernel(
    sizes, slab, odd, flags, vol, lo1, hi1, first, second, cot, taps, mix, mix_t, hid_i, hid_e, sl1_e, gpl2_i,
    lo2, hi2, pl1, ax1, hid, pl2, ax2, gpre2, gax2, gpl2, gpre1, gax1, gpl1_lo, gpl1_hi, to_first, to_second, sl1,
):
    sort_sides(odd[0], first, second, lo2, hi2)
    inner, edges, rims = range(1, slab - 1), (0, slab - 1), (-1, slab)
    outer = (-1, 0, slab - 1, slab)
    masks = {-1: flags[0], slab: flags[1]}
    volume = Planes(
        sizes, (vol, range(slab)), (lo1, (-1,)), (hi1, (slab,)), (lo2, (-2,)), (hi2, (slab + 1,))
    )
    axial = Planes(sizes, (ax1, rims))
    forward_taps(taps, 0, rims, volume, Planes(sizes, (pl1, rims)), axial)
    hidden_of(mix, rims, axial, Planes(sizes, (hid, rims)), Planes(sizes, (sl1, rims)), masks)
    hidden = Planes(sizes, (hid_i, inner), (hid_e, edges), (hid, rims))
    cotangent = Planes(sizes, (cot, range(slab)))
    axial, grad_pre = Planes(sizes, (ax2, edges)), Planes(sizes, (gpre2, edges))
    grad_axial = Planes(sizes, (gax2, edges))
    forward_taps(taps, 1, edges, hidden, Planes(sizes, (pl2, edges)), axial)
    top_gradient(mix, edges, axial, cotangent, grad_pre)
    axial_gradient(mix_t, 1, edges, grad_pre, grad_axial)
    planar_gradient(taps, 1, edges, grad_axial, Planes(sizes, (gpl2, edges)))
    grad_planar = Planes(sizes, (gpl2, edges), (gpl2_i, inner))
    slope = Planes(sizes, (sl1_e, edges), (sl1, rims))
    grad_pre, grad_axial = Planes(sizes, (gpre1, outer)), Planes(sizes, (gax1, outer))
    input_gradient(taps, 1, outer, grad_planar, grad_pre, slope)
    axial_gradient(mix_t, 0, outer, grad_pre, grad_axial)
    grad_planar = Planes(sizes, (gpl1_lo, outer[:2]), (gpl1_hi, outer[2:]))
    planar_gradient(taps, 0, outer, grad_axial, grad_planar)
    sort_sides(odd[0], gpl1_lo, gpl1_hi, to_first, to_second)


def weight_kernel(
    sizes, slab, factor, vol, lo1, hi1, lo2, hi2, taps, mix_t,
    pl1_i, ax1_i, sl1_i, hid_i, pl1_e, ax1_e, hid_e, gpl2_i, sums_i, mixing_i,
    pl1_r, ax1_r, hid_r, pl2_e, ax2_e, gpre2_e, gax2_e, gpl2_e, gpre1_o, gax1_o, gpl1_lo, gpl1_hi,
    gpl1, payload, gpre1, gax1, sums,
):
    inner, edges, rims = range(1, slab - 1), (0, slab - 1), (-1, slab)
    outer, own, wide = (-1, 0, slab - 1, slab), range(slab), range(-1, slab + 1)
    channels, _, ny = sizes
    grad_planar2 = Planes(sizes, (gpl2_i, inner), (gpl2_e, edges))
    grad_pre1 = Planes(sizes, (gpre1, inner), (gpre1_o, outer))
    grad_axial1 = Planes(sizes, (gax1, inner), (gax1_o, outer))
    grad_planar1 = Planes(sizes, (gpl1, inner), (gpl1_lo, outer[:2]), (gpl1_hi, outer[2:]))
    input_gradient(taps, 1, inner, grad_planar2, grad_pre1, Planes(sizes, (sl1_i, inner)))
    axial_gradient(mix_t, 0, inner, grad_pre1, grad_axial1)
    planar_gradient(taps, 0, inner, grad_axial1, grad_planar1)
    volume = Planes(
        sizes, (vol, own), (lo1, (-1,)), (hi1, (slab,)), (lo2, (-2,)), (hi2, (slab + 1,))
    )
    hidden = Planes(sizes, (hid_i, inner), (hid_e, edges), (hid_r, rims))
    planar1 = Planes(sizes, (pl1_i, inner), (pl1_e, edges), (pl1_r, rims))
    axial1 = Planes(sizes, (ax1_i, inner), (ax1_e, edges), (ax1_r, rims))
    planar2, axial2 = Planes(sizes, (pl2_e, edges)), Planes(sizes, (ax2_e, edges))
    grad_pre2, grad_axial2 = Planes(sizes, (gpre2_e, edges)), Planes(sizes, (gax2_e, edges))
    tap_sums(wide, grad_planar1, volume, grad_axial1, planar1, sums.at[0])
    tap_sums(edges, grad_planar2, hidden, grad_axial2, planar2, sums.at[1], sums_i)
    mixing = (
        mixing_sum(wide, grad_pre1, axial1),
        mixing_sum(edges, grad_pre2, axial2) + mixing_i[...],
    )
    lane = lax.broadcasted_iota(jnp.int32, (channels, payload.shape[1]), 1)
    for block in range(2):
        at = block * channels
        payload[at : at + channels, :channels] = (mixing[block] * factor).astype(BF16)
        packed = jnp.zeros((channels, payload.shape[1]), F32)
        for t in range(12):
            total = jnp.sum(sums[block, t], axis=1, keepdims=True)
            packed = jnp.where(lane == t, total, packed)
        turned = (packed * factor).T
        at = 2 * channels + GROUP * block
        payload[at : at + GROUP, :channels] = turned[:GROUP].astype(BF16)


def volume_kernel(sizes, slab, taps, gpl1_i, gpl1_lo, gpl1_hi, out):
    inner, outer = range(1, slab - 1), (-1, 0, slab - 1, slab)
    grad_planar = Planes(sizes, (gpl1_i, inner), (gpl1_lo, outer[:2]), (gpl1_hi, outer[2:]))
    input_gradient(taps, 0, range(slab), grad_planar, Planes(sizes, (out, range(slab))), None)


def final_kernel(sizes, slab, odd, taps, own, first, second, out, from_lo, from_hi):
    sort_sides(odd[0], first, second, from_lo, from_hi)
    outer = (-1, 0, slab - 1, slab)
    arrived = Planes(sizes, (from_lo, outer[:2]), (from_hi, outer[2:]))
    start, result = Planes(sizes, (own, range(slab))), Planes(sizes, (out, range(slab)))
    input_gradient(taps, 0, range(slab), arrived, result, None, start)


def added(*terms):
    terms = [term.astype(F32) for term in terms]
    while len(terms) > 1:
        terms = [left + right for left, right in zip(terms[::2], terms[1::2])]
    return terms[0]


def result_kernel(channels, count, *refs):
    terms, (mixing, plane_taps, depth_taps) = refs[:count], refs[count:]
    for block in range(2):
        rows = pl.ds(block * channels, channels)
        total = added(*(term[rows, :] for term in terms))
        mixing[block] = total[:, :channels]
        rows = pl.ds(2 * channels + GROUP * block, GROUP)
        total = added(*(term[rows, :] for term in terms))
        for t in range(9):
            plane_taps[t, block : block + 1, :] = total[t : t + 1, :channels]
        for t in range(3):
            depth_taps[t, block : block + 1, :] = total[9 + t : 10 + t, :channels]


def call(kernel, name, operands, outputs, scratch=(), cost=1, scalars=0):
    vmem = pl.BlockSpec(memory_space=pltpu.VMEM)
    smem = pl.BlockSpec(memory_space=pltpu.SMEM)
    return pl.pallas_call(
        kernel,
        name=name,
        out_shape=outputs,
        in_specs=[smem] * scalars + [vmem] * (len(operands) - scalars),
        out_specs=[vmem] * len(outputs),
        scratch_shapes=scratch,
        compiler_params=pltpu.CompilerParams(vmem_limit_bytes=16 << 20),
        cost_estimate=pl.CostEstimate(flops=0, bytes_accessed=cost, transcendentals=0),
    )(*operands)


def chunks(bits):
    bits = list(bits)
    return [bits[at : at + 2] for at in range(0, len(bits), 2)]


def sum_groups(dp_bits, sp_bits):
    return chunks(range(dp_bits + 1, dp_bits + sp_bits)) + chunks(range(dp_bits)) + [[dp_bits]]


def all_sum(mine, arrivals):
    arrived, others = [], []
    dp_bits, sp_bits = (lax.axis_size(axis).bit_length() - 1 for axis in ("dp", "sp"))
    places = range(1 << (dp_bits + sp_bits))
    for spot, bits in enumerate(sum_groups(dp_bits, sp_bits)):
        if others:
            mine = added(mine, *others).astype(BF16)
        for value in arrivals.get(spot, ()):
            mine, value = lax.optimization_barrier((mine, value))
            arrived.append(value)
        steps = [1 << bits[0]]
        if len(bits) > 1:
            steps += [1 << bits[1], (1 << bits[0]) + (1 << bits[1])]
        others = [lax.ppermute(mine, ("sp", "dp"), [(i, i ^ step) for i in places]) for step in steps]
    for value in arrivals.get(-1, ()):
        arrived.append(value)
    return (mine, *others), arrived


def on_device(volume, cotangent, kernels_xy, kernels_z, mixing):
    _, channels, slab, nz, ny = volume.shape
    plane = nz * ny
    sizes = (channels, nz, ny)
    ranks, place = lax.axis_size("sp"), lax.axis_index("sp")
    odd = place % 2
    firsts = [(i, i ^ 1) for i in range(ranks)]
    seconds = [(i, i + 1) for i in range(1, ranks - 1, 2)] + [(i + 1, i) for i in range(1, ranks - 1, 2)]

    def rims(volume, low, high, cost):
        return pl.pallas_call(
            functools.partial(rim_kernel, low, high),
            name="rims",
            out_shape=[jax.ShapeDtypeStruct((channels, plane), BF16)] * 2,
            in_specs=[pl.BlockSpec(memory_space=pl.ANY)],
            out_specs=[pl.BlockSpec(memory_space=pltpu.VMEM)] * 2,
            scratch_shapes=[pltpu.VMEM((channels, nz, ny), BF16)] * 2 + [pltpu.SemaphoreType.DMA((2,))],
            compiler_params=pltpu.CompilerParams(vmem_limit_bytes=16 << 20),
            cost_estimate=pl.CostEstimate(flops=0, bytes_accessed=cost, transcendentals=0),
        )(volume)

    def exchange(sent):
        return lax.ppermute(sent[0], "sp", firsts), lax.ppermute(sent[1], "sp", seconds)

    near = rims(volume, 0, slab - 1, 1)
    later, *near = lax.optimization_barrier((volume, *near))
    far = rims(later, 1, slab - 2, 3 << 20)
    near, far = exchange(near), exchange(far)
    vol = volume[0].reshape(channels, -1)
    cot = cotangent[0].reshape(channels, -1)
    taps = wide_taps(kernels_xy, kernels_z, ny)
    mix, mix_t = mixing, jnp.swapaxes(mixing, 1, 2)
    flags = jnp.stack([place > 0, place < ranks - 1]).astype(F32)
    odd = odd.reshape(1)

    def planes(count):
        return jax.ShapeDtypeStruct((channels, count * plane), BF16)

    def scratch(count):
        return pltpu.VMEM((channels, count * plane), BF16)

    def sums(*shape):
        return jax.ShapeDtypeStruct(shape, F32)

    inside = slab - 2
    pl1_i, ax1_i, sl1_i, hid_i = call(
        functools.partial(inner_kernel, sizes, slab),
        "inner",
        (vol, taps, mix),
        [planes(inside)] * 4,
        cost=4 << 20,
    )
    lo1, hi1, pl1_e, ax1_e, sl1_e, hid_e, gpl2_i, sums_i, mixing_i = call(
        functools.partial(middle_kernel, sizes, slab),
        "middle",
        (odd, vol, *near, cot, taps, mix, mix_t, hid_i),
        [planes(1)] * 2 + [planes(2)] * 4 + [planes(inside), sums(12, channels, ny), sums(channels, channels)],
        scratch=[scratch(inside)] * 4,
        scalars=1,
        cost=12 << 20,
    )
    (
        lo2, hi2, pl1_r, ax1_r, hid_r, pl2_e, ax2_e, gpre2_e, gax2_e, gpl2_e,
        gpre1_o, gax1_o, gpl1_lo, gpl1_hi, to_first, to_second,
    ) = call(
        functools.partial(edge_kernel, sizes, slab),
        "edge",
        (odd, flags, vol, lo1, hi1, *far, cot, taps, mix, mix_t, hid_i, hid_e, sl1_e, gpl2_i),
        [planes(1)] * 2 + [planes(2)] * 8 + [planes(4)] * 2 + [planes(2)] * 4,
        scratch=[scratch(2)],
        scalars=2,
        cost=18 << 20,
    )
    arrived = exchange((to_first, to_second))
    count = lax.axis_size("dp") * slab * ranks * nz * ny
    gpl1_i, payload = call(
        functools.partial(weight_kernel, sizes, slab, 1.0 / math.sqrt(count)),
        "weights",
        (
            vol, lo1, hi1, lo2, hi2, taps, mix_t,
            pl1_i, ax1_i, sl1_i, hid_i, pl1_e, ax1_e, hid_e, gpl2_i, sums_i, mixing_i,
            pl1_r, ax1_r, hid_r, pl2_e, ax2_e, gpre2_e, gax2_e, gpl2_e, gpre1_o, gax1_o, gpl1_lo, gpl1_hi,
        ),
        [planes(inside), jax.ShapeDtypeStruct((2 * channels + 2 * GROUP, 128), BF16)],
        scratch=[scratch(inside), scratch(inside), pltpu.VMEM((2, 12, channels, ny), F32)],
    )
    terms, arrived = all_sum(payload, {1: arrived[:1], -1: arrived[1:]})
    (own,) = call(
        functools.partial(volume_kernel, sizes, slab),
        "volume",
        (taps, gpl1_i, gpl1_lo, gpl1_hi),
        [planes(slab)],
    )
    (grad,) = call(
        functools.partial(final_kernel, sizes, slab),
        "final",
        (odd, taps, own, *arrived),
        [planes(slab)],
        scratch=[scratch(2)] * 2,
        scalars=1,
    )
    mixing_grad, plane_grad, depth_grad = call(
        functools.partial(result_kernel, channels, len(terms)),
        "result",
        terms,
        [sums(2, channels, channels), sums(9, 2, channels), sums(3, 2, channels)],
    )
    return (
        grad.reshape(1, channels, slab, nz, ny),
        mixing_grad,
        jnp.transpose(plane_grad.reshape(3, 3, 2, channels), (2, 3, 0, 1)),
        jnp.transpose(depth_grad, (1, 2, 0)),
    )


def solution(mesh):
    return jax.shard_map(
        on_device,
        mesh=mesh,
        in_specs=(P("dp", None, "sp", None, None), P("dp", None, "sp", None, None), P(), P(), P()),
        out_specs=(P("dp", None, "sp", None, None), P(), P(), P()),
        check_vma=False,
    )
```

```python
import functools
import math

import jax
import jax.numpy as jnp
from jax import lax
from jax.experimental import pallas as pl
from jax.experimental.pallas import tpu as pltpu
from jax.sharding import PartitionSpec as P

GROUP = 16
BF16 = jnp.bfloat16
F32 = jnp.float32


class Planes:
    def __init__(self, sizes, *parts):
        self.channels, self.nz, self.ny = sizes
        self.at = {}
        for ref, indices in parts:
            for spot, index in enumerate(indices):
                self.at[index] = (ref, spot)

    def __contains__(self, index):
        return index in self.at

    def tile(self, index, z, rows):
        ref, spot = self.at[index]
        return ref.at[rows, pl.ds((spot * self.nz + z) * self.ny, self.ny)]

    def span(self, index, start, size):
        ref, spot = self.at[index]
        return ref.at[:, pl.ds(spot * self.nz * self.ny + start, size)]

    def get(self, index, z, rows):
        return self.tile(index, z, rows)[...].astype(F32)

    def put(self, index, z, rows, value):
        self.tile(index, z, rows)[...] = value.astype(BF16)


def over_groups(channels, body, unroll=3):
    def step(group, carry):
        body(pl.ds(pl.multiple_of(group * GROUP, GROUP), GROUP))
        return carry

    lax.fori_loop(0, channels // GROUP, step, 0, unroll=unroll)


def spread(taps_ref, block, rows, first, count):
    return [taps_ref[block, t, rows, :].astype(F32) for t in range(first, first + count)]


def plane_taps(taps_ref, block, rows, flip):
    taps = spread(taps_ref, block, rows, 9 if flip else 0, 9)
    return [taps[3 * i : 3 * i + 3] for i in range(3)]


def wide_taps(kernels_xy, kernels_z, ny):
    channels = kernels_xy.shape[1]
    lane = lax.broadcasted_iota(jnp.int32, (1, 1, 3, 1, ny), 4)
    column = lax.broadcasted_iota(jnp.int32, (1, 1, 3, 1, ny), 2)
    keep = ((column != 0) | (lane != ny - 1)) & ((column != 2) | (lane != 0))
    planes = jnp.moveaxis(kernels_xy, 1, 3)
    planes = jnp.concatenate([planes, planes[:, ::-1, ::-1]], axis=1)[..., None]
    planes = jnp.where(keep, planes, jnp.zeros((), planes.dtype)).reshape(2, 18, channels, ny)
    depth = jnp.broadcast_to(jnp.moveaxis(kernels_z, 1, 2)[..., None], (2, 3, channels, ny))
    return jnp.concatenate([planes, depth], axis=1)


def plane_conv(taps, source, index, z, rows, ny):
    sums = [None, None, None]
    for i in range(3):
        if index + i - 1 in source:
            value = source.get(index + i - 1, z, rows)
            for j in range(3):
                term = taps[i][j] * value
                sums[j] = term if sums[j] is None else sums[j] + term
    return sums[1] + pltpu.roll(sums[0], 1, 1) + pltpu.roll(sums[2], ny - 1, 1)


def depth_conv(taps, values, z):
    total = taps[1] * values[z]
    if z > 0:
        total = total + taps[0] * values[z - 1]
    if z < len(values) - 1:
        total = total + taps[2] * values[z + 1]
    return total


def forward_taps(taps_ref, block, indices, source, planar, axial):
    nz, ny = source.nz, source.ny

    def body(rows):
        taps = plane_taps(taps_ref, block, rows, False)
        depth = spread(taps_ref, block, rows, 18, 3)
        for index in indices:
            values = [plane_conv(taps, source, index, z, rows, ny) for z in range(nz)]
            for z in range(nz):
                planar.put(index, z, rows, values[z])
                axial.put(index, z, rows, depth_conv(depth, values, z))

    over_groups(source.channels, body, 6)


def mixed(mix_ref, block, indices, source, use):
    size = source.nz * source.ny
    step = math.gcd(size, 256)
    weights = mix_ref[block]
    for index in indices:
        for start in range(0, size, step):
            product = jnp.dot(weights, source.span(index, start, step)[...], preferred_element_type=F32)
            use(index, start, step, product)


def gate(preact):
    sigma = 0.5 * jnp.tanh(0.5 * preact) + 0.5
    value = preact * sigma
    return value, sigma + value * (1.0 - sigma)


def hidden_of(mix_ref, indices, axial, hidden, slope, masks):
    def use(index, start, step, preact):
        value, rate = gate(preact)
        if index in masks:
            value, rate = value * masks[index], rate * masks[index]
        hidden.span(index, start, step)[...] = value.astype(BF16)
        slope.span(index, start, step)[...] = rate.astype(BF16)

    mixed(mix_ref, 0, indices, axial, use)


def top_gradient(mix_ref, indices, axial, cotangent, grad_pre):
    def use(index, start, step, preact):
        _, rate = gate(preact)
        grad = cotangent.span(index, start, step)[...].astype(F32) * rate
        grad_pre.span(index, start, step)[...] = grad.astype(BF16)

    mixed(mix_ref, 1, indices, axial, use)


def axial_gradient(mix_t_ref, block, indices, grad_pre, grad_axial):
    def use(index, start, step, product):
        grad_axial.span(index, start, step)[...] = product.astype(BF16)

    mixed(mix_t_ref, block, indices, grad_pre, use)


def planar_gradient(taps_ref, block, indices, grad_axial, grad_planar):
    nz = grad_axial.nz

    def body(rows):
        depth = [taps_ref[block, t, rows, :] for t in (20, 19, 18)]
        for index in indices:
            values = [grad_axial.tile(index, z, rows)[...] for z in range(nz)]
            for z in range(nz):
                grad_planar.put(index, z, rows, depth_conv(depth, values, z))

    over_groups(grad_axial.channels, body, 6)


def input_gradient(taps_ref, block, indices, grad_planar, target, slope, start=None):
    nz, ny = grad_planar.nz, grad_planar.ny

    def body(rows):
        taps = plane_taps(taps_ref, block, rows, True)
        for index in indices:
            for z in range(nz):
                value = plane_conv(taps, grad_planar, index, z, rows, ny)
                if slope is not None:
                    value = value * slope.get(index, z, rows)
                if start is not None:
                    value = value + start.get(index, z, rows)
                target.put(index, z, rows, value)

    over_groups(grad_planar.channels, body, 6)


def tap_sums(indices, grad_planar, source, grad_axial, planar, sums_ref, before=None):
    nz, ny = source.nz, source.ny

    def body(rows):
        lane = lax.broadcasted_iota(jnp.int32, (GROUP, ny), 1)
        sums = [None] * 12 if before is None else [before[t, rows, :] for t in range(12)]
        for index in indices:
            part = [None] * 12

            def add(tap, term):
                part[tap] = term if part[tap] is None else part[tap] + term

            for z in range(nz):
                grad = grad_planar.tile(index, z, rows)[...]
                shifted = (pltpu.roll(grad, ny - 1, 1), grad, pltpu.roll(grad, 1, 1))
                for i in range(3):
                    if index + i - 1 in source:
                        value = source.tile(index + i - 1, z, rows)[...]
                        for j in range(3):
                            add(3 * i + j, shifted[j] * value)
                grad = grad_axial.tile(index, z, rows)[...]
                for t in range(3):
                    if 0 <= z + t - 1 < nz:
                        add(9 + t, grad * planar.tile(index, z + t - 1, rows)[...])
            for t in range(12):
                if part[t] is not None:
                    term = part[t].astype(F32)
                    sums[t] = term if sums[t] is None else sums[t] + term
        for i in range(3):
            sums[3 * i] = jnp.where(lane != ny - 1, sums[3 * i], 0.0)
            sums[3 * i + 2] = jnp.where(lane != 0, sums[3 * i + 2], 0.0)
        for t in range(12):
            sums_ref[t, rows, :] = sums[t]

    over_groups(source.channels, body, 6)


def mixing_sum(indices, grad_pre, axial):
    size = grad_pre.nz * grad_pre.ny
    total = None
    for index in indices:
        term = lax.dot_general(
            grad_pre.span(index, 0, size)[...],
            axial.span(index, 0, size)[...],
            (((1,), (1,)), ((), ())),
            preferred_element_type=F32,
        )
        total = term if total is None else total + term
    return total


def rim_kernel(low, high, vol, first, second, plane_a, plane_b, arrived):
    odd = lax.rem(lax.axis_index("sp"), 2) != 0
    copies = [
        pltpu.make_async_copy(vol.at[0, :, jnp.where(odd, low, high)], plane_a, arrived.at[0]),
        pltpu.make_async_copy(vol.at[0, :, jnp.where(odd, high, low)], plane_b, arrived.at[1]),
    ]
    for copy in copies:
        copy.start()
    for copy, plane, out in zip(copies, (plane_a, plane_b), (first, second)):
        copy.wait()
        out[...] = plane[...].astype(F32).reshape(out.shape).astype(BF16)


def sort_sides(odd, first, second, low, high):
    @pl.when(odd != 0)
    def _():
        low[...], high[...] = first[...], second[...]

    @pl.when(odd == 0)
    def _():
        low[...], high[...] = second[...], first[...]


def inner_kernel(sizes, slab, vol, taps, mix, pl1, ax1, sl1, hid):
    inner = range(1, slab - 1)
    planar, axial, slope, hidden = (Planes(sizes, (ref, inner)) for ref in (pl1, ax1, sl1, hid))
    forward_taps(taps, 0, inner, Planes(sizes, (vol, range(slab))), planar, axial)
    hidden_of(mix, inner, axial, hidden, slope, {})


def middle_kernel(
    sizes, slab, odd, vol, first, second, cot, taps, mix, mix_t, hid_i,
    lo1, hi1, pl1, ax1, sl1, hid, gpl2, sums, mixing, pl2, ax2, gpre2, gax2,
):
    inner, edges = range(1, slab - 1), (0, slab - 1)
    sort_sides(odd[0], first, second, lo1, hi1)
    volume = Planes(sizes, (vol, range(slab)), (lo1, (-1,)), (hi1, (slab,)))
    axial = Planes(sizes, (ax1, edges))
    forward_taps(taps, 0, edges, volume, Planes(sizes, (pl1, edges)), axial)
    hidden_of(mix, edges, axial, Planes(sizes, (hid, edges)), Planes(sizes, (sl1, edges)), {})
    hidden = Planes(sizes, (hid_i, inner), (hid, edges))
    cotangent = Planes(sizes, (cot, range(slab)))
    axial, grad_pre = Planes(sizes, (ax2, inner)), Planes(sizes, (gpre2, inner))
    grad_axial = Planes(sizes, (gax2, inner))
    planar, grad_planar = Planes(sizes, (pl2, inner)), Planes(sizes, (gpl2, inner))
    forward_taps(taps, 1, inner, hidden, planar, axial)
    top_gradient(mix, inner, axial, cotangent, grad_pre)
    axial_gradient(mix_t, 1, inner, grad_pre, grad_axial)
    planar_gradient(taps, 1, inner, grad_axial, grad_planar)
    tap_sums(inner, grad_planar, hidden, grad_axial, planar, sums)
    mixing[...] = mixing_sum(inner, grad_pre, axial)


def edge_kernel(
    sizes, slab, odd, flags, vol, lo1, hi1, first, second, cot, taps, mix, mix_t, hid_i, hid_e, sl1_e, gpl2_i,
    lo2, hi2, pl1, ax1, hid, pl2, ax2, gpre2, gax2, gpl2, gpre1, gax1, gpl1_lo, gpl1_hi, to_first, to_second, sl1,
):
    sort_sides(odd[0], first, second, lo2, hi2)
    inner, edges, rims = range(1, slab - 1), (0, slab - 1), (-1, slab)
    outer = (-1, 0, slab - 1, slab)
    masks = {-1: flags[0], slab: flags[1]}
    volume = Planes(
        sizes, (vol, range(slab)), (lo1, (-1,)), (hi1, (slab,)), (lo2, (-2,)), (hi2, (slab + 1,))
    )
    axial = Planes(sizes, (ax1, rims))
    forward_taps(taps, 0, rims, volume, Planes(sizes, (pl1, rims)), axial)
    hidden_of(mix, rims, axial, Planes(sizes, (hid, rims)), Planes(sizes, (sl1, rims)), masks)
    hidden = Planes(sizes, (hid_i, inner), (hid_e, edges), (hid, rims))
    cotangent = Planes(sizes, (cot, range(slab)))
    axial, grad_pre = Planes(sizes, (ax2, edges)), Planes(sizes, (gpre2, edges))
    grad_axial = Planes(sizes, (gax2, edges))
    forward_taps(taps, 1, edges, hidden, Planes(sizes, (pl2, edges)), axial)
    top_gradient(mix, edges, axial, cotangent, grad_pre)
    axial_gradient(mix_t, 1, edges, grad_pre, grad_axial)
    planar_gradient(taps, 1, edges, grad_axial, Planes(sizes, (gpl2, edges)))
    grad_planar = Planes(sizes, (gpl2, edges), (gpl2_i, inner))
    slope = Planes(sizes, (sl1_e, edges), (sl1, rims))
    grad_pre, grad_axial = Planes(sizes, (gpre1, outer)), Planes(sizes, (gax1, outer))
    input_gradient(taps, 1, outer, grad_planar, grad_pre, slope)
    axial_gradient(mix_t, 0, outer, grad_pre, grad_axial)
    grad_planar = Planes(sizes, (gpl1_lo, outer[:2]), (gpl1_hi, outer[2:]))
    planar_gradient(taps, 0, outer, grad_axial, grad_planar)
    sort_sides(odd[0], gpl1_lo, gpl1_hi, to_first, to_second)


def weight_kernel(
    sizes, slab, factor, vol, lo1, hi1, lo2, hi2, taps, mix_t,
    pl1_i, ax1_i, sl1_i, hid_i, pl1_e, ax1_e, hid_e, gpl2_i, sums_i, mixing_i,
    pl1_r, ax1_r, hid_r, pl2_e, ax2_e, gpre2_e, gax2_e, gpl2_e, gpre1_o, gax1_o, gpl1_lo, gpl1_hi,
    gpl1, payload, gpre1, gax1, sums,
):
    inner, edges, rims = range(1, slab - 1), (0, slab - 1), (-1, slab)
    outer, own, wide = (-1, 0, slab - 1, slab), range(slab), range(-1, slab + 1)
    channels, _, ny = sizes
    grad_planar2 = Planes(sizes, (gpl2_i, inner), (gpl2_e, edges))
    grad_pre1 = Planes(sizes, (gpre1, inner), (gpre1_o, outer))
    grad_axial1 = Planes(sizes, (gax1, inner), (gax1_o, outer))
    grad_planar1 = Planes(sizes, (gpl1, inner), (gpl1_lo, outer[:2]), (gpl1_hi, outer[2:]))
    input_gradient(taps, 1, inner, grad_planar2, grad_pre1, Planes(sizes, (sl1_i, inner)))
    axial_gradient(mix_t, 0, inner, grad_pre1, grad_axial1)
    planar_gradient(taps, 0, inner, grad_axial1, grad_planar1)
    volume = Planes(
        sizes, (vol, own), (lo1, (-1,)), (hi1, (slab,)), (lo2, (-2,)), (hi2, (slab + 1,))
    )
    hidden = Planes(sizes, (hid_i, inner), (hid_e, edges), (hid_r, rims))
    planar1 = Planes(sizes, (pl1_i, inner), (pl1_e, edges), (pl1_r, rims))
    axial1 = Planes(sizes, (ax1_i, inner), (ax1_e, edges), (ax1_r, rims))
    planar2, axial2 = Planes(sizes, (pl2_e, edges)), Planes(sizes, (ax2_e, edges))
    grad_pre2, grad_axial2 = Planes(sizes, (gpre2_e, edges)), Planes(sizes, (gax2_e, edges))
    tap_sums(wide, grad_planar1, volume, grad_axial1, planar1, sums.at[0])
    tap_sums(edges, grad_planar2, hidden, grad_axial2, planar2, sums.at[1], sums_i)
    mixing = (
        mixing_sum(wide, grad_pre1, axial1),
        mixing_sum(edges, grad_pre2, axial2) + mixing_i[...],
    )
    lane = lax.broadcasted_iota(jnp.int32, (channels, payload.shape[1]), 1)
    for block in range(2):
        at = block * channels
        payload[at : at + channels, :channels] = (mixing[block] * factor).astype(BF16)
        packed = jnp.zeros((channels, payload.shape[1]), F32)
        for t in range(12):
            total = jnp.sum(sums[block, t], axis=1, keepdims=True)
            packed = jnp.where(lane == t, total, packed)
        turned = (packed * factor).T
        at = 2 * channels + GROUP * block
        payload[at : at + GROUP, :channels] = turned[:GROUP].astype(BF16)


def volume_kernel(sizes, slab, taps, gpl1_i, gpl1_lo, gpl1_hi, out):
    inner, outer = range(1, slab - 1), (-1, 0, slab - 1, slab)
    grad_planar = Planes(sizes, (gpl1_i, inner), (gpl1_lo, outer[:2]), (gpl1_hi, outer[2:]))
    input_gradient(taps, 0, range(slab), grad_planar, Planes(sizes, (out, range(slab))), None)


def final_kernel(sizes, slab, odd, taps, own, first, second, out, from_lo, from_hi):
    sort_sides(odd[0], first, second, from_lo, from_hi)
    outer = (-1, 0, slab - 1, slab)
    arrived = Planes(sizes, (from_lo, outer[:2]), (from_hi, outer[2:]))
    start, result = Planes(sizes, (own, range(slab))), Planes(sizes, (out, range(slab)))
    input_gradient(taps, 0, range(slab), arrived, result, None, start)


def added(*terms):
    terms = [term.astype(F32) for term in terms]
    while len(terms) > 1:
        terms = [left + right for left, right in zip(terms[::2], terms[1::2])]
    return terms[0]


def result_kernel(channels, count, *refs):
    terms, (mixing, plane_taps, depth_taps) = refs[:count], refs[count:]
    for block in range(2):
        rows = pl.ds(block * channels, channels)
        total = added(*(term[rows, :] for term in terms))
        mixing[block] = total[:, :channels]
        rows = pl.ds(2 * channels + GROUP * block, GROUP)
        total = added(*(term[rows, :] for term in terms))
        for t in range(9):
            plane_taps[t, block : block + 1, :] = total[t : t + 1, :channels]
        for t in range(3):
            depth_taps[t, block : block + 1, :] = total[9 + t : 10 + t, :channels]


def call(kernel, name, operands, outputs, scratch=(), cost=1, scalars=0):
    vmem = pl.BlockSpec(memory_space=pltpu.VMEM)
    smem = pl.BlockSpec(memory_space=pltpu.SMEM)
    return pl.pallas_call(
        kernel,
        name=name,
        out_shape=outputs,
        in_specs=[smem] * scalars + [vmem] * (len(operands) - scalars),
        out_specs=[vmem] * len(outputs),
        scratch_shapes=scratch,
        compiler_params=pltpu.CompilerParams(vmem_limit_bytes=16 << 20),
        cost_estimate=pl.CostEstimate(flops=0, bytes_accessed=cost, transcendentals=0),
    )(*operands)


def chunks(bits):
    bits = list(bits)
    return [bits[at : at + 2] for at in range(0, len(bits), 2)]


def sum_groups(dp_bits, sp_bits):
    return chunks(range(dp_bits + 1, dp_bits + sp_bits)) + chunks(range(dp_bits)) + [[dp_bits]]


def all_sum(mine, arrivals):
    arrived, others = [], []
    dp_bits, sp_bits = (lax.axis_size(axis).bit_length() - 1 for axis in ("dp", "sp"))
    places = range(1 << (dp_bits + sp_bits))
    for spot, bits in enumerate(sum_groups(dp_bits, sp_bits)):
        if others:
            mine = added(mine, *others).astype(BF16)
        for value in arrivals.get(spot, ()):
            mine, value = lax.optimization_barrier((mine, value))
            arrived.append(value)
        steps = [1 << bits[0]]
        if len(bits) > 1:
            steps += [1 << bits[1], (1 << bits[0]) + (1 << bits[1])]
        others = [lax.ppermute(mine, ("sp", "dp"), [(i, i ^ step) for i in places]) for step in steps]
    for value in arrivals.get(-1, ()):
        arrived.append(value)
    return (mine, *others), arrived


def on_device(volume, cotangent, kernels_xy, kernels_z, mixing):
    _, channels, slab, nz, ny = volume.shape
    plane = nz * ny
    sizes = (channels, nz, ny)
    ranks, place = lax.axis_size("sp"), lax.axis_index("sp")
    odd = place % 2
    firsts = [(i, i ^ 1) for i in range(ranks)]
    seconds = [(i, i + 1) for i in range(1, ranks - 1, 2)] + [(i + 1, i) for i in range(1, ranks - 1, 2)]

    def rims(volume, low, high, cost):
        return pl.pallas_call(
            functools.partial(rim_kernel, low, high),
            name="rims",
            out_shape=[jax.ShapeDtypeStruct((channels, plane), BF16)] * 2,
            in_specs=[pl.BlockSpec(memory_space=pl.ANY)],
            out_specs=[pl.BlockSpec(memory_space=pltpu.VMEM)] * 2,
            scratch_shapes=[pltpu.VMEM((channels, nz, ny), BF16)] * 2 + [pltpu.SemaphoreType.DMA((2,))],
            compiler_params=pltpu.CompilerParams(vmem_limit_bytes=16 << 20),
            cost_estimate=pl.CostEstimate(flops=0, bytes_accessed=cost, transcendentals=0),
        )(volume)

    def exchange(sent):
        return lax.ppermute(sent[0], "sp", firsts), lax.ppermute(sent[1], "sp", seconds)

    near = rims(volume, 0, slab - 1, 1)
    later, *near = lax.optimization_barrier((volume, *near))
    far = rims(later, 1, slab - 2, 3 << 20)
    near, far = exchange(near), exchange(far)
    vol = volume[0].reshape(channels, -1)
    cot = cotangent[0].reshape(channels, -1)
    taps = wide_taps(kernels_xy, kernels_z, ny)
    mix, mix_t = mixing, jnp.swapaxes(mixing, 1, 2)
    flags = jnp.stack([place > 0, place < ranks - 1]).astype(F32)
    odd = odd.reshape(1)

    def planes(count):
        return jax.ShapeDtypeStruct((channels, count * plane), BF16)

    def scratch(count):
        return pltpu.VMEM((channels, count * plane), BF16)

    def sums(*shape):
        return jax.ShapeDtypeStruct(shape, F32)

    inside = slab - 2
    pl1_i, ax1_i, sl1_i, hid_i = call(
        functools.partial(inner_kernel, sizes, slab),
        "inner",
        (vol, taps, mix),
        [planes(inside)] * 4,
        cost=4 << 20,
    )
    lo1, hi1, pl1_e, ax1_e, sl1_e, hid_e, gpl2_i, sums_i, mixing_i = call(
        functools.partial(middle_kernel, sizes, slab),
        "middle",
        (odd, vol, *near, cot, taps, mix, mix_t, hid_i),
        [planes(1)] * 2 + [planes(2)] * 4 + [planes(inside), sums(12, channels, ny), sums(channels, channels)],
        scratch=[scratch(inside)] * 4,
        scalars=1,
        cost=12 << 20,
    )
    (
        lo2, hi2, pl1_r, ax1_r, hid_r, pl2_e, ax2_e, gpre2_e, gax2_e, gpl2_e,
        gpre1_o, gax1_o, gpl1_lo, gpl1_hi, to_first, to_second,
    ) = call(
        functools.partial(edge_kernel, sizes, slab),
        "edge",
        (odd, flags, vol, lo1, hi1, *far, cot, taps, mix, mix_t, hid_i, hid_e, sl1_e, gpl2_i),
        [planes(1)] * 2 + [planes(2)] * 8 + [planes(4)] * 2 + [planes(2)] * 4,
        scratch=[scratch(2)],
        scalars=2,
        cost=18 << 20,
    )
    arrived = exchange((to_first, to_second))
    count = lax.axis_size("dp") * slab * ranks * nz * ny
    gpl1_i, payload = call(
        functools.partial(weight_kernel, sizes, slab, 1.0 / math.sqrt(count)),
        "weights",
        (
            vol, lo1, hi1, lo2, hi2, taps, mix_t,
            pl1_i, ax1_i, sl1_i, hid_i, pl1_e, ax1_e, hid_e, gpl2_i, sums_i, mixing_i,
            pl1_r, ax1_r, hid_r, pl2_e, ax2_e, gpre2_e, gax2_e, gpl2_e, gpre1_o, gax1_o, gpl1_lo, gpl1_hi,
        ),
        [planes(inside), jax.ShapeDtypeStruct((2 * channels + 2 * GROUP, 128), BF16)],
        scratch=[scratch(inside), scratch(inside), pltpu.VMEM((2, 12, channels, ny), F32)],
    )
    terms, arrived = all_sum(payload, {1: arrived[:1], -1: arrived[1:]})
    (own,) = call(
        functools.partial(volume_kernel, sizes, slab),
        "volume",
        (taps, gpl1_i, gpl1_lo, gpl1_hi),
        [planes(slab)],
    )
    (grad,) = call(
        functools.partial(final_kernel, sizes, slab),
        "final",
        (odd, taps, own, *arrived),
        [planes(slab)],
        scratch=[scratch(2)] * 2,
        scalars=1,
    )
    mixing_grad, plane_grad, depth_grad = call(
        functools.partial(result_kernel, channels, len(terms)),
        "result",
        terms,
        [sums(2, channels, channels), sums(9, 2, channels), sums(3, 2, channels)],
    )
    return (
        grad.reshape(1, channels, slab, nz, ny),
        mixing_grad,
        jnp.transpose(plane_grad.reshape(3, 3, 2, channels), (2, 3, 0, 1)),
        jnp.transpose(depth_grad, (1, 2, 0)),
    )


def solution(mesh):
    return jax.shard_map(
        on_device,
        mesh=mesh,
        in_specs=(P("dp", None, "sp", None, None), P("dp", None, "sp", None, None), P(), P(), P()),
        out_specs=(P("dp", None, "sp", None, None), P(), P(), P()),
        check_vma=False,
    )
```

```python
import functools
import math

import jax
import jax.numpy as jnp
from jax import lax
from jax.experimental import pallas as pl
from jax.experimental.pallas import tpu as pltpu
from jax.sharding import PartitionSpec as P

GROUP = 16
BF16 = jnp.bfloat16
F32 = jnp.float32


class Planes:
    def __init__(self, sizes, *parts):
        self.channels, self.nz, self.ny = sizes
        self.at = {}
        for ref, indices in parts:
            for spot, index in enumerate(indices):
                self.at[index] = (ref, spot)

    def __contains__(self, index):
        return index in self.at

    def tile(self, index, z, rows):
        ref, spot = self.at[index]
        return ref.at[rows, pl.ds((spot * self.nz + z) * self.ny, self.ny)]

    def span(self, index, start, size):
        ref, spot = self.at[index]
        return ref.at[:, pl.ds(spot * self.nz * self.ny + start, size)]

    def get(self, index, z, rows):
        return self.tile(index, z, rows)[...].astype(F32)

    def put(self, index, z, rows, value):
        self.tile(index, z, rows)[...] = value.astype(BF16)


def over_groups(channels, body, unroll=3):
    def step(group, carry):
        body(pl.ds(pl.multiple_of(group * GROUP, GROUP), GROUP))
        return carry

    lax.fori_loop(0, channels // GROUP, step, 0, unroll=unroll)


def spread(taps_ref, block, rows, first, count):
    return [taps_ref[block, t, rows, :].astype(F32) for t in range(first, first + count)]


def plane_taps(taps_ref, block, rows, flip):
    first = 9 if flip else 0
    taps = [taps_ref[block, t, rows, :] for t in range(first, first + 9)]
    return [taps[3 * i : 3 * i + 3] for i in range(3)]


def wide_taps(kernels_xy, kernels_z, ny):
    channels = kernels_xy.shape[1]
    lane = lax.broadcasted_iota(jnp.int32, (1, 1, 3, 1, ny), 4)
    column = lax.broadcasted_iota(jnp.int32, (1, 1, 3, 1, ny), 2)
    keep = ((column != 0) | (lane != ny - 1)) & ((column != 2) | (lane != 0))
    planes = jnp.moveaxis(kernels_xy, 1, 3)
    planes = jnp.concatenate([planes, planes[:, ::-1, ::-1]], axis=1)[..., None]
    planes = jnp.where(keep, planes, jnp.zeros((), planes.dtype)).reshape(2, 18, channels, ny)
    depth = jnp.broadcast_to(jnp.moveaxis(kernels_z, 1, 2)[..., None], (2, 3, channels, ny))
    return jnp.concatenate([planes, depth], axis=1)


def plane_conv(taps, source, index, z, rows, ny):
    sums = [None, None, None]
    for i in range(3):
        if index + i - 1 in source:
            value = source.tile(index + i - 1, z, rows)[...]
            for j in range(3):
                term = taps[i][j] * value
                sums[j] = term if sums[j] is None else sums[j] + term
    return sums[1].astype(F32) + pltpu.roll(sums[0], 1, 1).astype(F32) + pltpu.roll(sums[2], ny - 1, 1).astype(F32)


def depth_conv(taps, values, z):
    total = taps[1] * values[z]
    if z > 0:
        total = total + taps[0] * values[z - 1]
    if z < len(values) - 1:
        total = total + taps[2] * values[z + 1]
    return total


def forward_taps(taps_ref, block, indices, source, planar, axial):
    nz, ny = source.nz, source.ny

    def body(rows):
        taps = plane_taps(taps_ref, block, rows, False)
        depth = spread(taps_ref, block, rows, 18, 3)
        for index in indices:
            values = [plane_conv(taps, source, index, z, rows, ny) for z in range(nz)]
            for z in range(nz):
                planar.put(index, z, rows, values[z])
                axial.put(index, z, rows, depth_conv(depth, values, z))

    over_groups(source.channels, body, 6)


def mixed(mix_ref, block, indices, source, use):
    size = source.nz * source.ny
    step = math.gcd(size, 256)
    weights = mix_ref[block]
    for index in indices:
        for start in range(0, size, step):
            product = jnp.dot(weights, source.span(index, start, step)[...], preferred_element_type=F32)
            use(index, start, step, product)


def gate(preact):
    sigma = 0.5 * jnp.tanh(0.5 * preact) + 0.5
    value = preact * sigma
    return value, sigma + value * (1.0 - sigma)


def hidden_of(mix_ref, indices, axial, hidden, slope, masks):
    def use(index, start, step, preact):
        value, rate = gate(preact)
        if index in masks:
            value, rate = value * masks[index], rate * masks[index]
        hidden.span(index, start, step)[...] = value.astype(BF16)
        slope.span(index, start, step)[...] = rate.astype(BF16)

    mixed(mix_ref, 0, indices, axial, use)


def top_gradient(mix_ref, indices, axial, cotangent, grad_pre):
    def use(index, start, step, preact):
        _, rate = gate(preact)
        grad = cotangent.span(index, start, step)[...].astype(F32) * rate
        grad_pre.span(index, start, step)[...] = grad.astype(BF16)

    mixed(mix_ref, 1, indices, axial, use)


def axial_gradient(mix_t_ref, block, indices, grad_pre, grad_axial):
    def use(index, start, step, product):
        grad_axial.span(index, start, step)[...] = product.astype(BF16)

    mixed(mix_t_ref, block, indices, grad_pre, use)


def planar_gradient(taps_ref, block, indices, grad_axial, grad_planar):
    nz = grad_axial.nz

    def body(rows):
        depth = [taps_ref[block, t, rows, :] for t in (20, 19, 18)]
        for index in indices:
            values = [grad_axial.tile(index, z, rows)[...] for z in range(nz)]
            for z in range(nz):
                grad_planar.put(index, z, rows, depth_conv(depth, values, z))

    over_groups(grad_axial.channels, body, 6)


def input_gradient(taps_ref, block, indices, grad_planar, target, slope, start=None):
    nz, ny = grad_planar.nz, grad_planar.ny

    def body(rows):
        taps = plane_taps(taps_ref, block, rows, True)
        for index in indices:
            for z in range(nz):
                value = plane_conv(taps, grad_planar, index, z, rows, ny)
                if slope is not None:
                    value = value * slope.get(index, z, rows)
                if start is not None:
                    value = value + start.get(index, z, rows)
                target.put(index, z, rows, value)

    over_groups(grad_planar.channels, body, 6)


def tap_sums(indices, grad_planar, source, grad_axial, planar, sums_ref, before=None):
    nz, ny = source.nz, source.ny

    def body(rows):
        lane = lax.broadcasted_iota(jnp.int32, (GROUP, ny), 1)
        sums = [None] * 12 if before is None else [before[t, rows, :] for t in range(12)]
        for index in indices:
            part = [None] * 12

            def add(tap, term):
                part[tap] = term if part[tap] is None else part[tap] + term

            for z in range(nz):
                grad = grad_planar.tile(index, z, rows)[...]
                shifted = (pltpu.roll(grad, ny - 1, 1), grad, pltpu.roll(grad, 1, 1))
                for i in range(3):
                    if index + i - 1 in source:
                        value = source.tile(index + i - 1, z, rows)[...]
                        for j in range(3):
                            add(3 * i + j, shifted[j] * value)
                grad = grad_axial.tile(index, z, rows)[...]
                for t in range(3):
                    if 0 <= z + t - 1 < nz:
                        add(9 + t, grad * planar.tile(index, z + t - 1, rows)[...])
            for t in range(12):
                if part[t] is not None:
                    term = part[t].astype(F32)
                    sums[t] = term if sums[t] is None else sums[t] + term
        for i in range(3):
            sums[3 * i] = jnp.where(lane != ny - 1, sums[3 * i], 0.0)
            sums[3 * i + 2] = jnp.where(lane != 0, sums[3 * i + 2], 0.0)
        for t in range(12):
            sums_ref[t, rows, :] = sums[t]

    over_groups(source.channels, body, 6)


def mixing_sum(indices, grad_pre, axial):
    size = grad_pre.nz * grad_pre.ny
    total = None
    for index in indices:
        term = lax.dot_general(
            grad_pre.span(index, 0, size)[...],
            axial.span(index, 0, size)[...],
            (((1,), (1,)), ((), ())),
            preferred_element_type=F32,
        )
        total = term if total is None else total + term
    return total


def rim_kernel(low, high, vol, first, second, plane_a, plane_b, arrived):
    odd = lax.rem(lax.axis_index("sp"), 2) != 0
    copies = [
        pltpu.make_async_copy(vol.at[0, :, jnp.where(odd, low, high)], plane_a, arrived.at[0]),
        pltpu.make_async_copy(vol.at[0, :, jnp.where(odd, high, low)], plane_b, arrived.at[1]),
    ]
    for copy in copies:
        copy.start()
    for copy, plane, out in zip(copies, (plane_a, plane_b), (first, second)):
        copy.wait()
        out[...] = plane[...].astype(F32).reshape(out.shape).astype(BF16)


def sort_sides(odd, first, second, low, high):
    @pl.when(odd != 0)
    def _():
        low[...], high[...] = first[...], second[...]

    @pl.when(odd == 0)
    def _():
        low[...], high[...] = second[...], first[...]


def inner_kernel(sizes, slab, vol, taps, mix, pl1, ax1, sl1, hid):
    inner = range(1, slab - 1)
    planar, axial, slope, hidden = (Planes(sizes, (ref, inner)) for ref in (pl1, ax1, sl1, hid))
    forward_taps(taps, 0, inner, Planes(sizes, (vol, range(slab))), planar, axial)
    hidden_of(mix, inner, axial, hidden, slope, {})


def middle_kernel(
    sizes, slab, odd, vol, first, second, cot, taps, mix, mix_t, hid_i,
    lo1, hi1, pl1, ax1, sl1, hid, gpl2, sums, mixing, pl2, ax2, gpre2, gax2,
):
    inner, edges = range(1, slab - 1), (0, slab - 1)
    sort_sides(odd[0], first, second, lo1, hi1)
    volume = Planes(sizes, (vol, range(slab)), (lo1, (-1,)), (hi1, (slab,)))
    axial = Planes(sizes, (ax1, edges))
    forward_taps(taps, 0, edges, volume, Planes(sizes, (pl1, edges)), axial)
    hidden_of(mix, edges, axial, Planes(sizes, (hid, edges)), Planes(sizes, (sl1, edges)), {})
    hidden = Planes(sizes, (hid_i, inner), (hid, edges))
    cotangent = Planes(sizes, (cot, range(slab)))
    axial, grad_pre = Planes(sizes, (ax2, inner)), Planes(sizes, (gpre2, inner))
    grad_axial = Planes(sizes, (gax2, inner))
    planar, grad_planar = Planes(sizes, (pl2, inner)), Planes(sizes, (gpl2, inner))
    forward_taps(taps, 1, inner, hidden, planar, axial)
    top_gradient(mix, inner, axial, cotangent, grad_pre)
    axial_gradient(mix_t, 1, inner, grad_pre, grad_axial)
    planar_gradient(taps, 1, inner, grad_axial, grad_planar)
    tap_sums(inner, grad_planar, hidden, grad_axial, planar, sums)
    mixing[...] = mixing_sum(inner, grad_pre, axial)


def edge_kernel(
    sizes, slab, odd, flags, vol, lo1, hi1, first, second, cot, taps, mix, mix_t, hid_i, hid_e, sl1_e, gpl2_i,
    lo2, hi2, pl1, ax1, hid, pl2, ax2, gpre2, gax2, gpl2, gpre1, gax1, gpl1_lo, gpl1_hi, to_first, to_second, sl1,
):
    sort_sides(odd[0], first, second, lo2, hi2)
    inner, edges, rims = range(1, slab - 1), (0, slab - 1), (-1, slab)
    outer = (-1, 0, slab - 1, slab)
    masks = {-1: flags[0], slab: flags[1]}
    volume = Planes(
        sizes, (vol, range(slab)), (lo1, (-1,)), (hi1, (slab,)), (lo2, (-2,)), (hi2, (slab + 1,))
    )
    axial = Planes(sizes, (ax1, rims))
    forward_taps(taps, 0, rims, volume, Planes(sizes, (pl1, rims)), axial)
    hidden_of(mix, rims, axial, Planes(sizes, (hid, rims)), Planes(sizes, (sl1, rims)), masks)
    hidden = Planes(sizes, (hid_i, inner), (hid_e, edges), (hid, rims))
    cotangent = Planes(sizes, (cot, range(slab)))
    axial, grad_pre = Planes(sizes, (ax2, edges)), Planes(sizes, (gpre2, edges))
    grad_axial = Planes(sizes, (gax2, edges))
    forward_taps(taps, 1, edges, hidden, Planes(sizes, (pl2, edges)), axial)
    top_gradient(mix, edges, axial, cotangent, grad_pre)
    axial_gradient(mix_t, 1, edges, grad_pre, grad_axial)
    planar_gradient(taps, 1, edges, grad_axial, Planes(sizes, (gpl2, edges)))
    grad_planar = Planes(sizes, (gpl2, edges), (gpl2_i, inner))
    slope = Planes(sizes, (sl1_e, edges), (sl1, rims))
    grad_pre, grad_axial = Planes(sizes, (gpre1, outer)), Planes(sizes, (gax1, outer))
    input_gradient(taps, 1, outer, grad_planar, grad_pre, slope)
    axial_gradient(mix_t, 0, outer, grad_pre, grad_axial)
    grad_planar = Planes(sizes, (gpl1_lo, outer[:2]), (gpl1_hi, outer[2:]))
    planar_gradient(taps, 0, outer, grad_axial, grad_planar)
    sort_sides(odd[0], gpl1_lo, gpl1_hi, to_first, to_second)


def weight_kernel(
    sizes, slab, factor, vol, lo1, hi1, lo2, hi2, taps, mix_t,
    pl1_i, ax1_i, sl1_i, hid_i, pl1_e, ax1_e, hid_e, gpl2_i, sums_i, mixing_i,
    pl1_r, ax1_r, hid_r, pl2_e, ax2_e, gpre2_e, gax2_e, gpl2_e, gpre1_o, gax1_o, gpl1_lo, gpl1_hi,
    gpl1, payload, gpre1, gax1, sums,
):
    inner, edges, rims = range(1, slab - 1), (0, slab - 1), (-1, slab)
    outer, own, wide = (-1, 0, slab - 1, slab), range(slab), range(-1, slab + 1)
    channels, _, ny = sizes
    grad_planar2 = Planes(sizes, (gpl2_i, inner), (gpl2_e, edges))
    grad_pre1 = Planes(sizes, (gpre1, inner), (gpre1_o, outer))
    grad_axial1 = Planes(sizes, (gax1, inner), (gax1_o, outer))
    grad_planar1 = Planes(sizes, (gpl1, inner), (gpl1_lo, outer[:2]), (gpl1_hi, outer[2:]))
    input_gradient(taps, 1, inner, grad_planar2, grad_pre1, Planes(sizes, (sl1_i, inner)))
    axial_gradient(mix_t, 0, inner, grad_pre1, grad_axial1)
    planar_gradient(taps, 0, inner, grad_axial1, grad_planar1)
    volume = Planes(
        sizes, (vol, own), (lo1, (-1,)), (hi1, (slab,)), (lo2, (-2,)), (hi2, (slab + 1,))
    )
    hidden = Planes(sizes, (hid_i, inner), (hid_e, edges), (hid_r, rims))
    planar1 = Planes(sizes, (pl1_i, inner), (pl1_e, edges), (pl1_r, rims))
    axial1 = Planes(sizes, (ax1_i, inner), (ax1_e, edges), (ax1_r, rims))
    planar2, axial2 = Planes(sizes, (pl2_e, edges)), Planes(sizes, (ax2_e, edges))
    grad_pre2, grad_axial2 = Planes(sizes, (gpre2_e, edges)), Planes(sizes, (gax2_e, edges))
    tap_sums(wide, grad_planar1, volume, grad_axial1, planar1, sums.at[0])
    tap_sums(edges, grad_planar2, hidden, grad_axial2, planar2, sums.at[1], sums_i)
    mixing = (
        mixing_sum(wide, grad_pre1, axial1),
        mixing_sum(edges, grad_pre2, axial2) + mixing_i[...],
    )
    lane = lax.broadcasted_iota(jnp.int32, (channels, payload.shape[1]), 1)
    for block in range(2):
        at = block * channels
        payload[at : at + channels, :channels] = (mixing[block] * factor).astype(BF16)
        packed = jnp.zeros((channels, payload.shape[1]), F32)
        for t in range(12):
            total = jnp.sum(sums[block, t], axis=1, keepdims=True)
            packed = jnp.where(lane == t, total, packed)
        turned = (packed * factor).T
        at = 2 * channels + GROUP * block
        payload[at : at + GROUP, :channels] = turned[:GROUP].astype(BF16)


def volume_kernel(sizes, slab, taps, gpl1_i, gpl1_lo, gpl1_hi, out):
    inner, outer = range(1, slab - 1), (-1, 0, slab - 1, slab)
    grad_planar = Planes(sizes, (gpl1_i, inner), (gpl1_lo, outer[:2]), (gpl1_hi, outer[2:]))
    input_gradient(taps, 0, range(slab), grad_planar, Planes(sizes, (out, range(slab))), None)


def final_kernel(sizes, slab, odd, taps, own, first, second, out, from_lo, from_hi):
    sort_sides(odd[0], first, second, from_lo, from_hi)
    outer = (-1, 0, slab - 1, slab)
    arrived = Planes(sizes, (from_lo, outer[:2]), (from_hi, outer[2:]))
    start, result = Planes(sizes, (own, range(slab))), Planes(sizes, (out, range(slab)))
    input_gradient(taps, 0, range(slab), arrived, result, None, start)


def added(*terms):
    terms = [term.astype(F32) for term in terms]
    while len(terms) > 1:
        terms = [left + right for left, right in zip(terms[::2], terms[1::2])]
    return terms[0]


def result_kernel(channels, count, *refs):
    terms, (mixing, plane_taps, depth_taps) = refs[:count], refs[count:]
    for block in range(2):
        rows = pl.ds(block * channels, channels)
        total = added(*(term[rows, :] for term in terms))
        mixing[block] = total[:, :channels]
        rows = pl.ds(2 * channels + GROUP * block, GROUP)
        total = added(*(term[rows, :] for term in terms))
        for t in range(9):
            plane_taps[t, block : block + 1, :] = total[t : t + 1, :channels]
        for t in range(3):
            depth_taps[t, block : block + 1, :] = total[9 + t : 10 + t, :channels]


def call(kernel, name, operands, outputs, scratch=(), cost=1, scalars=0):
    vmem = pl.BlockSpec(memory_space=pltpu.VMEM)
    smem = pl.BlockSpec(memory_space=pltpu.SMEM)
    return pl.pallas_call(
        kernel,
        name=name,
        out_shape=outputs,
        in_specs=[smem] * scalars + [vmem] * (len(operands) - scalars),
        out_specs=[vmem] * len(outputs),
        scratch_shapes=scratch,
        compiler_params=pltpu.CompilerParams(vmem_limit_bytes=16 << 20),
        cost_estimate=pl.CostEstimate(flops=0, bytes_accessed=cost, transcendentals=0),
    )(*operands)


def chunks(bits):
    bits = list(bits)
    return [bits[at : at + 2] for at in range(0, len(bits), 2)]


def sum_groups(dp_bits, sp_bits):
    return chunks(range(dp_bits + 1, dp_bits + sp_bits)) + chunks(range(dp_bits)) + [[dp_bits]]


def all_sum(mine, arrivals):
    arrived, others = [], []
    dp_bits, sp_bits = (lax.axis_size(axis).bit_length() - 1 for axis in ("dp", "sp"))
    places = range(1 << (dp_bits + sp_bits))
    for spot, bits in enumerate(sum_groups(dp_bits, sp_bits)):
        if others:
            mine = added(mine, *others).astype(BF16)
        for value in arrivals.get(spot, ()):
            mine, value = lax.optimization_barrier((mine, value))
            arrived.append(value)
        steps = [1 << bits[0]]
        if len(bits) > 1:
            steps += [1 << bits[1], (1 << bits[0]) + (1 << bits[1])]
        others = [lax.ppermute(mine, ("sp", "dp"), [(i, i ^ step) for i in places]) for step in steps]
    for value in arrivals.get(-1, ()):
        arrived.append(value)
    return (mine, *others), arrived


def on_device(volume, cotangent, kernels_xy, kernels_z, mixing):
    _, channels, slab, nz, ny = volume.shape
    plane = nz * ny
    sizes = (channels, nz, ny)
    ranks, place = lax.axis_size("sp"), lax.axis_index("sp")
    odd = place % 2
    firsts = [(i, i ^ 1) for i in range(ranks)]
    seconds = [(i, i + 1) for i in range(1, ranks - 1, 2)] + [(i + 1, i) for i in range(1, ranks - 1, 2)]

    def rims(volume, low, high, cost):
        return pl.pallas_call(
            functools.partial(rim_kernel, low, high),
            name="rims",
            out_shape=[jax.ShapeDtypeStruct((channels, plane), BF16)] * 2,
            in_specs=[pl.BlockSpec(memory_space=pl.ANY)],
            out_specs=[pl.BlockSpec(memory_space=pltpu.VMEM)] * 2,
            scratch_shapes=[pltpu.VMEM((channels, nz, ny), BF16)] * 2 + [pltpu.SemaphoreType.DMA((2,))],
            compiler_params=pltpu.CompilerParams(vmem_limit_bytes=16 << 20),
            cost_estimate=pl.CostEstimate(flops=0, bytes_accessed=cost, transcendentals=0),
        )(volume)

    def exchange(sent):
        return lax.ppermute(sent[0], "sp", firsts), lax.ppermute(sent[1], "sp", seconds)

    near = rims(volume, 0, slab - 1, 1)
    later, *near = lax.optimization_barrier((volume, *near))
    far = rims(later, 1, slab - 2, 3 << 20)
    near, far = exchange(near), exchange(far)
    vol = volume[0].reshape(channels, -1)
    cot = cotangent[0].reshape(channels, -1)
    taps = wide_taps(kernels_xy, kernels_z, ny)
    mix, mix_t = mixing, jnp.swapaxes(mixing, 1, 2)
    flags = jnp.stack([place > 0, place < ranks - 1]).astype(F32)
    odd = odd.reshape(1)

    def planes(count):
        return jax.ShapeDtypeStruct((channels, count * plane), BF16)

    def scratch(count):
        return pltpu.VMEM((channels, count * plane), BF16)

    def sums(*shape):
        return jax.ShapeDtypeStruct(shape, F32)

    inside = slab - 2
    pl1_i, ax1_i, sl1_i, hid_i = call(
        functools.partial(inner_kernel, sizes, slab),
        "inner",
        (vol, taps, mix),
        [planes(inside)] * 4,
        cost=4 << 20,
    )
    lo1, hi1, pl1_e, ax1_e, sl1_e, hid_e, gpl2_i, sums_i, mixing_i = call(
        functools.partial(middle_kernel, sizes, slab),
        "middle",
        (odd, vol, *near, cot, taps, mix, mix_t, hid_i),
        [planes(1)] * 2 + [planes(2)] * 4 + [planes(inside), sums(12, channels, ny), sums(channels, channels)],
        scratch=[scratch(inside)] * 4,
        scalars=1,
        cost=12 << 20,
    )
    (
        lo2, hi2, pl1_r, ax1_r, hid_r, pl2_e, ax2_e, gpre2_e, gax2_e, gpl2_e,
        gpre1_o, gax1_o, gpl1_lo, gpl1_hi, to_first, to_second,
    ) = call(
        functools.partial(edge_kernel, sizes, slab),
        "edge",
        (odd, flags, vol, lo1, hi1, *far, cot, taps, mix, mix_t, hid_i, hid_e, sl1_e, gpl2_i),
        [planes(1)] * 2 + [planes(2)] * 8 + [planes(4)] * 2 + [planes(2)] * 4,
        scratch=[scratch(2)],
        scalars=2,
        cost=18 << 20,
    )
    arrived = exchange((to_first, to_second))
    count = lax.axis_size("dp") * slab * ranks * nz * ny
    gpl1_i, payload = call(
        functools.partial(weight_kernel, sizes, slab, 1.0 / math.sqrt(count)),
        "weights",
        (
            vol, lo1, hi1, lo2, hi2, taps, mix_t,
            pl1_i, ax1_i, sl1_i, hid_i, pl1_e, ax1_e, hid_e, gpl2_i, sums_i, mixing_i,
            pl1_r, ax1_r, hid_r, pl2_e, ax2_e, gpre2_e, gax2_e, gpl2_e, gpre1_o, gax1_o, gpl1_lo, gpl1_hi,
        ),
        [planes(inside), jax.ShapeDtypeStruct((2 * channels + 2 * GROUP, 128), BF16)],
        scratch=[scratch(inside), scratch(inside), pltpu.VMEM((2, 12, channels, ny), F32)],
    )
    terms, arrived = all_sum(payload, {1: arrived[:1], -1: arrived[1:]})
    (own,) = call(
        functools.partial(volume_kernel, sizes, slab),
        "volume",
        (taps, gpl1_i, gpl1_lo, gpl1_hi),
        [planes(slab)],
    )
    (grad,) = call(
        functools.partial(final_kernel, sizes, slab),
        "final",
        (odd, taps, own, *arrived),
        [planes(slab)],
        scratch=[scratch(2)] * 2,
        scalars=1,
    )
    mixing_grad, plane_grad, depth_grad = call(
        functools.partial(result_kernel, channels, len(terms)),
        "result",
        terms,
        [sums(2, channels, channels), sums(9, 2, channels), sums(3, 2, channels)],
    )
    return (
        grad.reshape(1, channels, slab, nz, ny),
        mixing_grad,
        jnp.transpose(plane_grad.reshape(3, 3, 2, channels), (2, 3, 0, 1)),
        jnp.transpose(depth_grad, (1, 2, 0)),
    )


def solution(mesh):
    return jax.shard_map(
        on_device,
        mesh=mesh,
        in_specs=(P("dp", None, "sp", None, None), P("dp", None, "sp", None, None), P(), P(), P()),
        out_specs=(P("dp", None, "sp", None, None), P(), P(), P()),
        check_vma=False,
    )
```
